32 devices in a mesh: outer: 4 (over y, x), inner: 2 (over core), heads: 4 (over z).
Axes of the slice: x: 2, y: 2, z: 4, core: 2. Of those that a mesh axis runs over, the one named last changes fastest.
Arguments:
- queries: bfloat16 [4096, 4096], P(('outer', 'inner', 'heads')), may hold values from -6 to 6
- keys: bfloat16 [4096, 4096], P(('outer', 'inner', 'heads')), may hold values from -6 to 6
- values: bfloat16 [4096, 4096], P(('outer', 'inner', 'heads')), may hold values from -6 to 6
- out_grad: bfloat16 [4096, 4096], P(('outer', 'inner', 'heads')), may hold values from -6 to 6
- doc_ids: int32 [4096], P(('outer', 'inner')), may hold values from 0 to 3, never falling along the last dimension, each value on 1 to 2048 neighbouring positions
- carry_in: float32 [32, 128, 128], P('heads'), may hold values from -0.5 to 0.5
- carry_cot: float32 [32, 128, 128], P('heads'), may hold values from -256 to 256
Outputs:
- attended: bfloat16 [4096, 4096], P(('outer', 'inner', 'heads'))
- query_grad: bfloat16 [4096, 4096], P(('outer', 'inner', 'heads'))
- key_grad: bfloat16 [4096, 4096], P(('outer', 'inner', 'heads'))
- value_grad: bfloat16 [4096, 4096], P(('outer', 'inner', 'heads'))
The draws below stay inside these ranges and needn't reach their ends.
Inputs may be any that keep to these rules, and one draw needn't show every extreme that they name: doc_ids never fall along the tokens; every document 0 to 3 has 1 to 2048 tokens and one has exactly 2048; document 0 continues the document whose state carry_in holds.
All inputs are finite; a program needn't handle non-finite values.
Results may differ from the reference program's by a relative error of at most 0.015.
Values may be sent and summed in bfloat16 or wider, within the bound.
No kernel may reach another device: no remote copies, remote signals or barrier semaphores. Data moves between devices by JAX's collectives and lax.ppermute only.
A program may use at most 192 MiB of HBM per device.

```python
import math
import jax
import jax.numpy as jnp
import numpy as np
from jax import lax

HEADS = 32
DH = 128
SPAN = 128
DOCS = 4
TOKENS = 4096
DOC_MOST = 2048


def level_of(rng, extent, pieces, low, high):
    gain, own = 1.0, jax.random.fold_in(rng, 6)
    for axis_at, shards_of in pieces:
        steps = jnp.exp(jax.random.uniform(jax.random.fold_in(own, axis_at), (shards_of,), jnp.float32, low / len(pieces), high / len(pieces)))
        gain = gain * jnp.repeat(steps, extent[axis_at] // shards_of).reshape([-1 if axis == axis_at else 1 for axis in range(len(extent))])
    return gain


def length_profile(number_of, total, most, skew):
    weights = [(1 << 20) // math.isqrt(grade ** skew) + 1 for grade in range(2, number_of + 1)]
    spare, counts = total - most - (number_of - 1), [1] * (number_of - 1)
    while spare > 0:
        candidates = [i for i in range(number_of - 1) if counts[i] < most]
        pool, left = sum([weights[i] for i in candidates]), spare
        for i in candidates:
            extra = min(most - counts[i], max(1, left * weights[i] // pool), spare)
            counts[i] = counts[i] + extra
            spare = spare - extra
    return np.array([most] + counts)


def ragged(rng, count, total, reach, lean):
    if count == 2:
        one = jax.random.randint(rng, (), max(1, total - reach), min(reach, total - 1) + 1)
        return jnp.stack([one, total - one])
    lengths = jnp.asarray(length_profile(count, total, reach, lean), jnp.int32)
    twos = (count - 1) // 2
    source_of, taker = lengths[1:1 + 2 * twos:2], lengths[2:2 + 2 * twos:2]
    slack = jnp.minimum(source_of - 1, reach - taker)
    shifted = jax.random.randint(jax.random.fold_in(rng, 1), (twos,), 0, 1 << 20) % (slack + 1)
    lengths = lengths.at[1:1 + 2 * twos:2].set(source_of - shifted).at[2:2 + 2 * twos:2].set(taker + shifted)
    return lengths[jax.random.permutation(jax.random.fold_in(rng, 2), count)]


def noise(rng, dims, spread, reach, split=(), kind=jnp.bfloat16):
    array = jax.random.normal(rng, dims, jnp.float32) * spread
    if len(split) > 0:
        array = level_of(rng, dims, split, -0.22, 0.18) * array
    return jnp.clip(array, min=-reach, max=reach).astype(kind)


def setup_inputs(seed: int = 0) -> dict:
    streams_of = jax.random.split(jax.random.key(seed), 8)
    queries = noise(streams_of[0], (TOKENS, HEADS * DH), 1.0, 6.0, ((0, 32),))
    keys = noise(streams_of[1], (TOKENS, HEADS * DH), 1.0, 6.0, ((0, 32),))
    values = noise(streams_of[2], (TOKENS, HEADS * DH), 1.0, 6.0, ((0, 32),))
    out_grad = noise(streams_of[3], (TOKENS, HEADS * DH), 1.0, 6.0, ((0, 32),))
    doc_ids = jnp.searchsorted(jnp.cumsum(ragged(streams_of[4], DOCS, TOKENS, DOC_MOST, 1)), jnp.arange(TOKENS), side="right").astype(jnp.int32)
    carry_in = noise(streams_of[5], (HEADS, DH, DH), DH ** -0.5, 0.5, ((0, 4),), jnp.float32)
    carry_cot = noise(streams_of[6], (HEADS, DH, DH), ((TOKENS // 2) ** 0.5), 256.0, ((0, 4),), jnp.float32)
    return dict(queries=queries, keys=keys, values=values, out_grad=out_grad, doc_ids=doc_ids, carry_in=carry_in, carry_cot=carry_cot)


def rounded(tensor):
    return lax.optimization_barrier(tensor.astype(jnp.bfloat16)).astype(jnp.float32)


def reference(queries, keys, values, out_grad, doc_ids, carry_in, carry_cot):
    factor = float(DH * DOC_MOST) ** -0.5
    blocks = TOKENS // SPAN

    def split_heads(tensor):
        return tensor.reshape(blocks, SPAN, HEADS, DH).transpose(0, 2, 1, 3).astype(jnp.float32)

    def merge_heads(tensor):
        return tensor.transpose(0, 2, 1, 3).reshape(TOKENS, HEADS * DH)

    inputs = (split_heads(queries), split_heads(keys), split_heads(values), split_heads(out_grad), doc_ids.reshape(blocks, SPAN))
    positions = jnp.arange(SPAN)
    causal = positions[:, None] >= positions[None, :]

    def block_scores(query_block, key_block, value_block, grad_block, doc_block):
        allowed = causal & (doc_block[:, None] == doc_block[None, :])
        scores = rounded(jnp.where(allowed[None], jnp.einsum('htd,hud->htu', query_block, key_block) * factor, 0.0))
        grad_scores = rounded(jnp.where(allowed[None], jnp.einsum('hte,hue->htu', grad_block, value_block) * factor, 0.0))
        return scores, grad_scores

    def forward(running, block_inputs):
        current, memory = running
        query_block, key_block, value_block, grad_block, doc_block = block_inputs
        first_doc = doc_block[0]
        last_doc = doc_block[-1]
        scores, grad_scores = block_scores(query_block, key_block, value_block, grad_block, doc_block)
        before = rounded(jnp.where(current == first_doc, memory, 0.0))
        in_first = (doc_block == first_doc)[None, :, None]
        attended = jnp.einsum('htu,hud->htd', scores, value_block) + jnp.where(in_first, jnp.einsum('htd,hde->hte', query_block, before), 0.0)
        query_grad = jnp.einsum('htu,hud->htd', grad_scores, key_block) + jnp.where(in_first, jnp.einsum('hte,hde->htd', grad_block, before), 0.0)
        in_last = (doc_block == last_doc)[None, :, None]
        new_terms = jnp.einsum('hud,hue->hde', jnp.where(in_last, key_block, 0.0), value_block) * factor
        memory = jnp.where(current == last_doc, memory, 0.0) + new_terms
        return (last_doc, memory), (attended.astype(jnp.bfloat16), query_grad.astype(jnp.bfloat16))

    def backward(running, block_inputs):
        current, memory = running
        query_block, key_block, value_block, grad_block, doc_block = block_inputs
        first_doc = doc_block[0]
        last_doc = doc_block[-1]
        scores, grad_scores = block_scores(query_block, key_block, value_block, grad_block, doc_block)
        state_after = rounded(jnp.where(current == last_doc, memory, 0.0))
        in_last = (doc_block == last_doc)[None, :, None]
        key_grad = jnp.einsum('htu,htd->hud', grad_scores, query_block) + jnp.where(in_last, jnp.einsum('hue,hde->hud', value_block, state_after), 0.0)
        value_grad = jnp.einsum('htu,hte->hue', scores, grad_block) + jnp.where(in_last, jnp.einsum('hud,hde->hue', key_block, state_after), 0.0)
        in_first = (doc_block == first_doc)[None, :, None]
        new_terms = jnp.einsum('htd,hte->hde', jnp.where(in_first, query_block, 0.0), grad_block) * factor
        memory = jnp.where(current == first_doc, memory, 0.0) + new_terms
        return (first_doc, memory), (key_grad.astype(jnp.bfloat16), value_grad.astype(jnp.bfloat16))

    initial = (doc_ids[0].astype(jnp.int32) * 0, carry_in)
    final_forward, forward_outputs = lax.scan(forward, initial, inputs)
    closing = (doc_ids[-1].astype(jnp.int32), factor * carry_cot)
    final_backward, backward_outputs = lax.scan(backward, closing, inputs, reverse=True)
    return (merge_heads(forward_outputs[0]), merge_heads(forward_outputs[1]), merge_heads(backward_outputs[0]), merge_heads(backward_outputs[1]))
```

```python
import functools

import jax
import jax.numpy as jnp
from jax import lax
from jax.experimental import pallas as pl
from jax.experimental.pallas import tpu as pltpu
from jax.sharding import PartitionSpec as P

DH = 128
SPAN = 128
CHUNK = 4
STREAMS = 2
F32 = jnp.float32
BF16 = jnp.bfloat16


def flag(condition):
    return condition.astype(F32)


def both(a, b):
    return flag(jnp.logical_and(a, b))


def swap(array, axis, distance):
    count = lax.axis_size(axis)
    return lax.ppermute(array, axis, [(i, i ^ distance) for i in range(count)])


def shift(array, axis, step):
    count = lax.axis_size(axis)
    return lax.ppermute(
        array, axis, [(i, i + step) for i in range(count) if 0 <= i + step < count]
    )


def total(terms):
    out = None
    for weight, array in terms:
        piece = weight * array.astype(F32)
        out = piece if out is None else out + piece
    return out


def transposed_dot(a, b):
    return lax.dot_general(a, b, (((0,), (0,)), ((), ())), preferred_element_type=F32)


def dot_transposed(a, b):
    return lax.dot_general(a, b, (((1,), (1,)), ((), ())), preferred_element_type=F32)


def dot(a, b):
    return lax.dot_general(a, b, (((1,), (0,)), ((), ())), preferred_element_type=F32)


def term_kernel(factor, group, docs_ref, q_ref, k_ref, v_ref, g_ref, forward_ref, backward_ref):
    docs = docs_ref[...]
    in_first = docs == docs[0:1]
    in_last = docs == docs[SPAN - 1 : SPAN]
    for i in range(group):
        at = slice(i * DH, (i + 1) * DH)
        keys = jnp.where(in_last, k_ref[:, at], 0)
        queries = jnp.where(in_first, q_ref[:, at], 0)
        forward_ref[i] = (transposed_dot(keys, v_ref[:, at]) * factor).astype(BF16)
        backward_ref[i] = (transposed_dot(queries, g_ref[:, at]) * factor).astype(BF16)


def state_terms(docs_column, arrays, factor, head, heads):
    group = min(heads, 4)
    steps = heads // group
    first = head // group
    columns = pl.BlockSpec((SPAN, group * DH), lambda i: (0, first + i))
    states = pl.BlockSpec((group, DH, DH), lambda i: (i, 0, 0))
    shape = jax.ShapeDtypeStruct((heads, DH, DH), BF16)
    return pl.pallas_call(
        functools.partial(term_kernel, factor, group),
        grid=(steps,),
        in_specs=[pl.BlockSpec((SPAN, DH), lambda i: (0, 0))] + [columns] * 4,
        out_specs=[states, states],
        out_shape=[shape, shape],
        cost_estimate=pl.CostEstimate(
            flops=heads * 4 * SPAN * DH * DH, bytes_accessed=heads * 6 * SPAN * DH * 2, transcendentals=0
        ),
    )(docs_column, *arrays)


def output_kernel(factor, group, docs_ref, row_ref, q_ref, k_ref, v_ref, g_ref, before_ref, after_ref, *refs):
    attended_ref, query_grad_ref, key_grad_ref, value_grad_ref = refs[-4:]
    docs = docs_ref[...]
    in_first = docs == docs[0:1]
    in_last = docs == docs[SPAN - 1 : SPAN]
    places = lax.broadcasted_iota(jnp.int32, (SPAN, SPAN), 0)
    others = lax.broadcasted_iota(jnp.int32, (SPAN, SPAN), 1)
    allowed = jnp.logical_and(others <= places, docs == row_ref[0:1])
    for i in range(group):
        at = slice(i * DH, (i + 1) * DH)
        q, k, v, g = q_ref[:, at], k_ref[:, at], v_ref[:, at], g_ref[:, at]
        before, after = before_ref[i], after_ref[i]
        scores = jnp.where(allowed, dot_transposed(q, k) * factor, 0.0).astype(BF16)
        grad_scores = jnp.where(allowed, dot_transposed(g, v) * factor, 0.0).astype(BF16)
        attended_ref[:, at] = (dot(scores, v) + dot(jnp.where(in_first, q, 0), before)).astype(BF16)
        query_grad_ref[:, at] = (
            dot(grad_scores, k) + dot_transposed(jnp.where(in_first, g, 0), before)
        ).astype(BF16)
        key_grad_ref[:, at] = (
            transposed_dot(grad_scores, q) + dot_transposed(jnp.where(in_last, v, 0), after)
        ).astype(BF16)
        value_grad_ref[:, at] = (
            transposed_dot(scores, g) + dot(jnp.where(in_last, k, 0), after)
        ).astype(BF16)


def outputs_of(docs_column, docs_row, arrays, before, after, held, factor, head, heads):
    group = min(heads, 4)
    steps = heads // group
    first = head // group
    columns = pl.BlockSpec((SPAN, group * DH), lambda i: (0, first + i))
    states = pl.BlockSpec((group, DH, DH), lambda i: (i, 0, 0))
    whole = pl.BlockSpec((SPAN, DH), lambda i: (0, 0))
    row = pl.BlockSpec((8, SPAN), lambda i: (0, 0))
    shape = jax.ShapeDtypeStruct(arrays[0].shape, BF16)
    return pl.pallas_call(
        functools.partial(output_kernel, factor, group),
        grid=(steps,),
        in_specs=[whole, row] + [columns] * 4 + [states] * 2 + [pl.BlockSpec(memory_space=pl.ANY)] * len(held),
        out_specs=[columns] * 4,
        out_shape=[shape] * 4,
        input_output_aliases={8 + i: i for i in range(len(held))},
        cost_estimate=pl.CostEstimate(
            flops=heads * 20 * SPAN * DH * DH, bytes_accessed=heads * 10 * SPAN * DH * 2, transcendentals=0
        ),
    )(docs_column, docs_row, *arrays, before, after, *held)


def shards(queries, keys, values, out_grad, doc_ids, carry_in, carry_cot):
    outer_count, inner_count, depth = (lax.axis_size(a) for a in ("outer", "inner", "heads"))
    o, c, z = (lax.axis_index(a) for a in ("outer", "inner", "heads"))
    tokens_all = doc_ids.shape[0] * outer_count * inner_count
    factor = float(DH * (tokens_all // 2)) ** (-0.5)
    head_count = queries.shape[1] // DH
    held_heads = head_count // depth
    arrays = (queries, keys, values, out_grad)
    piece_heads = max(CHUNK * STREAMS, inner_count)
    part = piece_heads // inner_count
    pieces = head_count // piece_heads
    inner_turns, outer_turns = range(1, inner_count), range(1, outer_count)

    blocks = doc_ids.reshape(depth, SPAN)
    firsts, lasts = blocks[:, 0].astype(F32), blocks[:, -1].astype(F32)
    edges = jnp.concatenate([firsts, lasts])
    inner_edges = [edges] + [swap(edges, "inner", d) for d in inner_turns]
    group_first = [e[0] for e in inner_edges]
    group_last = [e[2 * depth - 1] for e in inner_edges]
    block_first = [lax.dynamic_index_in_dim(e, z, 0, False) for e in inner_edges]
    block_last = [lax.dynamic_index_in_dim(e, depth + z, 0, False) for e in inner_edges]
    outer_first = functools.reduce(jnp.minimum, group_first)
    outer_last = functools.reduce(jnp.maximum, group_last)
    outer_edge = jnp.stack([outer_first, outer_last])
    outer_edges = [swap(outer_edge, "outer", d) for d in outer_turns]
    newest = functools.reduce(jnp.maximum, [e[1] for e in outer_edges], outer_last)
    outer_prior = functools.reduce(
        jnp.maximum, [jnp.where((o ^ d) < o, e[1], 0.0) for d, e in zip(outer_turns, outer_edges)], F32(0.0)
    )
    outer_later = functools.reduce(
        jnp.minimum, [jnp.where((o ^ d) > o, e[0], newest) for d, e in zip(outer_turns, outer_edges)], newest
    )
    prior, later = [], []
    for t in range(inner_count):
        prior.append(functools.reduce(
            jnp.maximum, [jnp.where((c ^ d) < (c ^ t), group_last[d], 0.0) for d in range(inner_count)], outer_prior
        ))
        later.append(functools.reduce(
            jnp.minimum, [jnp.where((c ^ d) > (c ^ t), group_first[d], newest) for d in range(inner_count)], outer_later
        ))
    first, last = block_first[0], block_last[0]
    last_before = lax.dynamic_index_in_dim(lasts, jnp.maximum(z - 1, 0), 0, False)
    first_after = lax.dynamic_index_in_dim(firsts, jnp.minimum(z + 1, depth - 1), 0, False)

    docs_block = lax.dynamic_index_in_dim(blocks, z, 0, False)
    docs_column = jnp.broadcast_to(docs_block[:, None], (SPAN, DH))
    docs_row = jnp.broadcast_to(docs_block[None, :], (8, SPAN))

    chunks = head_count // CHUNK
    terms_f, terms_b, prefix_f, prefix_b = [], [], [], []
    for p in range(pieces):
        forward, backward = state_terms(docs_column, arrays, factor, p * piece_heads, piece_heads)
        shape = (inner_count, part, DH, DH)
        split_f, split_b = forward.reshape(shape), backward.reshape(shape)

        def sent(d):
            at = c ^ d
            return jnp.stack(
                [lax.dynamic_index_in_dim(split_f, at, 0, False), lax.dynamic_index_in_dim(split_b, at, 0, False)]
            )

        received = [sent(0)] + [swap(sent(d), "inner", d) for d in inner_turns]
        sum_f = total([(flag(block_last[d] == outer_last), received[d][0]) for d in range(inner_count)])
        sum_b = total([(flag(block_first[d] == outer_first), received[d][1]) for d in range(inner_count)])
        sum_f, sum_b = sum_f.astype(BF16), sum_b.astype(BF16)
        fans = [swap(jnp.where(o < (o ^ d), sum_f, sum_b), "outer", d) for d in outer_turns]
        own, given = None, []
        for t in range(inner_count):
            x_f = total(
                [(both((o ^ d) < o, e[1] == prior[t]), r) for d, e, r in zip(outer_turns, outer_edges, fans)]
                + [
                    (both((c ^ d) < (c ^ t), block_last[d] == prior[t]), received[d][0])
                    for d in range(inner_count) if d != t
                ]
            )
            x_b = total(
                [(both((o ^ d) > o, e[0] == later[t]), r) for d, e, r in zip(outer_turns, outer_edges, fans)]
                + [
                    (both((c ^ d) > (c ^ t), block_first[d] == later[t]), received[d][1])
                    for d in range(inner_count) if d != t
                ]
            )
            x = jnp.stack([x_f, x_b]).astype(BF16)
            given.append(x if t == 0 else swap(x, "inner", t))
        if inner_count == 2:
            x = jnp.where(
                c == 0, jnp.concatenate(given, axis=1), jnp.concatenate(given[::-1], axis=1)
            )
        else:
            x = jnp.take(jnp.stack(given), c ^ jnp.arange(inner_count), axis=0)
            x = x.transpose(1, 0, 2, 3, 4).reshape(2, piece_heads, DH, DH)
        for i in range(0, piece_heads, CHUNK):
            head = p * piece_heads + i
            owner, at = head // held_heads, head % held_heads
            mine = z == owner
            terms_f.append(forward[i : i + CHUNK])
            terms_b.append(backward[i : i + CHUNK])
            prefix_f.append((
                x[0, i : i + CHUNK].astype(F32) + both(mine, prior[0] == 0.0) * carry_in[at : at + CHUNK]
            ).astype(BF16))
            prefix_b.append((
                x[1, i : i + CHUNK].astype(F32)
                + both(mine, later[0] == newest) * (factor * carry_cot[at : at + CHUNK])
            ).astype(BF16))

    keep_f = both(z > 0, last_before == last)
    keep_b = both(z < depth - 1, first_after == first)
    join_f, join_b = flag(prior[0] == last), flag(later[0] == first)
    turns = chunks // STREAMS
    steps = turns + depth - 2

    def picked(lists, stream, turn_of):
        out = None
        for place in range(depth):
            turn = min(max(turn_of(place), 0), turns - 1)
            options = [l[turn * STREAMS + stream] for l in lists]
            if out is None:
                out = options
            else:
                out = [jnp.where(z == place, b, a) for a, b in zip(out, options)]
        return [a.astype(F32) for a in out]

    up = [[None] * steps for _ in range(STREAMS)]
    down = [[None] * steps for _ in range(STREAMS)]
    for s in range(steps):
        for stream in range(STREAMS):
            t_f, x_f, x_b = picked((terms_f, prefix_f, prefix_b), stream, lambda place: s - place)
            state, rest = t_f + join_f * x_f, x_b
            if s > 0:
                state = state + keep_f * up[stream][s - 1][0].astype(F32)
                rest = rest + up[stream][s - 1][1].astype(F32)
            up[stream][s] = shift(jnp.stack([state, rest]).astype(BF16), "heads", 1)
            t_b, x_f, x_b = picked((terms_b, prefix_f, prefix_b), stream, lambda place: s - (depth - 1 - place))
            state, rest = t_b + join_b * x_b, x_f
            if s > 0:
                state = state + keep_b * down[stream][s - 1][0].astype(F32)
                rest = rest + down[stream][s - 1][1].astype(F32)
            down[stream][s] = shift(jnp.stack([state, rest]).astype(BF16), "heads", -1)

    from_before, from_after = flag(last_before == first), flag(first_after == last)
    reach_f, reach_b = flag(prior[0] == first), flag(later[0] == last)
    held = ()
    for turn in range(turns):
        befores, afters = [], []
        for stream in range(STREAMS):
            j = turn * STREAMS + stream
            before = [(reach_f, prefix_f[j])]
            after = [(reach_b, prefix_b[j])]
            for place in range(depth):
                here = flag(z == place)
                if place > 0:
                    got = up[stream][turn + place - 1]
                    before.append((here * from_before, got[0]))
                    after.append((here * reach_b, got[1]))
                if place < depth - 1:
                    got = down[stream][turn + depth - 2 - place]
                    after.append((here * from_after, got[0]))
                    before.append((here * reach_f, got[1]))
            befores.append(total(before).astype(BF16))
            afters.append(total(after).astype(BF16))
        held = outputs_of(
            docs_column, docs_row, arrays, jnp.concatenate(befores), jnp.concatenate(afters),
            held, factor, turn * STREAMS * CHUNK, STREAMS * CHUNK,
        )
    return tuple(held)


def solution(mesh):
    tokens = P(("outer", "inner", "heads"), None)
    carry = P("heads", None, None)
    return jax.shard_map(
        shards,
        mesh=mesh,
        in_specs=(tokens,) * 4 + (P(("outer", "inner")), carry, carry),
        out_specs=(tokens,) * 4,
        check_vma=False,
    )
```

```python
import functools

import jax
import jax.numpy as jnp
from jax import lax
from jax.experimental import pallas as pl
from jax.experimental.pallas import tpu as pltpu
from jax.sharding import PartitionSpec as P

DH = 128
SPAN = 128
LABELS = 16
DEPTH = 4
F32 = jnp.float32
BF16 = jnp.bfloat16
VMEM = pl.BlockSpec(memory_space=pltpu.VMEM)
SMEM = pl.BlockSpec(memory_space=pltpu.SMEM)
ANY = pl.BlockSpec(memory_space=pl.ANY)
LIMIT = 24 * 1024 * 1024


def pairs(array, axis, distance):
    count = lax.axis_size(axis)
    return lax.ppermute(array, axis, [(i, i ^ distance) for i in range(count)])


def transposed_dot(a, b):
    return lax.dot_general(a, b, (((0,), (0,)), ((), ())), preferred_element_type=F32)


def dot_transposed(a, b):
    return lax.dot_general(a, b, (((1,), (1,)), ((), ())), preferred_element_type=F32)


def dot(a, b):
    return lax.dot_general(a, b, (((1,), (0,)), ((), ())), preferred_element_type=F32)


def flag(row):
    return jnp.where(row, 1.0, 0.0).astype(F32)


def call(kernel, operands, out_shape, flops, scratch=(), aliases=None, specs=None, out_specs=None):
    size = sum(a.size * a.dtype.itemsize for a in operands) + sum(a.size * a.dtype.itemsize for a in out_shape)
    return pl.pallas_call(
        kernel,
        in_specs=specs,
        out_specs=out_specs or [VMEM] * len(out_shape),
        out_shape=out_shape,
        scratch_shapes=list(scratch),
        input_output_aliases=aliases or {},
        compiler_params=pltpu.CompilerParams(vmem_limit_bytes=LIMIT),
        cost_estimate=pl.CostEstimate(flops=flops, bytes_accessed=size, transcendentals=0),
    )(*operands)


def document_masks(docs):
    return docs == docs[0:1], docs == docs[SPAN - 1 : SPAN]


def term_kernel(factor, first, part, ids, docs_ref, q_ref, k_ref, v_ref, g_ref, *outs):
    c = ids[1]
    in_first, in_last = document_masks(docs_ref[...])
    for t, out in enumerate(outs):
        base = first + (c ^ t) * part
        for i in range(part):
            at = pl.ds(pl.multiple_of((base + i) * DH, DH), DH)
            keys = jnp.where(in_last, k_ref[:, at], 0)
            queries = jnp.where(in_first, q_ref[:, at], 0)
            out[0, i] = (transposed_dot(keys, v_ref[:, at]) * factor).astype(BF16)
            out[1, i] = (transposed_dot(queries, g_ref[:, at]) * factor).astype(BF16)


def own_row(ref, at):
    return ref[pl.ds(at, 1), :]


def sum_kernel(inner, part, levels, ids, *refs):
    labels, terms, outs = refs[:inner], refs[inner : 2 * inner], refs[2 * inner :]
    o, z = ids[0], ids[2]
    newest = functools.reduce(jnp.maximum, [l[2 * DEPTH - 1 : 2 * DEPTH, :] for l in labels])
    oldest = functools.reduce(jnp.minimum, [l[0:1, :] for l in labels])
    keep_f = [flag(own_row(l, DEPTH + z) == newest) for l in labels]
    keep_b = [flag(own_row(l, z) == oldest) for l in labels]
    low = [((o >> level) & 1) == 0 for level in range(levels)]
    for i in range(part):
        sum_f = sum(m * r[0, i].astype(F32) for m, r in zip(keep_f, terms)).astype(BF16)
        sum_b = sum(m * r[1, i].astype(F32) for m, r in zip(keep_b, terms)).astype(BF16)
        for chosen, out in zip(low, outs):
            out[i * DH : (i + 1) * DH, :] = jnp.where(chosen, sum_f, sum_b)
    rows = lax.broadcasted_iota(jnp.int32, (LABELS, DH), 0)
    marks = jnp.where(rows < LABELS // 2, jnp.broadcast_to(newest, (LABELS, DH)), jnp.broadcast_to(oldest, (LABELS, DH)))
    for out in outs:
        out[part * DH :, :] = marks.astype(BF16)


def prefix_kernel(factor, first, part, inner, outer, ids, carry_ref, cot_ref, *refs):
    labels, terms, fans = refs[:inner], refs[inner : 2 * inner], refs[2 * inner : 2 * inner + outer - 1]
    outs, edge_ref = refs[2 * inner + outer - 1 : -1], refs[-1]
    o, c, z = ids[0], ids[1], ids[2]
    held = carry_ref.shape[0]
    group_first = [l[0:1, :] for l in labels]
    group_last = [l[2 * DEPTH - 1 : 2 * DEPTH, :] for l in labels]
    block_first = [own_row(l, z) for l in labels]
    block_last = [own_row(l, DEPTH + z) for l in labels]
    marks = [r[part * DH : part * DH + LABELS, :].astype(F32) for r in fans]
    outer_last = [m[0:1] for m in marks]
    outer_first = [m[LABELS // 2 : LABELS // 2 + 1] for m in marks]
    newest = functools.reduce(jnp.maximum, group_last + outer_last)
    prior_base, later_base = jnp.zeros_like(newest), newest
    earlier = [(o ^ (d + 1)) < o for d in range(outer - 1)]
    for d in range(outer - 1):
        prior_base = jnp.maximum(prior_base, jnp.where(earlier[d], outer_last[d], 0.0))
        later_base = jnp.minimum(later_base, jnp.where(earlier[d], newest, outer_first[d]))
    head = first + c * part
    priors, laters, plans = [], [], []
    for t in range(inner):
        prior, later = prior_base, later_base
        for d in range(inner):
            if d != t:
                before = (c ^ d) < (c ^ t)
                prior = jnp.maximum(prior, jnp.where(before, group_last[d], 0.0))
                later = jnp.minimum(later, jnp.where(before, newest, group_first[d]))
        forward = [(flag(jnp.logical_and(earlier[d], outer_last[d] == prior)), fans[d], None) for d in range(outer - 1)]
        backward = [
            (flag(jnp.logical_and(jnp.logical_not(earlier[d]), outer_first[d] == later)), fans[d], None)
            for d in range(outer - 1)
        ]
        for d in range(inner):
            if d != t:
                before = (c ^ d) < (c ^ t)
                forward.append((flag(jnp.logical_and(before, block_last[d] == prior)), terms[d], 0))
                backward.append((flag(jnp.logical_and(jnp.logical_not(before), block_first[d] == later)), terms[d], 1))
        priors.append(prior)
        laters.append(later)
        plans.append((forward, backward, flag(prior == 0.0), flag(later == newest) * factor))
    for i in range(part):
        place = head + i - z * held
        mine = jnp.logical_and(place >= 0, place < held)
        place = jnp.clip(place, 0, held - 1)
        carries = (jnp.where(mine, carry_ref[place], 0.0), jnp.where(mine, cot_ref[place], 0.0))

        def value(ref, side):
            return (ref[i * DH : (i + 1) * DH, :] if side is None else ref[side, i]).astype(F32)

        for t, out in enumerate(outs):
            for side in range(2):
                total = plans[t][2 + side] * carries[side]
                for weight, ref, which in plans[t][side]:
                    total = total + weight * value(ref, which)
                out[side, i] = total.astype(BF16)
    edge_ref[0:1, :] = priors[0]
    edge_ref[1:2, :] = laters[0]
    edge_ref[2:8, :] = jnp.broadcast_to(newest, (6, DH))


def edge_rows(z, labels, edges):
    first, last = own_row(labels, z), own_row(labels, DEPTH + z)
    last_before = own_row(labels, DEPTH + jnp.maximum(z - 1, 0))
    first_after = own_row(labels, jnp.minimum(z + 1, DEPTH - 1))
    return (last, last_before, edges[0:1, :], first), (first, first_after, edges[1:2, :], last)


def hop(side, rows, part, term_ref, prefix_ref, got_ref, out):
    own, neighbour, prior, _ = [jnp.where(side == 0, a, b) for a, b in zip(*rows)]
    join, keep = flag(prior == own), flag(neighbour == own)
    for i in range(part):
        state = term_ref[side, i].astype(F32) + join * prefix_ref[side, i].astype(F32)
        rest = prefix_ref[1 - side, i].astype(F32)
        if got_ref is not None:
            state = state + keep * got_ref[0, i].astype(F32)
            rest = rest + got_ref[1, i].astype(F32)
        out[0, i] = state.astype(BF16)
        out[1, i] = rest.astype(BF16)


def end_kernel(part, near, far, ids, labels, edges, *refs):
    z = ids[2]
    out = refs[-1]
    rows = edge_rows(z, labels, edges)
    side = jnp.where(z >= DEPTH // 2, 1, 0)
    at_end = jnp.logical_or(z == 0, z == DEPTH - 1)
    if near:

        @pl.when(at_end)
        def _():
            hop(side, rows, part, refs[0], refs[1], None, out)

    if far:

        @pl.when(jnp.logical_not(at_end))
        def _():
            term, prefix, got = refs[-4:-1]
            hop(1 - side, rows, part, term, prefix, got, out)


def middle_kernel(part, ids, labels, edges, term, prefix, got, out):
    z = ids[2]
    rows = edge_rows(z, labels, edges)
    side = jnp.where(z >= DEPTH // 2, 1, 0)
    hop(side, rows, part, term, prefix, got, out)


def output_kernel(
    factor, first, part, turn, ids, labels, edges, docs_ref, row_ref, q_ref, k_ref, v_ref, g_ref,
    prefix, near, middle, far, *refs,
):
    outs, (states, held, sems) = refs[-7:-3], refs[-3:]
    c, z = ids[1], ids[2]
    side = jnp.where(z >= DEPTH // 2, 1, 0)
    at_end = jnp.logical_or(z == 0, z == DEPTH - 1)
    rows = edge_rows(z, labels, edges)

    def state(which, over, rest):
        _, neighbour, prior, target = [jnp.where(which == 0, a, b) for a, b in zip(*rows)]
        reach, come = flag(prior == target), flag(neighbour == target)
        for i in range(part):
            value = reach * prefix[which, i].astype(F32)
            if over is not None:
                value = value + come * over[0, i].astype(F32)
            if rest is not None:
                value = value + reach * rest[1, i].astype(F32)
            states[which, i] = value.astype(BF16)

    @pl.when(at_end)
    def _():
        state(side, None, far)
        state(1 - side, far, None)

    @pl.when(jnp.logical_not(at_end))
    def _():
        state(side, near, middle)
        state(1 - side, middle, near)

    docs = docs_ref[...]
    in_first, in_last = document_masks(docs)
    places = lax.broadcasted_iota(jnp.int32, (SPAN, SPAN), 0)
    others = lax.broadcasted_iota(jnp.int32, (SPAN, SPAN), 1)
    allowed = jnp.logical_and(others <= places, docs == row_ref[0:1])
    base = first + (c ^ turn) * part
    copies = []
    for i in range(part):
        at = pl.ds(pl.multiple_of((base + i) * DH, DH), DH)
        q, k, v, g = q_ref[:, at], k_ref[:, at], v_ref[:, at], g_ref[:, at]
        before, after = states[0, i], states[1, i]
        scores = jnp.where(allowed, dot_transposed(q, k) * factor, 0.0).astype(BF16)
        grad_scores = jnp.where(allowed, dot_transposed(g, v) * factor, 0.0).astype(BF16)
        results = (
            dot(scores, v) + dot(jnp.where(in_first, q, 0), before),
            dot(grad_scores, k) + dot_transposed(jnp.where(in_first, g, 0), before),
            transposed_dot(grad_scores, q) + dot_transposed(jnp.where(in_last, v, 0), after),
            transposed_dot(scores, g) + dot(jnp.where(in_last, k, 0), after),
        )
        for n, result in enumerate(results):
            held[n, i] = result.astype(BF16)
            copy = pltpu.make_async_copy(held.at[n, i], outs[n].at[:, at], sems.at[n, i])
            copy.start()
            copies.append(copy)
    for copy in copies:
        copy.wait()


def shards(queries, keys, values, out_grad, doc_ids, carry_in, carry_cot):
    outer, inner, depth = (lax.axis_size(a) for a in ("outer", "inner", "heads"))
    assert depth == DEPTH
    tokens_all = doc_ids.shape[0] * outer * inner
    factor = float(DH * (tokens_all // 2)) ** (-0.5)
    head_count = queries.shape[1] // DH
    arrays = (queries, keys, values, out_grad)
    part = min(4, head_count // inner)
    piece = part * inner
    chunks = head_count // part
    lag = 4

    ids = jnp.stack([lax.axis_index(a) for a in ("outer", "inner", "heads")]).astype(jnp.int32)
    blocks = doc_ids.reshape(depth, SPAN)
    edges = jnp.concatenate([blocks[:, 0], blocks[:, -1]]).astype(F32)
    own_labels = jnp.broadcast_to(edges[:, None], (2 * depth, DH))
    labels = [own_labels] + [pairs(own_labels, "inner", d) for d in range(1, inner)]
    docs = lax.dynamic_index_in_dim(blocks, ids[2], 0, False)
    docs_column = jnp.broadcast_to(docs[:, None], (SPAN, DH))
    docs_row = jnp.broadcast_to(docs[None, :], (8, SPAN))

    state_pair = jax.ShapeDtypeStruct((2, part, DH, DH), BF16)
    levels = (outer - 1).bit_length()
    fan_shape = jax.ShapeDtypeStruct((part * DH + LABELS, DH), BF16)
    edge_shape = jax.ShapeDtypeStruct((8, DH), F32)
    product = 2 * SPAN * DH * DH

    terms, prefixes, edge = [], [], None
    for first in range(0, head_count, piece):
        own = call(
            functools.partial(term_kernel, factor, first, part),
            (ids, docs_column) + arrays,
            [state_pair] * inner,
            2 * piece * product,
            specs=[SMEM] + [VMEM] * 5,
        )
        received = [own[0]] + [pairs(own[d], "inner", d) for d in range(1, inner)]
        sums = call(
            functools.partial(sum_kernel, inner, part, levels),
            (ids, *labels, *received),
            [fan_shape] * levels,
            part * DH * DH * 8,
            specs=[SMEM] + [VMEM] * (2 * inner),
        )
        fans = [pairs(sums[d.bit_length() - 1], "outer", d) for d in range(1, outer)]
        given = call(
            functools.partial(prefix_kernel, factor, first, part, inner, outer),
            (ids, carry_in, carry_cot, *labels, *received, *fans),
            [state_pair] * inner + [edge_shape],
            part * DH * DH * 16 * inner,
            specs=[SMEM] + [VMEM] * (2 + 2 * inner + outer - 1),
        )
        edge = given[-1] if edge is None else edge
        terms.extend(own)
        prefixes.extend([given[0]] + [pairs(given[d], "inner", d) for d in range(1, inner)])

    near, middle = [None] * (chunks + lag), [None] * chunks
    for k in range(chunks + lag):
        operands, perm = [ids, own_labels, edge], []
        if k < chunks:
            operands += [terms[k], prefixes[k]]
            perm += [(0, 1), (3, 2)]
        if k >= lag:
            operands += [terms[k - lag], prefixes[k - lag], middle[k - lag]]
            perm += [(1, 0), (2, 3)]
        sent = call(
            functools.partial(end_kernel, part, k < chunks, k >= lag),
            operands,
            [state_pair],
            part * DH * DH * 8,
            specs=[SMEM] + [VMEM] * (len(operands) - 1),
        )[0]
        near[k] = lax.ppermute(sent, "heads", perm)
        if k < chunks:
            sent = call(
                functools.partial(middle_kernel, part),
                (ids, own_labels, edge, terms[k], prefixes[k], near[k]),
                [state_pair],
                part * DH * DH * 8,
                specs=[SMEM] + [VMEM] * 5,
            )[0]
            middle[k] = lax.ppermute(sent, "heads", [(1, 2), (2, 1)])

    out_shape = jax.ShapeDtypeStruct(queries.shape, BF16)
    results = ()
    for k in range(chunks):
        operands = (ids, own_labels, edge, docs_column, docs_row) + arrays
        operands += (prefixes[k], near[k], middle[k], near[k + lag])
        results = call(
            functools.partial(output_kernel, factor, k // inner * piece, part, k % inner),
            operands + tuple(results),
            [out_shape] * 4,
            10 * part * product,
            scratch=[
                pltpu.VMEM((2, part, DH, DH), BF16),
                pltpu.VMEM((4, part, SPAN, DH), BF16),
                pltpu.SemaphoreType.DMA((4, part)),
            ],
            aliases={len(operands) + i: i for i in range(len(results))},
            specs=[SMEM] + [VMEM] * (len(operands) - 1) + [ANY] * len(results),
            out_specs=[ANY] * 4,
        )
    return tuple(results)


def solution(mesh):
    tokens = P(("outer", "inner", "heads"), None)
    carry = P("heads", None, None)
    return jax.shard_map(
        shards,
        mesh=mesh,
        in_specs=(tokens,) * 4 + (P(("outer", "inner")), carry, carry),
        out_specs=(tokens,) * 4,
        check_vma=False,
    )
```

```python
import functools

import jax
import jax.numpy as jnp
from jax import lax
from jax.experimental import pallas as pl
from jax.experimental.pallas import tpu as pltpu
from jax.sharding import PartitionSpec as P

DH = 128
SPAN = 128
LABELS = 16
DEPTH = 4
F32 = jnp.float32
BF16 = jnp.bfloat16
VMEM = pl.BlockSpec(memory_space=pltpu.VMEM)
SMEM = pl.BlockSpec(memory_space=pltpu.SMEM)
ANY = pl.BlockSpec(memory_space=pl.ANY)
LIMIT = 24 * 1024 * 1024


def pairs(array, axis, distance):
    count = lax.axis_size(axis)
    return lax.ppermute(array, axis, [(i, i ^ distance) for i in range(count)])


def transposed_dot(a, b):
    return lax.dot_general(a, b, (((0,), (0,)), ((), ())), preferred_element_type=F32)


def dot_transposed(a, b):
    return lax.dot_general(a, b, (((1,), (1,)), ((), ())), preferred_element_type=F32)


def dot(a, b):
    return lax.dot_general(a, b, (((1,), (0,)), ((), ())), preferred_element_type=F32)


def flag(row):
    return jnp.where(row, 1.0, 0.0).astype(F32)


def call(token, kernel, operands, out_shape, flops, scratch=(), aliases=None, specs=None, out_specs=None):
    count, results = len(operands), len(out_shape)

    def ordered(*refs):
        kernel(*refs[:count], *refs[count + 1 : count + 1 + results], *refs[count + 2 + results :])

    size = sum(a.size * a.dtype.itemsize for a in operands) + sum(a.size * a.dtype.itemsize for a in out_shape)
    *outs, token = pl.pallas_call(
        ordered,
        in_specs=list(specs or [SMEM] + [VMEM] * (count - 1)) + [VMEM],
        out_specs=list(out_specs or [VMEM] * results) + [VMEM],
        out_shape=list(out_shape) + [jax.ShapeDtypeStruct(token.shape, token.dtype)],
        scratch_shapes=list(scratch),
        input_output_aliases={**(aliases or {}), count: results},
        compiler_params=pltpu.CompilerParams(vmem_limit_bytes=LIMIT),
        cost_estimate=pl.CostEstimate(flops=flops, bytes_accessed=size, transcendentals=0),
    )(*operands, token)
    return token, outs


def document_masks(docs):
    return docs == docs[0:1], docs == docs[SPAN - 1 : SPAN]


def columns(head):
    return pl.ds(pl.multiple_of(head * DH, DH), DH)


def own_row(ref, at):
    return ref[pl.ds(at, 1), :]


def term_kernel(factor, groups, part, docs_ref, ids, heads, q_ref, k_ref, v_ref, g_ref, outs, extra=None):
    c = ids[1]
    in_first, in_last = document_masks(docs_ref[...])
    for t, out in enumerate(outs):
        for s in range(groups):
            head_f, head_b = heads(s, c ^ t)
            for i in range(part):
                at = columns(head_f + i)
                forward = transposed_dot(jnp.where(in_last, k_ref[:, at], 0), v_ref[:, at]) * factor
                at = columns(head_b + i)
                backward = transposed_dot(jnp.where(in_first, q_ref[:, at], 0), g_ref[:, at]) * factor
                if extra is not None:
                    add_f, add_b = extra((c ^ t) * part + i)
                    forward, backward = forward + add_f, backward + add_b
                out[0, s * part + i] = forward.astype(BF16)
                out[1, s * part + i] = backward.astype(BF16)


def rest_terms(factor, unit, part, places, shift, total, ids, docs_ref, q_ref, k_ref, v_ref, g_ref, *outs):
    def heads(s, inner_place):
        g = places[s]
        return g * unit + inner_place * part, (g + shift) % total * unit + inner_place * part

    term_kernel(factor, len(places), part, docs_ref, ids, heads, q_ref, k_ref, v_ref, g_ref, outs)


def lead_terms(
    factor, unit, part, shift, outer, inner, ids, docs_ref, labels, q_hbm, k_hbm, v_hbm, g_hbm, carry_hbm, cot_hbm, *refs,
):
    outs, (q_ref, k_ref, v_ref, g_ref, carry_ref, cot_ref, sems) = refs[:inner], refs[inner:]
    o, c, z = ids[0], ids[1], ids[2]
    held = carry_hbm.shape[0]
    forward, backward = pl.ds(0, unit * DH), pl.ds(shift * unit * DH, unit * DH)
    copies = [
        pltpu.make_async_copy(k_hbm.at[:, forward], k_ref, sems.at[0]),
        pltpu.make_async_copy(v_hbm.at[:, forward], v_ref, sems.at[1]),
        pltpu.make_async_copy(q_hbm.at[:, backward], q_ref, sems.at[2]),
        pltpu.make_async_copy(g_hbm.at[:, backward], g_ref, sems.at[3]),
        pltpu.make_async_copy(carry_hbm.at[pl.ds(0, unit)], carry_ref, sems.at[4]),
        pltpu.make_async_copy(cot_hbm.at[pl.ds(held - unit, unit)], cot_ref, sems.at[5]),
    ]
    for copy in copies:
        copy.start()
    for copy in copies:
        copy.wait()
    first, last = own_row(labels, z), own_row(labels, DEPTH + z)
    opens = jnp.logical_and(jnp.logical_and(o == 0, c == 0), z == 0)
    closes = jnp.logical_and(jnp.logical_and(o == outer - 1, c == inner - 1), z == DEPTH - 1)
    open_f = flag(jnp.logical_and(opens, last == 0.0))
    close_b = flag(jnp.logical_and(closes, first == last)) * factor

    def extra(place):
        return open_f * carry_ref[place], close_b * cot_ref[place]

    term_kernel(
        factor, 1, part, docs_ref, ids, lambda s, place: (place * part, place * part),
        q_ref, k_ref, v_ref, g_ref, outs, extra,
    )


def block_rows(labels, z, grouped):
    if grouped:
        return [l[0:1, :] for l in labels], [l[2 * DEPTH - 1 : 2 * DEPTH, :] for l in labels]
    return [own_row(l, z) for l in labels], [own_row(l, DEPTH + z) for l in labels]


def sum_kernel(inner, levels, grouped, ids, *refs):
    labels, terms, outs = refs[:inner], refs[inner : 2 * inner], refs[2 * inner :]
    o, z = ids[0], ids[2]
    count = terms[0].shape[1]
    newest = functools.reduce(jnp.maximum, [l[2 * DEPTH - 1 : 2 * DEPTH, :] for l in labels])
    oldest = functools.reduce(jnp.minimum, [l[0:1, :] for l in labels])
    firsts, lasts = block_rows(labels, z, grouped)
    keep_f = [flag(l == newest) for l in lasts]
    keep_b = [flag(l == oldest) for l in firsts]
    low = [((o >> level) & 1) == 0 for level in range(levels)]
    for i in range(count):
        sum_f = sum(m * r[0, i].astype(F32) for m, r in zip(keep_f, terms)).astype(BF16)
        sum_b = sum(m * r[1, i].astype(F32) for m, r in zip(keep_b, terms)).astype(BF16)
        for chosen, out in zip(low, outs):
            out[i * DH : (i + 1) * DH, :] = jnp.where(chosen, sum_f, sum_b)
    rows = lax.broadcasted_iota(jnp.int32, (LABELS, DH), 0)
    marks = jnp.where(rows < LABELS // 2, jnp.broadcast_to(newest, (LABELS, DH)), jnp.broadcast_to(oldest, (LABELS, DH)))
    for out in outs:
        out[count * DH :, :] = marks.astype(BF16)


def prefix_kernel(factor, unit, part, places, shift, total, inner, outer, grouped, ids, carry_ref, cot_ref, *refs):
    labels, terms, fans = refs[:inner], refs[inner : 2 * inner], refs[2 * inner : 2 * inner + outer - 1]
    outs, edge_ref = refs[2 * inner + outer - 1 : -1], refs[-1]
    o, c, z = ids[0], ids[1], ids[2]
    held = carry_ref.shape[0]
    count = terms[0].shape[1]
    group_first, group_last = block_rows(labels, z, True)
    block_first, block_last = block_rows(labels, z, grouped)
    marks = [r[count * DH : count * DH + LABELS, :].astype(F32) for r in fans]
    outer_last = [m[0:1] for m in marks]
    outer_first = [m[LABELS // 2 : LABELS // 2 + 1] for m in marks]
    newest = functools.reduce(jnp.maximum, group_last + outer_last)
    prior_base, later_base = jnp.zeros_like(newest), newest
    earlier = [(o ^ (d + 1)) < o for d in range(outer - 1)]
    for d in range(outer - 1):
        prior_base = jnp.maximum(prior_base, jnp.where(earlier[d], outer_last[d], 0.0))
        later_base = jnp.minimum(later_base, jnp.where(earlier[d], newest, outer_first[d]))
    priors, laters, plans = [], [], []
    for t in range(inner):
        prior, later = prior_base, later_base
        for d in range(inner):
            if d != t:
                before = (c ^ d) < (c ^ t)
                prior = jnp.maximum(prior, jnp.where(before, group_last[d], 0.0))
                later = jnp.minimum(later, jnp.where(before, newest, group_first[d]))
        forward = [(flag(jnp.logical_and(earlier[d], outer_last[d] == prior)), fans[d], None) for d in range(outer - 1)]
        backward = [
            (flag(jnp.logical_and(jnp.logical_not(earlier[d]), outer_first[d] == later)), fans[d], None)
            for d in range(outer - 1)
        ]
        for d in range(inner):
            if d != t:
                before = (c ^ d) < (c ^ t)
                forward.append((flag(jnp.logical_and(before, block_last[d] == prior)), terms[d], 0))
                backward.append((flag(jnp.logical_and(jnp.logical_not(before), block_first[d] == later)), terms[d], 1))
        take_f, take_b = prior == 0.0, later == newest
        if grouped:
            take_f = jnp.logical_and(take_f, jnp.logical_and(o == 0, (c ^ t) == 0))
            take_b = jnp.logical_and(take_b, jnp.logical_and(o == outer - 1, (c ^ t) == inner - 1))
        priors.append(prior)
        laters.append(later)
        plans.append((forward, backward, flag(take_f), flag(take_b) * factor))
    for s, g in enumerate(places):
        for i in range(part):
            at = s * part + i

            def carried(head, ref):
                place = head - z * held
                mine = jnp.logical_and(place >= 0, place < held)
                return jnp.where(mine, ref[jnp.clip(place, 0, held - 1)], 0.0)

            carries = (
                carried(g * unit + c * part + i, carry_ref),
                carried((g + shift) % total * unit + c * part + i, cot_ref),
            )

            def value(ref, side):
                return (ref[at * DH : (at + 1) * DH, :] if side is None else ref[side, at]).astype(F32)

            for t, out in enumerate(outs):
                for side in range(2):
                    amount = plans[t][2 + side] * carries[side]
                    for weight, ref, which in plans[t][side]:
                        amount = amount + weight * value(ref, which)
                    out[side, at] = amount.astype(BF16)
    edge_ref[0:1, :] = priors[0]
    edge_ref[1:2, :] = laters[0]
    edge_ref[2:8, :] = jnp.broadcast_to(newest, (6, DH))


def place_of(ids):
    z = ids[2]
    side = jnp.where(z >= DEPTH // 2, 1, 0)
    return z, side, jnp.logical_or(z == 0, z == DEPTH - 1)


def edge_rows(z, labels, edges):
    first, last = own_row(labels, z), own_row(labels, DEPTH + z)
    last_before = own_row(labels, DEPTH + jnp.maximum(z - 1, 0))
    first_after = own_row(labels, jnp.minimum(z + 1, DEPTH - 1))
    final_f, final_b = labels[2 * DEPTH - 1 : 2 * DEPTH, :], labels[0:1, :]
    prior = later = final_f
    if edges is not None:
        prior, later = edges[0:1, :], edges[1:2, :]
    return (last, last_before, final_f, first, prior), (first, first_after, final_b, last, later)


def pick(which, rows):
    return [jnp.where(which == 0, a, b) for a, b in zip(*rows)]


def hop(side, rows, lead, off, part, term_ref, prefix_ref, got_ref, out):
    own, neighbour, _, _, prior = pick(side, rows)
    other, _, final, _, _ = pick(1 - side, rows)
    join, keep, counts = flag(prior == own), flag(neighbour == own), flag(other == final)
    for i in range(part):
        state = term_ref[side, off + i].astype(F32)
        if lead:
            rest = counts * term_ref[1 - side, off + i].astype(F32)
        else:
            state = state + join * prefix_ref[side, off + i].astype(F32)
            rest = prefix_ref[1 - side, off + i].astype(F32)
        if got_ref is not None:
            state = state + keep * got_ref[0, i].astype(F32)
            rest = rest + got_ref[1, i].astype(F32)
        out[0, i] = state.astype(BF16)
        out[1, i] = rest.astype(BF16)


def hop_kernel(part, near, far, has_edges, ids, labels, *refs):
    z, side, at_end = place_of(ids)
    out, refs = refs[-1], list(refs[:-1])
    rows = edge_rows(z, labels, refs.pop(0) if has_edges else None)
    if near is not None:
        lead, off = near
        term = refs.pop(0)
        prefix = None if lead else refs.pop(0)

        @pl.when(at_end)
        def _():
            hop(side, rows, lead, off, part, term, prefix, None, out)

    if far is not None:
        lead, off, across = far
        term_far = refs.pop(0)
        prefix_far = None if lead else refs.pop(0)
        got = refs.pop(0)

        @pl.when(jnp.logical_not(at_end))
        def _():
            hop(side if across else 1 - side, rows, lead, off, part, term_far, prefix_far, got, out)


def lead_total_kernel(part, turns, ids, labels, *refs):
    z, side, at_end = place_of(ids)
    rows = edge_rows(z, labels, None)
    for t in range(turns):
        term, near, middle, far = refs[4 * t : 4 * t + 4]
        out = refs[4 * turns + t]

        def total(which, over, rest):
            own, neighbour, final, _, _ = pick(which, rows)
            counts, come = flag(own == final), flag(neighbour == final)
            for i in range(part):
                value = counts * term[which, i].astype(F32)
                if over is not None:
                    value = value + come * over[0, i].astype(F32)
                if rest is not None:
                    value = value + rest[1, i].astype(F32)
                out[which, i] = value.astype(BF16)

        @pl.when(at_end)
        def _():
            total(side, None, far)
            total(1 - side, far, None)

        @pl.when(jnp.logical_not(at_end))
        def _():
            total(side, near, middle)
            total(1 - side, middle, near)


def output_kernel(
    factor, base, part, turn, sides, ids, labels, edges, docs_ref, row_ref, q_ref, k_ref, v_ref, g_ref, *refs,
):
    sources = (refs[:4], refs[4:8])
    outs, (states, held, sems) = refs[-7:-3], refs[-3:]
    c = ids[1]
    z, side, at_end = place_of(ids)
    rows = edge_rows(z, labels, edges)

    for which in range(2):
        lead, off = sides[which]
        prefix, near, middle, far = sources[which]
        _, neighbour, _, target, prior = rows[which]
        reach, come = flag(prior == target), flag(neighbour == target)

        def state(over, rest):
            for i in range(part):
                value = reach * prefix[which, off + i].astype(F32)
                if over is not None:
                    value = value + come * over[0, i].astype(F32)
                if rest is not None and not lead:
                    value = value + reach * rest[1, i].astype(F32)
                states[which, i] = value.astype(BF16)

        near_side = side == which
        for condition, over, rest in (
            (jnp.logical_and(at_end, near_side), None, far),
            (jnp.logical_and(at_end, jnp.logical_not(near_side)), far, None),
            (jnp.logical_and(jnp.logical_not(at_end), near_side), near, middle),
            (jnp.logical_and(jnp.logical_not(at_end), jnp.logical_not(near_side)), middle, near),
        ):
            pl.when(condition)(functools.partial(state, over, rest))

    docs = docs_ref[...]
    in_first, in_last = document_masks(docs)
    places = lax.broadcasted_iota(jnp.int32, (SPAN, SPAN), 0)
    others = lax.broadcasted_iota(jnp.int32, (SPAN, SPAN), 1)
    allowed = jnp.logical_and(others <= places, docs == row_ref[0:1])
    head = base + (c ^ turn) * part
    copies = []
    for i in range(part):
        at = columns(head + i)
        q, k, v, g = q_ref[:, at], k_ref[:, at], v_ref[:, at], g_ref[:, at]
        before, after = states[0, i], states[1, i]
        scores = jnp.where(allowed, dot_transposed(q, k) * factor, 0.0).astype(BF16)
        grad_scores = jnp.where(allowed, dot_transposed(g, v) * factor, 0.0).astype(BF16)
        results = (
            dot(scores, v) + dot(jnp.where(in_first, q, 0), before),
            dot(grad_scores, k) + dot_transposed(jnp.where(in_first, g, 0), before),
            transposed_dot(grad_scores, q) + dot_transposed(jnp.where(in_last, v, 0), after),
            transposed_dot(scores, g) + dot(jnp.where(in_last, k, 0), after),
        )
        for n, result in enumerate(results):
            held[n, i] = result.astype(BF16)
            copy = pltpu.make_async_copy(held.at[n, i], outs[n].at[:, at], sems.at[n, i])
            copy.start()
            copies.append(copy)
    for copy in copies:
        copy.wait()


def shards(queries, keys, values, out_grad, doc_ids, carry_in, carry_cot):
    outer, inner, depth = (lax.axis_size(a) for a in ("outer", "inner", "heads"))
    assert depth == DEPTH
    tokens_all = doc_ids.shape[0] * outer * inner
    factor = float(DH * (tokens_all // 2)) ** (-0.5)
    head_count = queries.shape[1] // DH
    held = carry_in.shape[0]
    arrays = (queries, keys, values, out_grad)
    part = min(4, head_count // inner)
    unit = part * inner
    groups = head_count // unit
    leads = held % unit == 0
    shift = groups - 1 if leads else 0

    ids = jnp.stack([lax.axis_index(a) for a in ("outer", "inner", "heads")]).astype(jnp.int32)
    blocks = doc_ids.reshape(depth, SPAN)
    corners = jnp.concatenate([blocks[:, 0], blocks[:, -1]]).astype(F32)
    own_labels = jnp.broadcast_to(corners[:, None], (2 * depth, DH))
    labels = [own_labels] + [pairs(own_labels, "inner", d) for d in range(1, inner)]
    docs = lax.dynamic_index_in_dim(blocks, ids[2], 0, False)
    docs_column = jnp.broadcast_to(docs[:, None], (SPAN, DH))
    docs_row = jnp.broadcast_to(docs[None, :], (8, SPAN))

    levels = (outer - 1).bit_length()
    product = 2 * SPAN * DH * DH
    token = jnp.zeros((8, DH), F32) + 0.0 * own_labels[0, 0]

    def state_pair(count):
        return jax.ShapeDtypeStruct((2, count, DH, DH), BF16)

    terms, prefixes, near, middle, far = {}, {}, {}, {}, {}
    edge = None

    def exchange(own):
        return [own[0]] + [pairs(own[d], "inner", d) for d in range(1, inner)]

    def make_lead_terms():
        nonlocal token
        block = pltpu.VMEM((SPAN, unit * DH), BF16)
        carry = pltpu.VMEM((unit, DH, DH), F32)
        token, own = call(
            token,
            functools.partial(lead_terms, factor, unit, part, shift, outer, inner),
            (ids, docs_column, own_labels) + arrays + (carry_in, carry_cot),
            [state_pair(part)] * inner,
            2 * unit * product,
            scratch=[block] * 4 + [carry] * 2 + [pltpu.SemaphoreType.DMA((6,))],
            specs=[SMEM, VMEM, VMEM] + [ANY] * 6,
        )
        terms[0] = [(a, 0) for a in own]

    def make_terms(places):
        nonlocal token
        token, own = call(
            token,
            functools.partial(rest_terms, factor, unit, part, places, shift, groups),
            (ids, docs_column) + arrays,
            [state_pair(part * len(places))] * inner,
            2 * unit * len(places) * product,
        )
        for s, g in enumerate(places):
            terms[g] = [(a, s * part) for a in own]
        return exchange(own)

    def make_sums(received, grouped):
        nonlocal token
        count = received[0].shape[1]
        token, sums = call(
            token,
            functools.partial(sum_kernel, inner, levels, grouped),
            (ids, *labels, *received),
            [jax.ShapeDtypeStruct((count * DH + LABELS, DH), BF16)] * levels,
            count * DH * DH * 8,
        )
        return [pairs(sums[d.bit_length() - 1], "outer", d) for d in range(1, outer)]

    def make_prefixes(places, received, fans, grouped):
        nonlocal token, edge
        count = received[0].shape[1]
        token, given = call(
            token,
            functools.partial(
                prefix_kernel, factor, unit, part, places, shift, groups, inner, outer, grouped
            ),
            (ids, carry_in, carry_cot, *labels, *received, *fans),
            [state_pair(count)] * inner + [jax.ShapeDtypeStruct((8, DH), F32)],
            count * DH * DH * 16 * inner,
        )
        edge = given[-1] if edge is None else edge
        given = exchange(given[:-1])
        for s, g in enumerate(places):
            prefixes[g] = [(a, s * part) for a in given]

    def operands_of(chunk):
        g, t = chunk
        lead = leads and g == 0
        array, off = terms[g][t]
        return lead, off, [array] if lead else [array, prefixes[g][t][0]]

    def move(near_chunk, far_chunk, across, perm):
        nonlocal token
        use_edges = any(c is not None and not (leads and c[0] == 0) for c in (near_chunk, far_chunk))
        operands = [ids, own_labels] + ([edge] if use_edges else [])
        near_plan = far_plan = None
        if near_chunk is not None:
            lead, off, more = operands_of(near_chunk)
            near_plan = (lead, off)
            operands += more
        if far_chunk is not None:
            lead, off, more = operands_of(far_chunk)
            far_plan = (lead, off, across)
            operands += more + [near[far_chunk] if across else middle[far_chunk]]
        token, sent = call(
            token,
            functools.partial(hop_kernel, part, near_plan, far_plan, use_edges),
            operands,
            [state_pair(part)],
            part * DH * DH * 8,
        )
        return lax.ppermute(sent[0], "heads", perm)

    def ends(near_chunk, far_chunk):
        perm = ([(0, 1), (3, 2)] if near_chunk is not None else []) + ([(1, 0), (2, 3)] if far_chunk is not None else [])
        got = move(near_chunk, far_chunk, False, perm)
        if near_chunk is not None:
            near[near_chunk] = got
        if far_chunk is not None:
            far[far_chunk] = got

    def across(chunk):
        middle[chunk] = move(None, chunk, True, [(1, 2), (2, 1)])

    out_shape = jax.ShapeDtypeStruct(queries.shape, BF16)
    results = ()

    def make_outputs(g, t):
        nonlocal token, results
        operands = (ids, own_labels, edge, docs_column, docs_row) + arrays
        sides = []
        for chunk in ((g, t), ((g - shift) % groups, t)):
            lead = leads and chunk[0] == 0
            array, off = prefixes[chunk[0]][t]
            sides.append((lead, off))
            operands += (array, near[chunk], middle[chunk], far[chunk])
        token, results = call(
            token,
            functools.partial(output_kernel, factor, g * unit, part, t, tuple(sides)),
            operands + tuple(results),
            [out_shape] * 4,
            10 * part * product,
            scratch=[
                pltpu.VMEM((2, part, DH, DH), BF16),
                pltpu.VMEM((4, part, SPAN, DH), BF16),
                pltpu.SemaphoreType.DMA((4, part)),
            ],
            aliases={len(operands) + i: i for i in range(len(results))},
            specs=[SMEM] + [VMEM] * (len(operands) - 1) + [ANY] * len(results),
            out_specs=[ANY] * 4,
        )

    if leads and groups == 4 and inner == 2:
        make_lead_terms()
        ends((0, 0), None)
        ends((0, 1), None)
        got_a = make_terms((1,))
        got_b = make_terms((2, 3))
        fans_a = make_sums(got_a, False)
        across((0, 0))
        fans_b = make_sums(got_b, False)
        across((0, 1))
        make_prefixes((1,), got_a, fans_a, False)
        ends((1, 0), (0, 0))
        ends((1, 1), (0, 1))
        make_prefixes((2, 3), got_b, fans_b, False)
        across((1, 0))
        token, totals = call(
            token,
            functools.partial(lead_total_kernel, part, inner),
            [ids, own_labels]
            + [a for t in range(inner) for a in (terms[0][t][0], near[0, t], middle[0, t], far[0, t])],
            [state_pair(part)] * inner,
            unit * DH * DH * 8,
        )
        got_lead = exchange(totals)
        across((1, 1))
        ends((2, 0), None)
        fans_lead = make_sums(got_lead, True)
        ends((2, 1), (1, 0))
        across((2, 0))
        ends((3, 0), (1, 1))
        across((2, 1))
        make_prefixes((0,), got_lead, fans_lead, True)
        make_outputs(0, 0)
        ends((3, 1), (2, 0))
        across((3, 0))
        make_outputs(0, 1)
        ends(None, (2, 1))
        across((3, 1))
        make_outputs(1, 0)
        ends(None, (3, 0))
        make_outputs(1, 1)
        ends(None, (3, 1))
        make_outputs(2, 0)
        make_outputs(3, 0)
        make_outputs(2, 1)
        make_outputs(3, 1)
    else:
        assert not leads
        for g in range(groups):
            got = make_terms((g,))
            make_prefixes((g,), got, make_sums(got, False), False)
        chunks = [(g, t) for g in range(groups) for t in range(inner)]
        lag = 4
        for k in range(len(chunks) + lag):
            ends(chunks[k] if k < len(chunks) else None, chunks[k - lag] if k >= lag else None)
            if k < len(chunks):
                across(chunks[k])
        for g, t in chunks:
            make_outputs(g, t)
    return tuple(results)


def solution(mesh):
    tokens = P(("outer", "inner", "heads"), None)
    carry = P("heads", None, None)
    return jax.shard_map(
        shards,
        mesh=mesh,
        in_specs=(tokens,) * 4 + (P(("outer", "inner")), carry, carry),
        out_specs=(tokens,) * 4,
        check_vma=False,
    )
```

```python
import functools

import jax
import jax.numpy as jnp
from jax import lax
from jax.experimental import pallas as pl
from jax.experimental.pallas import tpu as pltpu
from jax.sharding import PartitionSpec as P

DH = 128
SPAN = 128
LABELS = 16
DEPTH = 4
F32 = jnp.float32
BF16 = jnp.bfloat16
VMEM = pl.BlockSpec(memory_space=pltpu.VMEM)
SMEM = pl.BlockSpec(memory_space=pltpu.SMEM)
HBM = pl.BlockSpec(memory_space=pltpu.HBM)
LIMIT = 24 * 1024 * 1024


def pairs(array, axis, distance):
    count = lax.axis_size(axis)
    return lax.ppermute(array, axis, [(i, i ^ distance) for i in range(count)])


def transposed_dot(a, b):
    return lax.dot_general(a, b, (((0,), (0,)), ((), ())), preferred_element_type=F32)


def dot_transposed(a, b):
    return lax.dot_general(a, b, (((1,), (1,)), ((), ())), preferred_element_type=F32)


def dot(a, b):
    return lax.dot_general(a, b, (((1,), (0,)), ((), ())), preferred_element_type=F32)


def flag(row):
    return jnp.where(row, 1.0, 0.0).astype(F32)


def call(token, kernel, operands, out_shape, scratch=(), aliases=None, specs=None, out_specs=None):
    count, results = len(operands), len(out_shape)

    def ordered(*refs):
        kernel(*refs[:count], *refs[count + 1 : count + 1 + results], *refs[count + 2 + results :])

    *outs, token = pl.pallas_call(
        ordered,
        in_specs=list(specs or [SMEM] + [VMEM] * (count - 1)) + [VMEM],
        out_specs=list(out_specs or [VMEM] * results) + [VMEM],
        out_shape=list(out_shape) + [jax.ShapeDtypeStruct(token.shape, token.dtype)],
        scratch_shapes=list(scratch),
        input_output_aliases={**(aliases or {}), count: results},
        compiler_params=pltpu.CompilerParams(vmem_limit_bytes=LIMIT),
        cost_estimate=pl.CostEstimate(flops=0, bytes_accessed=0, transcendentals=0),
    )(*operands, token)
    return token, outs


def document_masks(docs):
    return docs == docs[0:1], docs == docs[SPAN - 1 : SPAN]


def columns(head):
    return pl.ds(pl.multiple_of(head * DH, DH), DH)


def own_row(ref, at):
    return ref[pl.ds(at, 1), :]


def label_kernel(ids, docs_ref, labels_ref, column_ref, row_ref):
    docs = docs_ref[...]
    for k in range(DEPTH):
        row = docs[k : k + 1, :].astype(F32)
        labels_ref[k : k + 1, :] = jnp.broadcast_to(row[:, 0:1], (1, DH))
        labels_ref[DEPTH + k : DEPTH + k + 1, :] = jnp.broadcast_to(row[:, SPAN - 1 :], (1, DH))
    own = own_row(docs_ref, ids[2]).astype(F32)
    column_ref[...] = jnp.broadcast_to(own, (SPAN, SPAN)).T
    row_ref[...] = jnp.broadcast_to(own, (8, SPAN))


def fetch(pairs_of_refs, sems):
    copies = [pltpu.make_async_copy(source, target, sems.at[n]) for n, (source, target) in enumerate(pairs_of_refs)]
    for copy in copies:
        copy.start()
    return copies


def add_terms(factor, part, docs_ref, c, q_ref, k_ref, v_ref, g_ref, outs, off, extra=None):
    in_first, in_last = document_masks(docs_ref[...])
    for t, out in enumerate(outs):
        for i in range(part):
            at = columns((c ^ t) * part + i)
            forward = transposed_dot(jnp.where(in_last, k_ref[:, at], 0), v_ref[:, at]) * factor
            backward = transposed_dot(jnp.where(in_first, q_ref[:, at], 0), g_ref[:, at]) * factor
            if extra is not None:
                add_f, add_b = extra((c ^ t) * part + i)
                forward, backward = forward + add_f, backward + add_b
            out[0, off + i] = forward.astype(BF16)
            out[1, off + i] = backward.astype(BF16)


def group_columns(group, unit):
    return pl.ds(group * unit * DH, unit * DH)


def rest_terms(factor, unit, part, places, shift, total, ids, docs_ref, q_hbm, k_hbm, v_hbm, g_hbm, *refs):
    outs, (q_ref, k_ref, v_ref, g_ref, sems) = refs[:-5], refs[-5:]
    waiting = []
    for s, g in enumerate(places):
        forward, backward = group_columns(g, unit), group_columns((g + shift) % total, unit)
        waiting.append(fetch(
            [
                (k_hbm.at[:, forward], k_ref.at[s]), (v_hbm.at[:, forward], v_ref.at[s]),
                (q_hbm.at[:, backward], q_ref.at[s]), (g_hbm.at[:, backward], g_ref.at[s]),
            ],
            sems.at[s],
        ))
    for s in range(len(places)):
        for copy in waiting[s]:
            copy.wait()
        add_terms(
            factor, part, docs_ref, ids[1], q_ref.at[s], k_ref.at[s], v_ref.at[s], g_ref.at[s], outs, s * part
        )


def lead_terms(
    factor, unit, part, shift, outer, inner, ids, docs_ref, labels, q_hbm, k_hbm, v_hbm, g_hbm, carry_hbm, cot_hbm, *refs,
):
    outs, (q_ref, k_ref, v_ref, g_ref, carry_ref, cot_ref, sems) = refs[:inner], refs[inner:]
    o, c, z = ids[0], ids[1], ids[2]
    held = carry_hbm.shape[0]
    forward, backward = group_columns(0, unit), group_columns(shift, unit)
    copies = fetch(
        [
            (k_hbm.at[:, forward], k_ref), (v_hbm.at[:, forward], v_ref),
            (q_hbm.at[:, backward], q_ref), (g_hbm.at[:, backward], g_ref),
            (carry_hbm.at[pl.ds(0, unit)], carry_ref), (cot_hbm.at[pl.ds(held - unit, unit)], cot_ref),
        ],
        sems,
    )
    for copy in copies:
        copy.wait()
    first, last = own_row(labels, z), own_row(labels, DEPTH + z)
    opens = jnp.logical_and(jnp.logical_and(o == 0, c == 0), z == 0)
    closes = jnp.logical_and(jnp.logical_and(o == outer - 1, c == inner - 1), z == DEPTH - 1)
    open_f = flag(jnp.logical_and(opens, last == 0.0))
    close_b = flag(jnp.logical_and(closes, first == last)) * factor

    def extra(place):
        return open_f * carry_ref[place], close_b * cot_ref[place]

    add_terms(factor, part, docs_ref, c, q_ref, k_ref, v_ref, g_ref, outs, 0, extra)


def block_rows(labels, z, grouped):
    if grouped:
        return [l[0:1, :] for l in labels], [l[2 * DEPTH - 1 : 2 * DEPTH, :] for l in labels]
    return [own_row(l, z) for l in labels], [own_row(l, DEPTH + z) for l in labels]


def sum_kernel(inner, levels, grouped, ids, *refs):
    labels, terms, outs = refs[:inner], refs[inner : 2 * inner], refs[2 * inner :]
    o, z = ids[0], ids[2]
    count = terms[0].shape[1]
    newest = functools.reduce(jnp.maximum, [l[2 * DEPTH - 1 : 2 * DEPTH, :] for l in labels])
    oldest = functools.reduce(jnp.minimum, [l[0:1, :] for l in labels])
    firsts, lasts = block_rows(labels, z, grouped)
    keep_f = [flag(l == newest) for l in lasts]
    keep_b = [flag(l == oldest) for l in firsts]
    low = [((o >> level) & 1) == 0 for level in range(levels)]
    for i in range(count):
        sum_f = sum(m * r[0, i].astype(F32) for m, r in zip(keep_f, terms)).astype(BF16)
        sum_b = sum(m * r[1, i].astype(F32) for m, r in zip(keep_b, terms)).astype(BF16)
        for chosen, out in zip(low, outs):
            out[i * DH : (i + 1) * DH, :] = jnp.where(chosen, sum_f, sum_b)
    rows = lax.broadcasted_iota(jnp.int32, (LABELS, DH), 0)
    marks = jnp.where(rows < LABELS // 2, jnp.broadcast_to(newest, (LABELS, DH)), jnp.broadcast_to(oldest, (LABELS, DH)))
    for out in outs:
        out[count * DH :, :] = marks.astype(BF16)


def prefix_kernel(factor, unit, part, places, shift, total, inner, outer, grouped, ids, carry_ref, cot_ref, *refs):
    labels, terms, fans = refs[:inner], refs[inner : 2 * inner], refs[2 * inner : 2 * inner + outer - 1]
    outs, edge_ref = refs[2 * inner + outer - 1 : -1], refs[-1]
    o, c, z = ids[0], ids[1], ids[2]
    held = carry_ref.shape[0]
    count = terms[0].shape[1]
    group_first, group_last = block_rows(labels, z, True)
    block_first, block_last = block_rows(labels, z, grouped)
    marks = [r[count * DH : count * DH + LABELS, :].astype(F32) for r in fans]
    outer_last = [m[0:1] for m in marks]
    outer_first = [m[LABELS // 2 : LABELS // 2 + 1] for m in marks]
    newest = functools.reduce(jnp.maximum, group_last + outer_last)
    prior_base, later_base = jnp.zeros_like(newest), newest
    earlier = [(o ^ (d + 1)) < o for d in range(outer - 1)]
    for d in range(outer - 1):
        prior_base = jnp.maximum(prior_base, jnp.where(earlier[d], outer_last[d], 0.0))
        later_base = jnp.minimum(later_base, jnp.where(earlier[d], newest, outer_first[d]))
    priors, laters, plans = [], [], []
    for t in range(inner):
        prior, later = prior_base, later_base
        for d in range(inner):
            if d != t:
                before = (c ^ d) < (c ^ t)
                prior = jnp.maximum(prior, jnp.where(before, group_last[d], 0.0))
                later = jnp.minimum(later, jnp.where(before, newest, group_first[d]))
        forward = [(flag(jnp.logical_and(earlier[d], outer_last[d] == prior)), fans[d], None) for d in range(outer - 1)]
        backward = [
            (flag(jnp.logical_and(jnp.logical_not(earlier[d]), outer_first[d] == later)), fans[d], None)
            for d in range(outer - 1)
        ]
        for d in range(inner):
            if d != t:
                before = (c ^ d) < (c ^ t)
                forward.append((flag(jnp.logical_and(before, block_last[d] == prior)), terms[d], 0))
                backward.append((flag(jnp.logical_and(jnp.logical_not(before), block_first[d] == later)), terms[d], 1))
        take_f, take_b = prior == 0.0, later == newest
        if grouped:
            take_f = jnp.logical_and(take_f, jnp.logical_and(o == 0, (c ^ t) == 0))
            take_b = jnp.logical_and(take_b, jnp.logical_and(o == outer - 1, (c ^ t) == inner - 1))
        priors.append(prior)
        laters.append(later)
        plans.append((forward, backward, flag(take_f), flag(take_b) * factor))
    for s, g in enumerate(places):
        for i in range(part):
            at = s * part + i

            def carried(head, ref):
                place = head - z * held
                mine = jnp.logical_and(place >= 0, place < held)
                return jnp.where(mine, ref[jnp.clip(place, 0, held - 1)], 0.0)

            carries = (
                carried(g * unit + c * part + i, carry_ref),
                carried((g + shift) % total * unit + c * part + i, cot_ref),
            )

            def value(ref, side):
                return (ref[at * DH : (at + 1) * DH, :] if side is None else ref[side, at]).astype(F32)

            for t, out in enumerate(outs):
                for side in range(2):
                    amount = plans[t][2 + side] * carries[side]
                    for weight, ref, which in plans[t][side]:
                        amount = amount + weight * value(ref, which)
                    out[side, at] = amount.astype(BF16)
    edge_ref[0:1, :] = priors[0]
    edge_ref[1:2, :] = laters[0]
    edge_ref[2:8, :] = jnp.broadcast_to(newest, (6, DH))


def place_of(ids):
    z = ids[2]
    side = jnp.where(z >= DEPTH // 2, 1, 0)
    return z, side, jnp.logical_or(z == 0, z == DEPTH - 1)


def edge_rows(z, labels, edges):
    first, last = own_row(labels, z), own_row(labels, DEPTH + z)
    last_before = own_row(labels, DEPTH + jnp.maximum(z - 1, 0))
    first_after = own_row(labels, jnp.minimum(z + 1, DEPTH - 1))
    final_f, final_b = labels[2 * DEPTH - 1 : 2 * DEPTH, :], labels[0:1, :]
    prior = later = final_f
    if edges is not None:
        prior, later = edges[0:1, :], edges[1:2, :]
    return (last, last_before, final_f, first, prior), (first, first_after, final_b, last, later)


def pick(which, rows):
    return [jnp.where(which == 0, a, b) for a, b in zip(*rows)]


def hop(side, rows, lead, off, part, term_ref, prefix_ref, got_ref, out):
    own, neighbour, _, _, prior = pick(side, rows)
    other, _, final, _, _ = pick(1 - side, rows)
    join, keep, counts = flag(prior == own), flag(neighbour == own), flag(other == final)
    for i in range(part):
        state = term_ref[side, off + i].astype(F32)
        if lead:
            rest = counts * term_ref[1 - side, off + i].astype(F32)
        else:
            state = state + join * prefix_ref[side, off + i].astype(F32)
            rest = prefix_ref[1 - side, off + i].astype(F32)
        if got_ref is not None:
            state = state + keep * got_ref[0, i].astype(F32)
            rest = rest + got_ref[1, i].astype(F32)
        out[0, i] = state.astype(BF16)
        out[1, i] = rest.astype(BF16)


def hop_kernel(part, near, far, has_edges, ids, labels, *refs):
    z, side, at_end = place_of(ids)
    out, refs = refs[-1], list(refs[:-1])
    rows = edge_rows(z, labels, refs.pop(0) if has_edges else None)
    if near is not None:
        lead, off = near
        term = refs.pop(0)
        prefix = None if lead else refs.pop(0)

        @pl.when(at_end)
        def _():
            hop(side, rows, lead, off, part, term, prefix, None, out)

    if far is not None:
        lead, off, across = far
        term_far = refs.pop(0)
        prefix_far = None if lead else refs.pop(0)
        got = refs.pop(0)

        @pl.when(jnp.logical_not(at_end))
        def _():
            hop(side if across else 1 - side, rows, lead, off, part, term_far, prefix_far, got, out)


def lead_total_kernel(part, turns, ids, labels, *refs):
    z, side, at_end = place_of(ids)
    rows = edge_rows(z, labels, None)
    for t in range(turns):
        term, near, middle, far = refs[4 * t : 4 * t + 4]
        out = refs[4 * turns + t]

        def total(which, over, rest):
            own, neighbour, final, _, _ = pick(which, rows)
            counts, come = flag(own == final), flag(neighbour == final)
            for i in range(part):
                value = counts * term[which, i].astype(F32)
                if over is not None:
                    value = value + come * over[0, i].astype(F32)
                if rest is not None:
                    value = value + rest[1, i].astype(F32)
                out[which, i] = value.astype(BF16)

        @pl.when(at_end)
        def _():
            total(side, None, far)
            total(1 - side, far, None)

        @pl.when(jnp.logical_not(at_end))
        def _():
            total(side, near, middle)
            total(1 - side, middle, near)


def output_kernel(
    factor, base, part, turn, sides, ids, labels, edges, docs_ref, row_ref, q_hbm, k_hbm, v_hbm, g_hbm, *refs,
):
    sources = (refs[:4], refs[4:8])
    outs, (q_ref, k_ref, v_ref, g_ref, states, held, sems, in_sems) = refs[-12:-8], refs[-8:]
    c = ids[1]
    head = base + (c ^ turn) * part
    own = pl.ds(pl.multiple_of(head * DH, part * DH), part * DH)
    waiting = fetch(
        [
            (q_hbm.at[:, own], q_ref), (k_hbm.at[:, own], k_ref),
            (v_hbm.at[:, own], v_ref), (g_hbm.at[:, own], g_ref),
        ],
        in_sems,
    )
    z, side, at_end = place_of(ids)
    rows = edge_rows(z, labels, edges)

    for which in range(2):
        lead, off = sides[which]
        prefix, near, middle, far = sources[which]
        _, neighbour, _, target, prior = rows[which]
        reach, come = flag(prior == target), flag(neighbour == target)

        def state(over, rest):
            for i in range(part):
                value = reach * prefix[which, off + i].astype(F32)
                if over is not None:
                    value = value + come * over[0, i].astype(F32)
                if rest is not None and not lead:
                    value = value + reach * rest[1, i].astype(F32)
                states[which, i] = value.astype(BF16)

        near_side = side == which
        for condition, over, rest in (
            (jnp.logical_and(at_end, near_side), None, far),
            (jnp.logical_and(at_end, jnp.logical_not(near_side)), far, None),
            (jnp.logical_and(jnp.logical_not(at_end), near_side), near, middle),
            (jnp.logical_and(jnp.logical_not(at_end), jnp.logical_not(near_side)), middle, near),
        ):
            pl.when(condition)(functools.partial(state, over, rest))

    docs = docs_ref[...]
    in_first, in_last = document_masks(docs)
    places = lax.broadcasted_iota(jnp.int32, (SPAN, SPAN), 0)
    others = lax.broadcasted_iota(jnp.int32, (SPAN, SPAN), 1)
    allowed = jnp.logical_and(others <= places, docs == row_ref[0:1])
    for copy in waiting:
        copy.wait()
    copies = []
    for i in range(part):
        at, to = slice(i * DH, (i + 1) * DH), columns(head + i)
        q, k, v, g = q_ref[:, at], k_ref[:, at], v_ref[:, at], g_ref[:, at]
        before, after = states[0, i], states[1, i]
        scores = jnp.where(allowed, dot_transposed(q, k) * factor, 0.0).astype(BF16)
        grad_scores = jnp.where(allowed, dot_transposed(g, v) * factor, 0.0).astype(BF16)
        results = (
            dot(scores, v) + dot(jnp.where(in_first, q, 0), before),
            dot(grad_scores, k) + dot_transposed(jnp.where(in_first, g, 0), before),
            transposed_dot(grad_scores, q) + dot_transposed(jnp.where(in_last, v, 0), after),
            transposed_dot(scores, g) + dot(jnp.where(in_last, k, 0), after),
        )
        for n, result in enumerate(results):
            held[n, i] = result.astype(BF16)
            copy = pltpu.make_async_copy(held.at[n, i], outs[n].at[:, to], sems.at[n, i])
            copy.start()
            copies.append(copy)
    for copy in copies:
        copy.wait()


def shards(queries, keys, values, out_grad, doc_ids, carry_in, carry_cot):
    outer, inner, depth = (lax.axis_size(a) for a in ("outer", "inner", "heads"))
    assert depth == DEPTH
    tokens_all = doc_ids.shape[0] * outer * inner
    factor = float(DH * (tokens_all // 2)) ** (-0.5)
    head_count = queries.shape[1] // DH
    held = carry_in.shape[0]
    arrays = (queries, keys, values, out_grad)
    part = min(4, head_count // inner)
    unit = part * inner
    groups = head_count // unit
    leads = held % unit == 0
    shift = groups - 1 if leads else 0

    ids = jnp.stack([lax.axis_index(a) for a in ("outer", "inner", "heads")]).astype(jnp.int32)
    token, (own_labels, docs_column, docs_row) = call(
        jnp.zeros((8, DH), F32),
        label_kernel,
        (ids, doc_ids.reshape(depth, SPAN)),
        [
            jax.ShapeDtypeStruct((2 * depth, DH), F32),
            jax.ShapeDtypeStruct((SPAN, SPAN), F32),
            jax.ShapeDtypeStruct((8, SPAN), F32),
        ],
    )
    labels = [own_labels] + [pairs(own_labels, "inner", d) for d in range(1, inner)]

    levels = (outer - 1).bit_length()

    def state_pair(count):
        return jax.ShapeDtypeStruct((2, count, DH, DH), BF16)

    terms, prefixes, near, middle, far = {}, {}, {}, {}, {}
    edge = None

    def exchange(own):
        return [own[0]] + [pairs(own[d], "inner", d) for d in range(1, inner)]

    def make_lead_terms():
        nonlocal token
        block = pltpu.VMEM((SPAN, unit * DH), BF16)
        carry = pltpu.VMEM((unit, DH, DH), F32)
        token, own = call(
            token,
            functools.partial(lead_terms, factor, unit, part, shift, outer, inner),
            (ids, docs_column, own_labels) + arrays + (carry_in, carry_cot),
            [state_pair(part)] * inner,
            scratch=[block] * 4 + [carry] * 2 + [pltpu.SemaphoreType.DMA((6,))],
            specs=[SMEM, VMEM, VMEM] + [HBM] * 6,
        )
        terms[0] = [(a, 0) for a in own]

    def make_terms(places):
        nonlocal token
        token, own = call(
            token,
            functools.partial(rest_terms, factor, unit, part, places, shift, groups),
            (ids, docs_column) + arrays,
            [state_pair(part * len(places))] * inner,
            scratch=[pltpu.VMEM((len(places), SPAN, unit * DH), BF16)] * 4
            + [pltpu.SemaphoreType.DMA((len(places), 4))],
            specs=[SMEM, VMEM] + [HBM] * 4,
        )
        for s, g in enumerate(places):
            terms[g] = [(a, s * part) for a in own]
        return exchange(own)

    def make_sums(received, grouped):
        nonlocal token
        count = received[0].shape[1]
        token, sums = call(
            token,
            functools.partial(sum_kernel, inner, levels, grouped),
            (ids, *labels, *received),
            [jax.ShapeDtypeStruct((count * DH + LABELS, DH), BF16)] * levels,
        )
        return [pairs(sums[d.bit_length() - 1], "outer", d) for d in range(1, outer)]

    def make_prefixes(places, received, fans, grouped):
        nonlocal token, edge
        count = received[0].shape[1]
        token, given = call(
            token,
            functools.partial(
                prefix_kernel, factor, unit, part, places, shift, groups, inner, outer, grouped
            ),
            (ids, carry_in, carry_cot, *labels, *received, *fans),
            [state_pair(count)] * inner + [jax.ShapeDtypeStruct((8, DH), F32)],
        )
        edge = given[-1] if edge is None else edge
        given = exchange(given[:-1])
        for s, g in enumerate(places):
            prefixes[g] = [(a, s * part) for a in given]

    def operands_of(chunk):
        g, t = chunk
        lead = leads and g == 0
        array, off = terms[g][t]
        return lead, off, [array] if lead else [array, prefixes[g][t][0]]

    def move(near_chunk, far_chunk, across, perm):
        nonlocal token
        use_edges = any(c is not None and not (leads and c[0] == 0) for c in (near_chunk, far_chunk))
        operands = [ids, own_labels] + ([edge] if use_edges else [])
        near_plan = far_plan = None
        if near_chunk is not None:
            lead, off, more = operands_of(near_chunk)
            near_plan = (lead, off)
            operands += more
        if far_chunk is not None:
            lead, off, more = operands_of(far_chunk)
            far_plan = (lead, off, across)
            operands += more + [near[far_chunk] if across else middle[far_chunk]]
        token, sent = call(
            token,
            functools.partial(hop_kernel, part, near_plan, far_plan, use_edges),
            operands,
            [state_pair(part)],
        )
        return lax.ppermute(sent[0], "heads", perm)

    def ends(near_chunk, far_chunk):
        perm = ([(0, 1), (3, 2)] if near_chunk is not None else []) + ([(1, 0), (2, 3)] if far_chunk is not None else [])
        got = move(near_chunk, far_chunk, False, perm)
        if near_chunk is not None:
            near[near_chunk] = got
        if far_chunk is not None:
            far[far_chunk] = got

    def across(chunk):
        middle[chunk] = move(None, chunk, True, [(1, 2), (2, 1)])

    out_shape = jax.ShapeDtypeStruct(queries.shape, BF16)
    results = ()

    def make_outputs(g, t):
        nonlocal token, results
        operands = (ids, own_labels, edge, docs_column, docs_row) + arrays
        sides = []
        for chunk in ((g, t), ((g - shift) % groups, t)):
            lead = leads and chunk[0] == 0
            array, off = prefixes[chunk[0]][t]
            sides.append((lead, off))
            operands += (array, near[chunk], middle[chunk], far[chunk])
        token, results = call(
            token,
            functools.partial(output_kernel, factor, g * unit, part, t, tuple(sides)),
            operands + tuple(results),
            [out_shape] * 4,
            scratch=[pltpu.VMEM((SPAN, part * DH), BF16)] * 4
            + [
                pltpu.VMEM((2, part, DH, DH), BF16),
                pltpu.VMEM((4, part, SPAN, DH), BF16),
                pltpu.SemaphoreType.DMA((4, part)),
                pltpu.SemaphoreType.DMA((4,)),
            ],
            aliases={len(operands) + i: i for i in range(len(results))},
            specs=[SMEM] + [VMEM] * 4 + [HBM] * 4 + [VMEM] * 8 + [HBM] * len(results),
            out_specs=[HBM] * 4,
        )

    if leads and groups == 4 and inner == 2:
        make_lead_terms()
        ends((0, 0), None)
        ends((0, 1), None)
        rest = tuple(range(1, groups))
        got_rest = make_terms(rest)
        fans_rest = make_sums(got_rest, False)
        across((0, 0))
        across((0, 1))
        ends(None, (0, 0))
        ends(None, (0, 1))
        make_prefixes(rest, got_rest, fans_rest, False)
        ends((1, 0), None)
        ends((2, 0), None)
        token, totals = call(
            token,
            functools.partial(lead_total_kernel, part, inner),
            [ids, own_labels]
            + [a for t in range(inner) for a in (terms[0][t][0], near[0, t], middle[0, t], far[0, t])],
            [state_pair(part)] * inner,
        )
        got_lead = exchange(totals)
        across((1, 0))
        ends((3, 0), None)
        across((2, 0))
        fans_lead = make_sums(got_lead, True)
        ends((1, 1), (1, 0))
        across((3, 0))
        make_prefixes((0,), got_lead, fans_lead, True)
        ends((2, 1), (2, 0))
        across((1, 1))
        make_outputs(0, 0)
        ends((3, 1), (3, 0))
        across((2, 1))
        make_outputs(1, 0)
        ends(None, (1, 1))
        across((3, 1))
        make_outputs(2, 0)
        make_outputs(3, 0)
        ends(None, (2, 1))
        ends(None, (3, 1))
        make_outputs(0, 1)
        make_outputs(1, 1)
        make_outputs(2, 1)
        make_outputs(3, 1)
    else:
        assert not leads
        for g in range(groups):
            got = make_terms((g,))
            make_prefixes((g,), got, make_sums(got, False), False)
        chunks = [(g, t) for g in range(groups) for t in range(inner)]
        lag = 4
        for k in range(len(chunks) + lag):
            ends(chunks[k] if k < len(chunks) else None, chunks[k - lag] if k >= lag else None)
            if k < len(chunks):
                across(chunks[k])
        for g, t in chunks:
            make_outputs(g, t)
    return tuple(results)


def solution(mesh):
    tokens = P(("outer", "inner", "heads"), None)
    carry = P("heads", None, None)
    return jax.shard_map(
        shards,
        mesh=mesh,
        in_specs=(tokens,) * 4 + (P(("outer", "inner")), carry, carry),
        out_specs=(tokens,) * 4,
        check_vma=False,
    )
```

```python
import functools

import jax
import jax.numpy as jnp
from jax import lax
from jax.experimental import pallas as pl
from jax.experimental.pallas import tpu as pltpu
from jax.sharding import PartitionSpec as P

DH = 128
SPAN = 128
LABELS = 16
DEPTH = 4
F32 = jnp.float32
BF16 = jnp.bfloat16
VMEM = pl.BlockSpec(memory_space=pltpu.VMEM)
SMEM = pl.BlockSpec(memory_space=pltpu.SMEM)
HBM = pl.BlockSpec(memory_space=pltpu.HBM)
LIMIT = 24 * 1024 * 1024


def pairs(array, axis, distance):
    count = lax.axis_size(axis)
    return lax.ppermute(array, axis, [(i, i ^ distance) for i in range(count)])


def transposed_dot(a, b):
    return lax.dot_general(a, b, (((0,), (0,)), ((), ())), preferred_element_type=F32)


def dot_transposed(a, b):
    return lax.dot_general(a, b, (((1,), (1,)), ((), ())), preferred_element_type=F32)


def dot(a, b):
    return lax.dot_general(a, b, (((1,), (0,)), ((), ())), preferred_element_type=F32)


def flag(row):
    return jnp.where(row, 1.0, 0.0).astype(F32)


def call(token, kernel, operands, out_shape, scratch=(), aliases=None, specs=None, out_specs=None):
    count, results = len(operands), len(out_shape)

    def ordered(*refs):
        kernel(*refs[:count], *refs[count + 1 : count + 1 + results], *refs[count + 2 + results :])

    *outs, token = pl.pallas_call(
        ordered,
        in_specs=list(specs or [SMEM] + [VMEM] * (count - 1)) + [VMEM],
        out_specs=list(out_specs or [VMEM] * results) + [VMEM],
        out_shape=list(out_shape) + [jax.ShapeDtypeStruct(token.shape, token.dtype)],
        scratch_shapes=list(scratch),
        input_output_aliases={**(aliases or {}), count: results},
        compiler_params=pltpu.CompilerParams(vmem_limit_bytes=LIMIT),
        cost_estimate=pl.CostEstimate(flops=0, bytes_accessed=0, transcendentals=0),
    )(*operands, token)
    return token, outs


def document_masks(docs):
    return docs == docs[0:1], docs == docs[SPAN - 1 : SPAN]


def columns(head):
    return pl.ds(pl.multiple_of(head * DH, DH), DH)


def own_row(ref, at):
    return ref[pl.ds(at, 1), :]


def label_kernel(ids, docs_ref, labels_ref, column_ref, row_ref):
    docs = docs_ref[...]
    for k in range(DEPTH):
        row = docs[k : k + 1, :].astype(F32)
        labels_ref[k : k + 1, :] = jnp.broadcast_to(row[:, 0:1], (1, DH))
        labels_ref[DEPTH + k : DEPTH + k + 1, :] = jnp.broadcast_to(row[:, SPAN - 1 :], (1, DH))
    own = own_row(docs_ref, ids[2]).astype(F32)
    column_ref[...] = jnp.broadcast_to(own, (SPAN, SPAN)).T
    row_ref[...] = jnp.broadcast_to(own, (8, SPAN))


def fetch(pairs_of_refs, sems):
    copies = [pltpu.make_async_copy(source, target, sems.at[n]) for n, (source, target) in enumerate(pairs_of_refs)]
    for copy in copies:
        copy.start()
    return copies


def add_terms(factor, part, docs_ref, c, q_ref, k_ref, v_ref, g_ref, outs, off, extra=None):
    in_first, in_last = document_masks(docs_ref[...])
    for t, out in enumerate(outs):
        for i in range(part):
            at = columns((c ^ t) * part + i)
            forward = transposed_dot(jnp.where(in_last, k_ref[:, at], 0), v_ref[:, at]) * factor
            backward = transposed_dot(jnp.where(in_first, q_ref[:, at], 0), g_ref[:, at]) * factor
            if extra is not None:
                add_f, add_b = extra((c ^ t) * part + i)
                forward, backward = forward + add_f, backward + add_b
            out[0, off + i] = forward.astype(BF16)
            out[1, off + i] = backward.astype(BF16)


def group_columns(group, unit):
    return pl.ds(group * unit * DH, unit * DH)


def rest_terms(factor, unit, part, places, shift, total, ids, docs_ref, q_hbm, k_hbm, v_hbm, g_hbm, *refs):
    outs, (q_ref, k_ref, v_ref, g_ref, sems) = refs[:-5], refs[-5:]
    waiting = []
    for s, g in enumerate(places):
        forward, backward = group_columns(g, unit), group_columns((g + shift) % total, unit)
        waiting.append(fetch(
            [
                (k_hbm.at[:, forward], k_ref.at[s]), (v_hbm.at[:, forward], v_ref.at[s]),
                (q_hbm.at[:, backward], q_ref.at[s]), (g_hbm.at[:, backward], g_ref.at[s]),
            ],
            sems.at[s],
        ))
    for s in range(len(places)):
        for copy in waiting[s]:
            copy.wait()
        add_terms(
            factor, part, docs_ref, ids[1], q_ref.at[s], k_ref.at[s], v_ref.at[s], g_ref.at[s], outs, s * part
        )


def lead_terms(
    factor, unit, part, shift, outer, inner, ids, docs_ref, labels, q_hbm, k_hbm, v_hbm, g_hbm, carry_hbm, cot_hbm, *refs,
):
    outs, sents, (q_ref, k_ref, v_ref, g_ref, carry_ref, cot_ref, sems) = refs[:inner], refs[inner : 2 * inner], refs[2 * inner :]
    o, c, z = ids[0], ids[1], ids[2]
    held = carry_hbm.shape[0]
    forward, backward = group_columns(0, unit), group_columns(shift, unit)
    copies = fetch(
        [
            (k_hbm.at[:, forward], k_ref), (v_hbm.at[:, forward], v_ref),
            (q_hbm.at[:, backward], q_ref), (g_hbm.at[:, backward], g_ref),
            (carry_hbm.at[pl.ds(0, unit)], carry_ref), (cot_hbm.at[pl.ds(held - unit, unit)], cot_ref),
        ],
        sems,
    )
    for copy in copies:
        copy.wait()
    first, last = own_row(labels, z), own_row(labels, DEPTH + z)
    opens = jnp.logical_and(jnp.logical_and(o == 0, c == 0), z == 0)
    closes = jnp.logical_and(jnp.logical_and(o == outer - 1, c == inner - 1), z == DEPTH - 1)
    open_f = flag(jnp.logical_and(opens, last == 0.0))
    close_b = flag(jnp.logical_and(closes, first == last)) * factor

    def extra(place):
        return open_f * carry_ref[place], close_b * cot_ref[place]

    add_terms(factor, part, docs_ref, c, q_ref, k_ref, v_ref, g_ref, outs, 0, extra)
    _, side, at_end = place_of(ids)

    @pl.when(at_end)
    def _():
        for term, out in zip(outs, sents):
            hop(side, edge_rows(z, labels, None), True, 0, part, term, None, None, 0, out, 0)


def block_rows(labels, z, grouped):
    if grouped:
        return [l[0:1, :] for l in labels], [l[2 * DEPTH - 1 : 2 * DEPTH, :] for l in labels]
    return [own_row(l, z) for l in labels], [own_row(l, DEPTH + z) for l in labels]


def sum_kernel(inner, levels, grouped, ids, *refs):
    labels, terms, outs = refs[:inner], refs[inner : 2 * inner], refs[2 * inner :]
    o, z = ids[0], ids[2]
    count = terms[0].shape[1]
    newest = functools.reduce(jnp.maximum, [l[2 * DEPTH - 1 : 2 * DEPTH, :] for l in labels])
    oldest = functools.reduce(jnp.minimum, [l[0:1, :] for l in labels])
    firsts, lasts = block_rows(labels, z, grouped)
    keep_f = [flag(l == newest) for l in lasts]
    keep_b = [flag(l == oldest) for l in firsts]
    low = [((o >> level) & 1) == 0 for level in range(levels)]
    for i in range(count):
        sum_f = sum(m * r[0, i].astype(F32) for m, r in zip(keep_f, terms)).astype(BF16)
        sum_b = sum(m * r[1, i].astype(F32) for m, r in zip(keep_b, terms)).astype(BF16)
        for chosen, out in zip(low, outs):
            out[i * DH : (i + 1) * DH, :] = jnp.where(chosen, sum_f, sum_b)
    rows = lax.broadcasted_iota(jnp.int32, (LABELS, DH), 0)
    marks = jnp.where(rows < LABELS // 2, jnp.broadcast_to(newest, (LABELS, DH)), jnp.broadcast_to(oldest, (LABELS, DH)))
    for out in outs:
        out[count * DH :, :] = marks.astype(BF16)


def prefix_kernel(factor, unit, part, places, shift, total, inner, outer, grouped, ids, carry_ref, cot_ref, *refs):
    labels, terms, fans = refs[:inner], refs[inner : 2 * inner], refs[2 * inner : 2 * inner + outer - 1]
    outs, edge_ref = refs[2 * inner + outer - 1 : -1], refs[-1]
    o, c, z = ids[0], ids[1], ids[2]
    held = carry_ref.shape[0]
    count = terms[0].shape[1]
    group_first, group_last = block_rows(labels, z, True)
    block_first, block_last = block_rows(labels, z, grouped)
    marks = [r[count * DH : count * DH + LABELS, :].astype(F32) for r in fans]
    outer_last = [m[0:1] for m in marks]
    outer_first = [m[LABELS // 2 : LABELS // 2 + 1] for m in marks]
    newest = functools.reduce(jnp.maximum, group_last + outer_last)
    prior_base, later_base = jnp.zeros_like(newest), newest
    earlier = [(o ^ (d + 1)) < o for d in range(outer - 1)]
    for d in range(outer - 1):
        prior_base = jnp.maximum(prior_base, jnp.where(earlier[d], outer_last[d], 0.0))
        later_base = jnp.minimum(later_base, jnp.where(earlier[d], newest, outer_first[d]))
    priors, laters, plans = [], [], []
    for t in range(inner):
        prior, later = prior_base, later_base
        for d in range(inner):
            if d != t:
                before = (c ^ d) < (c ^ t)
                prior = jnp.maximum(prior, jnp.where(before, group_last[d], 0.0))
                later = jnp.minimum(later, jnp.where(before, newest, group_first[d]))
        forward = [(flag(jnp.logical_and(earlier[d], outer_last[d] == prior)), fans[d], None) for d in range(outer - 1)]
        backward = [
            (flag(jnp.logical_and(jnp.logical_not(earlier[d]), outer_first[d] == later)), fans[d], None)
            for d in range(outer - 1)
        ]
        for d in range(inner):
            if d != t:
                before = (c ^ d) < (c ^ t)
                forward.append((flag(jnp.logical_and(before, block_last[d] == prior)), terms[d], 0))
                backward.append((flag(jnp.logical_and(jnp.logical_not(before), block_first[d] == later)), terms[d], 1))
        take_f, take_b = prior == 0.0, later == newest
        if grouped:
            take_f = jnp.logical_and(take_f, jnp.logical_and(o == 0, (c ^ t) == 0))
            take_b = jnp.logical_and(take_b, jnp.logical_and(o == outer - 1, (c ^ t) == inner - 1))
        priors.append(prior)
        laters.append(later)
        plans.append((forward, backward, flag(take_f), flag(take_b) * factor))
    for s, g in enumerate(places):
        for i in range(part):
            at = s * part + i

            def carried(head, ref):
                place = head - z * held
                mine = jnp.logical_and(place >= 0, place < held)
                return jnp.where(mine, ref[jnp.clip(place, 0, held - 1)], 0.0)

            carries = (
                carried(g * unit + c * part + i, carry_ref),
                carried((g + shift) % total * unit + c * part + i, cot_ref),
            )

            def value(ref, side):
                return (ref[at * DH : (at + 1) * DH, :] if side is None else ref[side, at]).astype(F32)

            for t, out in enumerate(outs):
                for side in range(2):
                    amount = plans[t][2 + side] * carries[side]
                    for weight, ref, which in plans[t][side]:
                        amount = amount + weight * value(ref, which)
                    out[side, at] = amount.astype(BF16)
    edge_ref[0:1, :] = priors[0]
    edge_ref[1:2, :] = laters[0]
    edge_ref[2:8, :] = jnp.broadcast_to(newest, (6, DH))


def place_of(ids):
    z = ids[2]
    side = jnp.where(z >= DEPTH // 2, 1, 0)
    return z, side, jnp.logical_or(z == 0, z == DEPTH - 1)


def edge_rows(z, labels, edges):
    first, last = own_row(labels, z), own_row(labels, DEPTH + z)
    last_before = own_row(labels, DEPTH + jnp.maximum(z - 1, 0))
    first_after = own_row(labels, jnp.minimum(z + 1, DEPTH - 1))
    final_f, final_b = labels[2 * DEPTH - 1 : 2 * DEPTH, :], labels[0:1, :]
    prior = later = final_f
    if edges is not None:
        prior, later = edges[0:1, :], edges[1:2, :]
    return (last, last_before, final_f, first, prior), (first, first_after, final_b, last, later)


def pick(which, rows):
    return [jnp.where(which == 0, a, b) for a, b in zip(*rows)]


def hop(side, rows, lead, off, part, term_ref, prefix_ref, got_ref, got_off, out, out_off):
    own, neighbour, _, _, prior = pick(side, rows)
    other, _, final, _, _ = pick(1 - side, rows)
    join, keep, counts = flag(prior == own), flag(neighbour == own), flag(other == final)
    for i in range(part):
        state = term_ref[side, off + i].astype(F32)
        if lead:
            rest = counts * term_ref[1 - side, off + i].astype(F32)
        else:
            state = state + join * prefix_ref[side, off + i].astype(F32)
            rest = prefix_ref[1 - side, off + i].astype(F32)
        if got_ref is not None:
            state = state + keep * got_ref[0, got_off + i].astype(F32)
            rest = rest + got_ref[1, got_off + i].astype(F32)
        out[0, out_off + i] = state.astype(BF16)
        out[1, out_off + i] = rest.astype(BF16)


def hop_kernel(part, near, far, across, has_edges, ids, labels, *refs):
    z, side, at_end = place_of(ids)
    out, refs = refs[-1], list(refs[:-1])
    rows = edge_rows(z, labels, refs.pop(0) if has_edges else None)

    def take(plans):
        return [(plan, refs.pop(0), None if plan[0] else refs.pop(0), refs.pop(0) if plan[2] is not None else None) for plan in plans]

    near, far = take(near), take(far)

    def write(side, entries):
        for n, ((lead, off, got_off), term, prefix, got) in enumerate(entries):
            hop(side, rows, lead, off, part, term, prefix, got, got_off, out, n * part)

    if near:
        pl.when(at_end)(lambda: write(side, near))
    if far:
        pl.when(jnp.logical_not(at_end))(lambda: write(side if across else 1 - side, far))


def lead_total_kernel(part, turns, ids, labels, *refs):
    z, side, at_end = place_of(ids)
    rows = edge_rows(z, labels, None)
    for t in range(turns):
        term, near, middle, far = refs[4 * t : 4 * t + 4]
        out = refs[4 * turns + t]

        def total(which, over, rest):
            own, neighbour, final, _, _ = pick(which, rows)
            counts, come = flag(own == final), flag(neighbour == final)
            for i in range(part):
                value = counts * term[which, i].astype(F32)
                if over is not None:
                    value = value + come * over[0, i].astype(F32)
                if rest is not None:
                    value = value + rest[1, i].astype(F32)
                out[which, i] = value.astype(BF16)

        @pl.when(at_end)
        def _():
            total(side, None, far)
            total(1 - side, far, None)

        @pl.when(jnp.logical_not(at_end))
        def _():
            total(side, near, middle)
            total(1 - side, middle, near)


def local_kernel(factor, base, count, docs_ref, row_ref, q_ref, k_ref, v_ref, g_ref, out):
    docs = docs_ref[...]
    places = lax.broadcasted_iota(jnp.int32, (SPAN, SPAN), 0)
    others = lax.broadcasted_iota(jnp.int32, (SPAN, SPAN), 1)
    allowed = jnp.logical_and(others <= places, docs == row_ref[0:1])
    for i in range(count):
        at = slice((base + i) * DH, (base + i + 1) * DH)
        q, k, v, g = q_ref[:, at], k_ref[:, at], v_ref[:, at], g_ref[:, at]
        scores = jnp.where(allowed, dot_transposed(q, k) * factor, 0.0).astype(BF16)
        grad_scores = jnp.where(allowed, dot_transposed(g, v) * factor, 0.0).astype(BF16)
        out[0, i] = dot(scores, v)
        out[1, i] = dot(grad_scores, k)
        out[2, i] = transposed_dot(grad_scores, q)
        out[3, i] = transposed_dot(scores, g)


def output_kernel(unit, part, plans, ids, labels, edges, docs_ref, q_ref, k_ref, v_ref, g_ref, *refs):
    count = len(plans)
    sources, locals_ = refs[: 8 * count], refs[8 * count : 9 * count]
    outs, (states, held, sems) = refs[-7:-3], refs[-3:]
    c = ids[1]
    z, side, at_end = place_of(ids)
    rows = edge_rows(z, labels, edges)

    def make_states(ends, side):
        for n, (_, _, both) in enumerate(plans):
            for which in range(2):
                lead, off, near_off, middle_off, far_off = both[which]
                prefix, near, middle, far = sources[8 * n + 4 * which : 8 * n + 4 * which + 4]
                _, neighbour, _, target, prior = rows[which]
                reach, come = flag(prior == target), flag(neighbour == target)
                if ends:
                    over, rest = (None, (far, far_off)) if side == which else ((far, far_off), None)
                elif side == which:
                    over, rest = (near, near_off), (middle, middle_off)
                else:
                    over, rest = (middle, middle_off), (near, near_off)
                for i in range(part):
                    value = reach * prefix[which, off + i].astype(F32)
                    if over is not None:
                        value = value + come * over[0][0, over[1] + i].astype(F32)
                    if rest is not None and not lead:
                        value = value + reach * rest[0][1, rest[1] + i].astype(F32)
                    states[n, which, i] = value.astype(BF16)

    for ends in (True, False):
        for which in range(2):
            here = jnp.logical_and(at_end if ends else jnp.logical_not(at_end), side == which)
            pl.when(here)(functools.partial(make_states, ends, which))

    in_first, in_last = document_masks(docs_ref[...])
    copies = []
    for n, (group, turn, _) in enumerate(plans):
        place = (c ^ turn) * part
        for i in range(part):
            at = columns(group * unit + place + i)
            before, after = states[n, 0, i], states[n, 1, i]
            results = (
                dot(jnp.where(in_first, q_ref[:, at], 0), before),
                dot_transposed(jnp.where(in_first, g_ref[:, at], 0), before),
                dot_transposed(jnp.where(in_last, v_ref[:, at], 0), after),
                dot(jnp.where(in_last, k_ref[:, at], 0), after),
            )
            for m, result in enumerate(results):
                held[n, m, i] = (locals_[n][m, place + i] + result).astype(BF16)
                copy = pltpu.make_async_copy(held.at[n, m, i], outs[m].at[:, at], sems.at[n, m, i])
                copy.start()
                copies.append(copy)
    for copy in copies:
        copy.wait()


def shards(queries, keys, values, out_grad, doc_ids, carry_in, carry_cot):
    outer, inner, depth = (lax.axis_size(a) for a in ("outer", "inner", "heads"))
    assert depth == DEPTH
    tokens_all = doc_ids.shape[0] * outer * inner
    factor = float(DH * (tokens_all // 2)) ** (-0.5)
    head_count = queries.shape[1] // DH
    held = carry_in.shape[0]
    part = min(4, head_count // inner)
    unit = part * inner
    groups = head_count // unit
    leads = held % unit == 0
    shift = groups - 1 if leads else 0

    ids = jnp.stack([lax.axis_index(a) for a in ("outer", "inner", "heads")]).astype(jnp.int32)
    token, (own_labels, docs_column, docs_row) = call(
        jnp.zeros((8, DH), F32),
        label_kernel,
        (ids, doc_ids.reshape(depth, SPAN)),
        [
            jax.ShapeDtypeStruct((2 * depth, DH), F32),
            jax.ShapeDtypeStruct((SPAN, SPAN), F32),
            jax.ShapeDtypeStruct((8, SPAN), F32),
        ],
    )
    labels = [own_labels] + [pairs(own_labels, "inner", d) for d in range(1, inner)]

    levels = (outer - 1).bit_length()

    def state_pair(count):
        return jax.ShapeDtypeStruct((2, count, DH, DH), BF16)

    terms, prefixes, near, middle, far, local = {}, {}, {}, {}, {}, {}
    edge, arrays, carries = None, (queries, keys, values, out_grad), (carry_in, carry_cot)
    far_arrays, far_carries = (
        tuple(pltpu.with_memory_space_constraint(a, pltpu.HBM) for a in group) for group in (arrays, carries)
    )

    def exchange(own):
        return [own[0]] + [pairs(own[d], "inner", d) for d in range(1, inner)]

    def receive(units, kind, sent, perm):
        got = lax.ppermute(sent, "heads", perm)
        for n, u in enumerate(units):
            kind[u] = (got, n * part)
        return got

    def make_lead_terms():
        nonlocal token
        block = pltpu.VMEM((SPAN, unit * DH), BF16)
        carry = pltpu.VMEM((unit, DH, DH), F32)
        token, own = call(
            token,
            functools.partial(lead_terms, factor, unit, part, shift, outer, inner),
            (ids, docs_column, own_labels) + far_arrays + far_carries,
            [state_pair(part)] * (2 * inner),
            scratch=[block] * 4 + [carry] * 2 + [pltpu.SemaphoreType.DMA((6,))],
            specs=[SMEM, VMEM, VMEM] + [HBM] * 6,
        )
        terms[0] = [(a, 0) for a in own[:inner]]
        for t in range(inner):
            receive([(0, t)], near, own[inner + t], [(0, 1), (3, 2)])

    def make_terms(places):
        nonlocal token
        token, own = call(
            token,
            functools.partial(rest_terms, factor, unit, part, places, shift, groups),
            (ids, docs_column) + far_arrays,
            [state_pair(part * len(places))] * inner,
            scratch=[pltpu.VMEM((len(places), SPAN, unit * DH), BF16)] * 4
            + [pltpu.SemaphoreType.DMA((len(places), 4))],
            specs=[SMEM, VMEM] + [HBM] * 4,
        )
        for s, g in enumerate(places):
            terms[g] = [(a, s * part) for a in own]
        return exchange(own)

    def make_sums(received, grouped):
        nonlocal token
        count = received[0].shape[1]
        token, sums = call(
            token,
            functools.partial(sum_kernel, inner, levels, grouped),
            (ids, *labels, *received),
            [jax.ShapeDtypeStruct((count * DH + LABELS, DH), BF16)] * levels,
        )
        return [pairs(sums[d.bit_length() - 1], "outer", d) for d in range(1, outer)]

    def make_prefixes(places, received, fans, grouped):
        nonlocal token, edge
        count = received[0].shape[1]
        token, given = call(
            token,
            functools.partial(
                prefix_kernel, factor, unit, part, places, shift, groups, inner, outer, grouped
            ),
            (ids, *carries, *labels, *received, *fans),
            [state_pair(count)] * inner + [jax.ShapeDtypeStruct((8, DH), F32)],
        )
        edge = given[-1] if edge is None else edge
        given = exchange(given[:-1])
        for s, g in enumerate(places):
            prefixes[g] = [(a, s * part) for a in given]

    def move(near_units, far_units, across, perm):
        nonlocal token
        units = list(near_units) + list(far_units)
        use_edges = not all(leads and g == 0 for g, _ in units)
        operands = [ids, own_labels] + ([edge] if use_edges else [])

        def plans_of(chosen, got):
            plans = []
            for u in chosen:
                g, t = u
                lead = leads and g == 0
                array, off = terms[g][t]
                operands.append(array)
                if not lead:
                    operands.append(prefixes[g][t][0])
                if got is not None:
                    operands.append(got[u][0])
                plans.append((lead, off, None if got is None else got[u][1]))
            return plans

        near_plans = plans_of(near_units, None)
        far_plans = plans_of(far_units, near if across else middle)
        token, sent = call(
            token,
            functools.partial(hop_kernel, part, near_plans, far_plans, across, use_edges),
            operands,
            [state_pair(part * max(len(near_units), len(far_units)))],
        )
        return sent[0]

    def ends(near_units, far_units):
        perm = ([(0, 1), (3, 2)] if near_units else []) + ([(1, 0), (2, 3)] if far_units else [])
        got = receive(near_units, near, move(near_units, far_units, False, perm), perm)
        for n, u in enumerate(far_units):
            far[u] = (got, n * part)

    def across(units):
        receive(units, middle, move([], units, True, None), [(1, 2), (2, 1)])

    def make_local(g):
        nonlocal token
        token, out = call(
            token,
            functools.partial(local_kernel, factor, g * unit, unit),
            (docs_column, docs_row) + arrays,
            [jax.ShapeDtypeStruct((4, unit, SPAN, DH), F32)],
            specs=[VMEM] * 6,
        )
        local[g] = out[0]

    out_shape = jax.ShapeDtypeStruct(queries.shape, BF16)
    results = ()

    def make_outputs(units):
        nonlocal token, results
        operands, plans = (ids, own_labels, edge, docs_column) + arrays, []
        for g, t in units:
            both = []
            for u in ((g, t), ((g - shift) % groups, t)):
                lead = leads and u[0] == 0
                array, off = prefixes[u[0]][t]
                both.append((lead, off, near[u][1], middle[u][1], far[u][1]))
                operands += (array, near[u][0], middle[u][0], far[u][0])
            plans.append((g, t, both))
        operands += tuple(local[g] for g, _ in units)
        count = len(units)
        token, results = call(
            token,
            functools.partial(output_kernel, unit, part, plans),
            operands + tuple(results),
            [out_shape] * 4,
            scratch=[
                pltpu.VMEM((count, 2, part, DH, DH), BF16),
                pltpu.VMEM((count, 4, part, SPAN, DH), BF16),
                pltpu.SemaphoreType.DMA((count, 4, part)),
            ],
            aliases={len(operands) + i: i for i in range(len(results))},
            specs=[SMEM] + [VMEM] * (len(operands) - 1) + [HBM] * len(results),
            out_specs=[HBM] * 4,
        )

    if leads and groups == 4 and inner == 2:
        make_lead_terms()
        rest = tuple(range(1, groups))
        got_rest = make_terms(rest)
        across([(0, 0)])
        fans_rest = make_sums(got_rest, False)
        across([(0, 1)])
        make_local(0)
        ends([], [(0, 0)])
        make_local(1)
        ends([], [(0, 1)])
        make_prefixes(rest, got_rest, fans_rest, False)
        ends([(1, 0), (2, 0)], [])
        token, totals = call(
            token,
            functools.partial(lead_total_kernel, part, inner),
            [ids, own_labels]
            + [a for t in range(inner) for a in (terms[0][t][0], near[0, t][0], middle[0, t][0], far[0, t][0])],
            [state_pair(part)] * inner,
        )
        got_lead = exchange(totals)
        ends([(3, 0), (1, 1)], [])
        fans_lead = make_sums(got_lead, True)
        across([(1, 0), (2, 0)])
        make_local(2)
        ends([(2, 1)], [(1, 0)])
        across([(3, 0), (1, 1)])
        make_prefixes((0,), got_lead, fans_lead, True)
        ends([(3, 1)], [(2, 0)])
        across([(2, 1)])
        make_local(3)
        ends([], [(3, 0), (1, 1)])
        across([(3, 1)])
        make_outputs([(1, 0), (0, 0)])
        ends([], [(2, 1)])
        make_outputs([(2, 0), (3, 0), (0, 1)])
        ends([], [(3, 1)])
        make_outputs([(1, 1)])
        make_outputs([(2, 1), (3, 1)])
    else:
        assert not leads
        places = tuple(range(groups))
        got = make_terms(places)
        make_prefixes(places, got, make_sums(got, False), False)
        units = [(g, t) for g in range(groups) for t in range(inner)]
        lag = 4
        for k in range(len(units) + lag):
            ends(units[k : k + 1], units[k - lag : k - lag + 1] if k >= lag else [])
            if k < len(units):
                across([units[k]])
        for g in range(groups):
            make_local(g)
        for u in units:
            make_outputs([u])
    return tuple(results)


def solution(mesh):
    tokens = P(("outer", "inner", "heads"), None)
    carry = P("heads", None, None)
    return jax.shard_map(
        shards,
        mesh=mesh,
        in_specs=(tokens,) * 4 + (P(("outer", "inner")), carry, carry),
        out_specs=(tokens,) * 4,
        check_vma=False,
    )
```

```python
import functools

import jax
import jax.numpy as jnp
from jax import lax
from jax.experimental import pallas as pl
from jax.experimental.pallas import tpu as pltpu
from jax.sharding import PartitionSpec as P

DH = 128
SPAN = 128
LABELS = 16
DEPTH = 4
F32 = jnp.float32
BF16 = jnp.bfloat16
VMEM = pl.BlockSpec(memory_space=pltpu.VMEM)
SMEM = pl.BlockSpec(memory_space=pltpu.SMEM)
HBM = pl.BlockSpec(memory_space=pltpu.HBM)
LIMIT = 24 * 1024 * 1024
COSTS = ()


def pairs(array, axis, distance):
    count = lax.axis_size(axis)
    return lax.ppermute(array, axis, [(i, i ^ distance) for i in range(count)])


def transposed_dot(a, b):
    return lax.dot_general(a, b, (((0,), (0,)), ((), ())), preferred_element_type=F32)


def dot_transposed(a, b):
    return lax.dot_general(a, b, (((1,), (1,)), ((), ())), preferred_element_type=F32)


def dot(a, b):
    return lax.dot_general(a, b, (((1,), (0,)), ((), ())), preferred_element_type=F32)


def flag(row):
    return jnp.where(row, 1.0, 0.0).astype(F32)


def call(token, kernel, operands, out_shape, cost=0, scratch=(), aliases=None, specs=None, out_specs=None, after=()):
    count, results, behind = len(operands), len(out_shape), len(operands) + len(after)

    def ordered(*refs):
        kernel(*refs[:count], *refs[behind + 1 : behind + 1 + results], *refs[behind + 2 + results :])

    *outs, token = pl.pallas_call(
        ordered,
        in_specs=list(specs or [SMEM] + [VMEM] * (count - 1)) + [VMEM] * (len(after) + 1),
        out_specs=list(out_specs or [VMEM] * results) + [VMEM],
        out_shape=list(out_shape) + [jax.ShapeDtypeStruct(token.shape, token.dtype)],
        scratch_shapes=list(scratch),
        input_output_aliases={**(aliases or {}), behind: results},
        compiler_params=pltpu.CompilerParams(vmem_limit_bytes=LIMIT),
        cost_estimate=pl.CostEstimate(flops=int(cost * 1e9), bytes_accessed=0, transcendentals=0),
    )(*operands, *after, token)
    return token, outs


def document_masks(docs):
    return docs == docs[0:1], docs == docs[SPAN - 1 : SPAN]


def columns(head):
    return pl.ds(pl.multiple_of(head * DH, DH), DH)


def own_row(ref, at):
    return ref[pl.ds(at, 1), :]


def label_kernel(ids, docs_ref, labels_ref, column_ref, row_ref):
    docs = docs_ref[...]
    for k in range(DEPTH):
        row = docs[k : k + 1, :].astype(F32)
        labels_ref[k : k + 1, :] = jnp.broadcast_to(row[:, 0:1], (1, DH))
        labels_ref[DEPTH + k : DEPTH + k + 1, :] = jnp.broadcast_to(row[:, SPAN - 1 :], (1, DH))
    own = own_row(docs_ref, ids[2]).astype(F32)
    column_ref[...] = jnp.broadcast_to(own, (SPAN, SPAN)).T
    row_ref[...] = jnp.broadcast_to(own, (8, SPAN))


def fetch(pairs_of_refs, sems):
    copies = [pltpu.make_async_copy(source, target, sems.at[n]) for n, (source, target) in enumerate(pairs_of_refs)]
    for copy in copies:
        copy.start()
    return copies


def add_terms(factor, part, docs_ref, c, q_ref, k_ref, v_ref, g_ref, outs, off, extra=None):
    in_first, in_last = document_masks(docs_ref[...])
    for t, out in enumerate(outs):
        for i in range(part):
            at = columns((c ^ t) * part + i)
            forward = transposed_dot(jnp.where(in_last, k_ref[:, at], 0), v_ref[:, at]) * factor
            backward = transposed_dot(jnp.where(in_first, q_ref[:, at], 0), g_ref[:, at]) * factor
            if extra is not None:
                add_f, add_b = extra((c ^ t) * part + i)
                forward, backward = forward + add_f, backward + add_b
            out[0, off + i] = forward.astype(BF16)
            out[1, off + i] = backward.astype(BF16)


def group_columns(group, unit):
    return pl.ds(group * unit * DH, unit * DH)


def rest_terms(factor, unit, part, places, mates, ids, docs_ref, q_hbm, k_hbm, v_hbm, g_hbm, *refs):
    outs, (q_ref, k_ref, v_ref, g_ref, sems) = refs[:-5], refs[-5:]
    waiting = []
    for s, (g, mate) in enumerate(zip(places, mates)):
        forward, backward = group_columns(g, unit), group_columns(mate, unit)
        waiting.append(fetch(
            [
                (k_hbm.at[:, forward], k_ref.at[s]), (v_hbm.at[:, forward], v_ref.at[s]),
                (q_hbm.at[:, backward], q_ref.at[s]), (g_hbm.at[:, backward], g_ref.at[s]),
            ],
            sems.at[s],
        ))
    for s in range(len(places)):
        for copy in waiting[s]:
            copy.wait()
        add_terms(
            factor, part, docs_ref, ids[1], q_ref.at[s], k_ref.at[s], v_ref.at[s], g_ref.at[s], outs, s * part
        )


def lead_terms(
    factor, unit, part, places, mates, outer, inner, ids, docs_ref, labels, q_hbm, k_hbm, v_hbm, g_hbm, carry_hbm, cot_hbm,
    *refs,
):
    outs, (sent, carried), (q_ref, k_ref, v_ref, g_ref, carry_ref, cot_ref, sems) = refs[:inner], refs[inner : inner + 2], refs[inner + 2 :]
    o, c, z = ids[0], ids[1], ids[2]
    waiting = [fetch([(carry_hbm, carry_ref), (cot_hbm, cot_ref)], sems.at[len(places)])]
    for s, (g, mate) in enumerate(zip(places, mates)):
        forward, backward = group_columns(g, unit), group_columns(mate, unit)
        waiting.append(fetch(
            [
                (k_hbm.at[:, forward], k_ref.at[s]), (v_hbm.at[:, forward], v_ref.at[s]),
                (q_hbm.at[:, backward], q_ref.at[s]), (g_hbm.at[:, backward], g_ref.at[s]),
            ],
            sems.at[s],
        ))
    for copy in waiting[0]:
        copy.wait()
    first, last = own_row(labels, z), own_row(labels, DEPTH + z)
    newest = labels[2 * DEPTH - 1 : 2 * DEPTH, :]
    opens, closes = jnp.logical_and(o == 0, c == 0), jnp.logical_and(o == outer - 1, c == inner - 1)
    for s in range(len(places)):
        for copy in waiting[1 + s]:
            copy.wait()
        open_f = flag(jnp.logical_and(jnp.logical_and(opens, z == s), last == 0.0))
        close_b = flag(jnp.logical_and(jnp.logical_and(closes, z == DEPTH - 1 - s), first == newest)) * factor

        def extra(place):
            return open_f * carry_ref[place], close_b * cot_ref[place]

        add_terms(
            factor, part, docs_ref, c, q_ref.at[s], k_ref.at[s], v_ref.at[s], g_ref.at[s], outs, s * part, extra
        )
    _, side, at_end = place_of(ids)

    @pl.when(at_end)
    def _():
        for t, term in enumerate(outs):
            hop(side, edge_rows(z, labels, None), True, 0, part, term, None, None, 0, sent, t * part)

    @pl.when(jnp.logical_not(at_end))
    def _():
        for i in range(unit):
            carried[i] = jnp.where(side == 0, carry_ref[i], cot_ref[i] * factor).astype(BF16)


def block_rows(labels, z, grouped):
    if grouped:
        return [l[0:1, :] for l in labels], [l[2 * DEPTH - 1 : 2 * DEPTH, :] for l in labels]
    return [own_row(l, z) for l in labels], [own_row(l, DEPTH + z) for l in labels]


def sum_kernel(inner, levels, grouped, ids, *refs):
    labels, terms, outs = refs[:inner], refs[inner : 2 * inner], refs[2 * inner :]
    o, z = ids[0], ids[2]
    count = terms[0].shape[1]
    newest = functools.reduce(jnp.maximum, [l[2 * DEPTH - 1 : 2 * DEPTH, :] for l in labels])
    oldest = functools.reduce(jnp.minimum, [l[0:1, :] for l in labels])
    firsts, lasts = block_rows(labels, z, grouped)
    keep_f = [flag(l == newest) for l in lasts]
    keep_b = [flag(l == oldest) for l in firsts]
    low = [((o >> level) & 1) == 0 for level in range(levels)]
    for i in range(count):
        sum_f = sum(m * r[0, i].astype(F32) for m, r in zip(keep_f, terms)).astype(BF16)
        sum_b = sum(m * r[1, i].astype(F32) for m, r in zip(keep_b, terms)).astype(BF16)
        for chosen, out in zip(low, outs):
            out[i * DH : (i + 1) * DH, :] = jnp.where(chosen, sum_f, sum_b)
    rows = lax.broadcasted_iota(jnp.int32, (LABELS, DH), 0)
    marks = jnp.where(rows < LABELS // 2, jnp.broadcast_to(newest, (LABELS, DH)), jnp.broadcast_to(oldest, (LABELS, DH)))
    for out in outs:
        out[count * DH :, :] = marks.astype(BF16)


def prefix_kernel(factor, unit, part, places, mates, inner, outer, grouped, lacking, ids, carry_ref, cot_ref, *refs):
    lacked, refs = (refs[0], refs[1:]) if lacking else (None, refs)
    labels, terms, fans = refs[:inner], refs[inner : 2 * inner], refs[2 * inner : 2 * inner + outer - 1]
    outs, edge_ref = refs[2 * inner + outer - 1 : -1], refs[-1]
    o, c, z = ids[0], ids[1], ids[2]
    held = carry_ref.shape[0]
    count = terms[0].shape[1]
    group_first, group_last = block_rows(labels, z, True)
    block_first, block_last = block_rows(labels, z, grouped)
    marks = [r[count * DH : count * DH + LABELS, :].astype(F32) for r in fans]
    outer_last = [m[0:1] for m in marks]
    outer_first = [m[LABELS // 2 : LABELS // 2 + 1] for m in marks]
    newest = functools.reduce(jnp.maximum, group_last + outer_last)
    prior_base, later_base = jnp.zeros_like(newest), newest
    earlier = [(o ^ (d + 1)) < o for d in range(outer - 1)]
    for d in range(outer - 1):
        prior_base = jnp.maximum(prior_base, jnp.where(earlier[d], outer_last[d], 0.0))
        later_base = jnp.minimum(later_base, jnp.where(earlier[d], newest, outer_first[d]))
    priors, laters, plans = [], [], []
    for t in range(inner):
        prior, later = prior_base, later_base
        for d in range(inner):
            if d != t:
                before = (c ^ d) < (c ^ t)
                prior = jnp.maximum(prior, jnp.where(before, group_last[d], 0.0))
                later = jnp.minimum(later, jnp.where(before, newest, group_first[d]))
        forward = [(flag(jnp.logical_and(earlier[d], outer_last[d] == prior)), fans[d], None) for d in range(outer - 1)]
        backward = [
            (flag(jnp.logical_and(jnp.logical_not(earlier[d]), outer_first[d] == later)), fans[d], None)
            for d in range(outer - 1)
        ]
        for d in range(inner):
            if d != t:
                before = (c ^ d) < (c ^ t)
                forward.append((flag(jnp.logical_and(before, block_last[d] == prior)), terms[d], 0))
                backward.append((flag(jnp.logical_and(jnp.logical_not(before), block_first[d] == later)), terms[d], 1))
        take_f, take_b = prior == 0.0, later == newest
        if grouped:
            take_f = jnp.logical_and(take_f, jnp.logical_and(o == 0, (c ^ t) == 0))
            take_b = jnp.logical_and(take_b, jnp.logical_and(o == outer - 1, (c ^ t) == inner - 1))
        priors.append(prior)
        laters.append(later)
        plans.append((forward, backward, flag(take_f), flag(take_b)))
    for s, (g, mate) in enumerate(zip(places, mates)):
        for i in range(part):
            at = s * part + i

            def carried(head, ref):
                place = head - z * held
                mine = jnp.logical_and(place >= 0, place < held)
                return jnp.where(mine, ref[jnp.clip(place, 0, held - 1)], 0.0)

            carries = [
                carried(g * unit + c * part + i, carry_ref),
                carried(mate * unit + c * part + i, cot_ref) * factor,
            ]
            if lacking:
                more = lacked[c * part + i].astype(F32)
                carries[0] = carries[0] + jnp.where(z == 0, more, 0.0)
                carries[1] = carries[1] + jnp.where(z == DEPTH - 1, more, 0.0)

            def value(ref, side):
                return (ref[at * DH : (at + 1) * DH, :] if side is None else ref[side, at]).astype(F32)

            for t, out in enumerate(outs):
                for side in range(2):
                    amount = plans[t][2 + side] * carries[side]
                    for weight, ref, which in plans[t][side]:
                        amount = amount + weight * value(ref, which)
                    out[side, at] = amount.astype(BF16)
    edge_ref[0:1, :] = priors[0]
    edge_ref[1:2, :] = laters[0]
    edge_ref[2:8, :] = jnp.broadcast_to(newest, (6, DH))


def place_of(ids):
    z = ids[2]
    side = jnp.where(z >= DEPTH // 2, 1, 0)
    return z, side, jnp.logical_or(z == 0, z == DEPTH - 1)


def edge_rows(z, labels, edges):
    first, last = own_row(labels, z), own_row(labels, DEPTH + z)
    last_before = own_row(labels, DEPTH + jnp.maximum(z - 1, 0))
    first_after = own_row(labels, jnp.minimum(z + 1, DEPTH - 1))
    final_f, final_b = labels[2 * DEPTH - 1 : 2 * DEPTH, :], labels[0:1, :]
    prior = later = final_f
    if edges is not None:
        prior, later = edges[0:1, :], edges[1:2, :]
    return (last, last_before, final_f, first, prior), (first, first_after, final_b, last, later)


def pick(which, rows):
    return [jnp.where(which == 0, a, b) for a, b in zip(*rows)]


def hop(side, rows, lead, off, part, term_ref, prefix_ref, got_ref, got_off, out, out_off):
    own, neighbour, _, _, prior = pick(side, rows)
    other, _, final, _, _ = pick(1 - side, rows)
    join, keep, counts = flag(prior == own), flag(neighbour == own), flag(other == final)
    for i in range(part):
        state = term_ref[side, off + i].astype(F32)
        if lead:
            rest = counts * term_ref[1 - side, off + i].astype(F32)
        else:
            state = state + join * prefix_ref[side, off + i].astype(F32)
            rest = prefix_ref[1 - side, off + i].astype(F32)
        if got_ref is not None:
            state = state + keep * got_ref[0, got_off + i].astype(F32)
            rest = rest + got_ref[1, got_off + i].astype(F32)
        out[0, out_off + i] = state.astype(BF16)
        out[1, out_off + i] = rest.astype(BF16)


def hop_kernel(part, near, far, across, has_edges, ids, labels, *refs):
    z, side, at_end = place_of(ids)
    out, refs = refs[-1], list(refs[:-1])
    rows = edge_rows(z, labels, refs.pop(0) if has_edges else None)

    def take(plans):
        return [(plan, refs.pop(0), None if plan[0] else refs.pop(0), refs.pop(0) if plan[2] is not None else None) for plan in plans]

    near, far = take(near), take(far)

    def write(side, entries):
        for n, ((lead, off, got_off), term, prefix, got) in enumerate(entries):
            hop(side, rows, lead, off, part, term, prefix, got, got_off, out, n * part)

    if near:
        pl.when(at_end)(lambda: write(side, near))
    if far:
        pl.when(jnp.logical_not(at_end))(lambda: write(side if across else 1 - side, far))


def lead_total_kernel(part, plans, ids, labels, *refs):
    z, side, at_end = place_of(ids)
    rows = edge_rows(z, labels, None)
    for t, (off, near_off, middle_off, far_off) in enumerate(plans):
        term, near, middle, far = refs[4 * t : 4 * t + 4]
        out = refs[4 * len(plans) + t]

        def total(which, over, over_off, rest, rest_off):
            own, neighbour, final, _, _ = pick(which, rows)
            counts, come = flag(own == final), flag(neighbour == final)
            for i in range(part):
                value = counts * term[which, off + i].astype(F32)
                if over is not None:
                    value = value + come * over[0, over_off + i].astype(F32)
                if rest is not None:
                    value = value + rest[1, rest_off + i].astype(F32)
                out[which, i] = value.astype(BF16)

        @pl.when(at_end)
        def _():
            total(side, None, 0, far, far_off)
            total(1 - side, far, far_off, None, 0)

        @pl.when(jnp.logical_not(at_end))
        def _():
            total(side, near, near_off, middle, middle_off)
            total(1 - side, middle, middle_off, near, near_off)


def local_kernel(factor, base, count, docs_ref, row_ref, q_ref, k_ref, v_ref, g_ref, out):
    docs = docs_ref[...]
    places = lax.broadcasted_iota(jnp.int32, (SPAN, SPAN), 0)
    others = lax.broadcasted_iota(jnp.int32, (SPAN, SPAN), 1)
    allowed = jnp.logical_and(others <= places, docs == row_ref[0:1])
    for i in range(count):
        at = slice((base + i) * DH, (base + i + 1) * DH)
        q, k, v, g = q_ref[:, at], k_ref[:, at], v_ref[:, at], g_ref[:, at]
        scores = jnp.where(allowed, dot_transposed(q, k) * factor, 0.0).astype(BF16)
        grad_scores = jnp.where(allowed, dot_transposed(g, v) * factor, 0.0).astype(BF16)
        out[0, i] = dot(scores, v)
        out[1, i] = dot(grad_scores, k)
        out[2, i] = transposed_dot(grad_scores, q)
        out[3, i] = transposed_dot(scores, g)


def output_kernel(unit, part, plans, ids, labels, edges, docs_ref, q_ref, k_ref, v_ref, g_ref, *refs):
    count = len(plans)
    sources, locals_ = refs[: 4 * count], refs[4 * count : 5 * count]
    outs, (states, held, sems) = refs[-7:-3], refs[-3:]
    c = ids[1]
    z, side, at_end = place_of(ids)
    rows = edge_rows(z, labels, edges)

    def make_states(ends, side):
        for n, (which, _, _, lead, off, near_off, middle_off, far_off) in enumerate(plans):
            prefix, near, middle, far = sources[4 * n : 4 * n + 4]
            _, neighbour, _, target, prior = rows[which]
            reach, come = flag(prior == target), flag(neighbour == target)
            if ends:
                over, rest = (None, (far, far_off)) if side == which else ((far, far_off), None)
            elif side == which:
                over, rest = (near, near_off), (middle, middle_off)
            else:
                over, rest = (middle, middle_off), (near, near_off)
            for i in range(part):
                value = reach * prefix[which, off + i].astype(F32)
                if over is not None:
                    value = value + come * over[0][0, over[1] + i].astype(F32)
                if rest is not None and not lead:
                    value = value + reach * rest[0][1, rest[1] + i].astype(F32)
                states[n, i] = value.astype(BF16)

    for ends in (True, False):
        for which in range(2):
            here = jnp.logical_and(at_end if ends else jnp.logical_not(at_end), side == which)
            pl.when(here)(functools.partial(make_states, ends, which))

    in_first, in_last = document_masks(docs_ref[...])
    copies = []
    for n, (which, group, turn, *_) in enumerate(plans):
        place = (c ^ turn) * part
        for i in range(part):
            at = columns(group * unit + place + i)
            state = states[n, i]
            if which == 0:
                results = (
                    dot(jnp.where(in_first, q_ref[:, at], 0), state),
                    dot_transposed(jnp.where(in_first, g_ref[:, at], 0), state),
                )
            else:
                results = (
                    dot_transposed(jnp.where(in_last, v_ref[:, at], 0), state),
                    dot(jnp.where(in_last, k_ref[:, at], 0), state),
                )
            for m, result in enumerate(results):
                held[n, m, i] = (locals_[n][2 * which + m, place + i] + result).astype(BF16)
                copy = pltpu.make_async_copy(held.at[n, m, i], outs[2 * which + m].at[:, at], sems.at[n, m, i])
                copy.start()
                copies.append(copy)
    for copy in copies:
        copy.wait()


def shards(queries, keys, values, out_grad, doc_ids, carry_in, carry_cot):
    outer, inner, depth = (lax.axis_size(a) for a in ("outer", "inner", "heads"))
    assert depth == DEPTH
    tokens_all = doc_ids.shape[0] * outer * inner
    factor = float(DH * (tokens_all // 2)) ** (-0.5)
    head_count = queries.shape[1] // DH
    held = carry_in.shape[0]
    part = min(4, head_count // inner)
    unit = part * inner
    groups = head_count // unit
    leads = 2 if held == unit and groups == DEPTH and inner == 2 else 0
    costs = iter(COSTS if leads else ())

    def mate(g):
        return groups - 1 - g if leads else g

    ids = jnp.stack([lax.axis_index(a) for a in ("outer", "inner", "heads")]).astype(jnp.int32)
    token, (own_labels, docs_column, docs_row) = call(
        jnp.zeros((8, DH), F32),
        label_kernel,
        (ids, doc_ids.reshape(depth, SPAN)),
        [
            jax.ShapeDtypeStruct((2 * depth, DH), F32),
            jax.ShapeDtypeStruct((SPAN, SPAN), F32),
            jax.ShapeDtypeStruct((8, SPAN), F32),
        ],
    )
    labels = [own_labels] + [pairs(own_labels, "inner", d) for d in range(1, inner)]

    levels = (outer - 1).bit_length()

    def state_pair(count):
        return jax.ShapeDtypeStruct((2, count, DH, DH), BF16)

    terms, prefixes, near, middle, far, local = {}, {}, {}, {}, {}, {}
    edge, arrays, carries = None, (queries, keys, values, out_grad), (carry_in, carry_cot)
    far_arrays, far_carries = (
        tuple(pltpu.with_memory_space_constraint(a, pltpu.HBM) for a in group) for group in (arrays, carries)
    )

    def exchange(own):
        return [own[0]] + [pairs(own[d], "inner", d) for d in range(1, inner)]

    def receive(units, kind, sent, perm):
        got = lax.ppermute(sent, "heads", perm)
        for n, u in enumerate(units):
            kind[u] = (got, n * part)
        return got

    def run(*args, **options):
        nonlocal token
        token, outs = call(token, *args, cost=next(costs, 0), **options)
        return outs

    def make_lead_terms():
        places = tuple(range(leads))
        block = pltpu.VMEM((leads, SPAN, unit * DH), BF16)
        carry = pltpu.VMEM((unit, DH, DH), F32)
        own = run(
            functools.partial(
                lead_terms, factor, unit, part, places, tuple(mate(g) for g in places), outer, inner
            ),
            (ids, docs_column, own_labels) + far_arrays + far_carries,
            [state_pair(part * leads)] * inner + [state_pair(part * inner), jax.ShapeDtypeStruct((unit, DH, DH), BF16)],
            scratch=[block] * 4 + [carry] * 2 + [pltpu.SemaphoreType.DMA((leads + 1, 4))],
            specs=[SMEM, VMEM, VMEM] + [HBM] * 6,
        )
        for g in places:
            terms[g] = [(a, g * part) for a in own[:inner]]
        receive([(0, t) for t in range(inner)], near, own[inner], [(0, 1), (3, 2)])
        return lax.ppermute(own[inner + 1], "heads", [(1, 0), (2, 3)])

    def make_terms(places):
        own = run(
            functools.partial(rest_terms, factor, unit, part, places, tuple(mate(g) for g in places)),
            (ids, docs_column) + far_arrays,
            [state_pair(part * len(places))] * inner,
            scratch=[pltpu.VMEM((len(places), SPAN, unit * DH), BF16)] * 4
            + [pltpu.SemaphoreType.DMA((len(places), 4))],
            specs=[SMEM, VMEM] + [HBM] * 4,
        )
        for s, g in enumerate(places):
            terms[g] = [(a, s * part) for a in own]
        return exchange(own)

    def make_sums(received, grouped):
        nonlocal token
        count = received[0].shape[1]
        sums = run(
            functools.partial(sum_kernel, inner, levels, grouped),
            (ids, *labels, *received),
            [jax.ShapeDtypeStruct((count * DH + LABELS, DH), BF16)] * levels,
        )
        return [pairs(sums[d.bit_length() - 1], "outer", d) for d in range(1, outer)]

    def make_prefixes(places, received, fans, grouped, lacked=None):
        nonlocal edge
        count = received[0].shape[1]
        given = run(
            functools.partial(
                prefix_kernel, factor, unit, part, places, tuple(mate(g) for g in places), inner, outer, grouped,
                lacked is not None,
            ),
            (ids, *carries, *([] if lacked is None else [lacked]), *labels, *received, *fans),
            [state_pair(count)] * inner + [jax.ShapeDtypeStruct((8, DH), F32)],
        )
        edge = given[-1] if edge is None else edge
        given = exchange(given[:-1])
        for s, g in enumerate(places):
            prefixes[g] = [(a, s * part) for a in given]

    def move(near_units, far_units, across):
        units = list(near_units) + list(far_units)
        use_edges = not all(g < leads for g, _ in units)
        operands = [ids, own_labels] + ([edge] if use_edges else [])

        def plans_of(chosen, got):
            plans = []
            for u in chosen:
                g, t = u
                lead = g < leads
                array, off = terms[g][t]
                operands.append(array)
                if not lead:
                    operands.append(prefixes[g][t][0])
                if got is not None:
                    operands.append(got[u][0])
                plans.append((lead, off, None if got is None else got[u][1]))
            return plans

        near_plans = plans_of(near_units, None)
        far_plans = plans_of(far_units, near if across else middle)
        sent = run(
            functools.partial(hop_kernel, part, near_plans, far_plans, across, use_edges),
            operands,
            [state_pair(part * max(len(near_units), len(far_units)))],
        )
        return sent[0]

    def ends(near_units, far_units):
        perm = ([(0, 1), (3, 2)] if near_units else []) + ([(1, 0), (2, 3)] if far_units else [])
        got = receive(near_units, near, move(near_units, far_units, False), perm)
        for n, u in enumerate(far_units):
            far[u] = (got, n * part)

    def across(units):
        receive(units, middle, move([], units, True), [(1, 2), (2, 1)])

    def make_local(g, after=()):
        out = run(
            functools.partial(local_kernel, factor, g * unit, unit),
            (docs_column, docs_row) + arrays,
            [jax.ShapeDtypeStruct((4, unit, SPAN, DH), F32)],
            specs=[VMEM] * 6,
            after=after,
        )
        local[g] = out[0]

    out_shape = jax.ShapeDtypeStruct(queries.shape, BF16)
    results = ()

    def make_outputs(halves):
        nonlocal results
        operands, plans = (ids, own_labels, edge, docs_column) + arrays, []
        for which, g, t in halves:
            array, off = prefixes[g][t]
            kept = [kind[g, t] for kind in (near, middle, far)]
            heads = mate(g) if which else g
            plans.append((which, heads, t, g < leads, off) + tuple(at for _, at in kept))
            operands += (array,) + tuple(a for a, _ in kept)
        operands += tuple(local[mate(g) if which else g] for which, g, _ in halves)
        count = len(halves)
        results = run(
            functools.partial(output_kernel, unit, part, plans),
            operands + tuple(results),
            [out_shape] * 4,
            scratch=[
                pltpu.VMEM((count, part, DH, DH), BF16),
                pltpu.VMEM((count, 2, part, SPAN, DH), BF16),
                pltpu.SemaphoreType.DMA((count, 2, part)),
            ],
            aliases={len(operands) + i: i for i in range(len(results))},
            specs=[SMEM] + [VMEM] * (len(operands) - 1) + [HBM] * len(results),
            out_specs=[HBM] * 4,
        )

    def make_totals(g):
        operands, plans = [ids, own_labels], []
        for t in range(inner):
            array, off = terms[g][t]
            kept = [kind[g, t] for kind in (near, middle, far)]
            operands += [array] + [a for a, _ in kept]
            plans.append((off,) + tuple(at for _, at in kept))
        totals = run(
            functools.partial(lead_total_kernel, part, plans),
            operands,
            [state_pair(part)] * inner,
        )
        return exchange(totals)

    def chunk(g):
        return [(g, t) for t in range(inner)]

    def halves_of(g):
        return [(which, g, t) for which in range(2) for t in range(inner)]

    if leads:
        lacked = make_lead_terms()
        got_rest = make_terms((2, 3))
        fans_rest = make_sums(got_rest, False)
        ends(chunk(1), [])
        across(chunk(0))
        make_local(0)
        make_local(1)
        make_prefixes((2, 3), got_rest, fans_rest, False)
        across(chunk(1))
        ends(chunk(2), chunk(0))
        make_local(2)
        make_local(3, after=[lacked])
        ends(chunk(3), chunk(1))
        across(chunk(2))
        got_first = make_totals(0)
        fans_first = make_sums(got_first, True)
        across(chunk(3))
        ends([], chunk(2))
        got_second = make_totals(1)
        make_prefixes((0,), got_first, fans_first, True)
        fans_second = make_sums(got_second, True)
        ends([], chunk(3))
        make_outputs(halves_of(0))
        make_prefixes((1,), got_second, fans_second, True, lacked)
        make_outputs(halves_of(1))
        make_outputs(halves_of(2))
        make_outputs(halves_of(3))
    else:
        assert not leads
        places = tuple(range(groups))
        got = make_terms(places)
        make_prefixes(places, got, make_sums(got, False), False)
        units = [(g, t) for g in range(groups) for t in range(inner)]
        lag = 4
        for k in range(len(units) + lag):
            ends(units[k : k + 1], units[k - lag : k - lag + 1] if k >= lag else [])
            if k < len(units):
                across([units[k]])
        for g in range(groups):
            make_local(g)
        for g, t in units:
            make_outputs([(0, g, t), (1, g, t)])
    return tuple(results)


def solution(mesh):
    tokens = P(("outer", "inner", "heads"), None)
    carry = P("heads", None, None)
    return jax.shard_map(
        shards,
        mesh=mesh,
        in_specs=(tokens,) * 4 + (P(("outer", "inner")), carry, carry),
        out_specs=(tokens,) * 4,
        check_vma=False,
    )
```

```python
import functools

import jax
import jax.numpy as jnp
from jax import lax
from jax.experimental import pallas as pl
from jax.experimental.pallas import tpu as pltpu
from jax.sharding import PartitionSpec as P

DH = 128
SPAN = 128
LABELS = 16
DEPTH = 4
F32 = jnp.float32
BF16 = jnp.bfloat16
VMEM = pl.BlockSpec(memory_space=pltpu.VMEM)
SMEM = pl.BlockSpec(memory_space=pltpu.SMEM)
HBM = pl.BlockSpec(memory_space=pltpu.HBM)
LIMIT = 24 * 1024 * 1024
COSTS = (0, 0, 0, 0, 0, 0, 16, 0, 0, 0, 0, 0, 0, 0, 0, 0, 0, 8, 0, 0, 0, 0, 0, 0, 0, 0, 0, 0)
ORDER = (
    "K1 K0 L3 A0"
    " E1 O0 B0 L0"
    " O1 J2 L1 L2"
    " J3 T0 O2 S0"
    " O3 T1 F2 P0"
    " S1 F3 W0 W2"
    " P1 W1 W3"
)


def pairs(array, axis, distance):
    count = lax.axis_size(axis)
    return lax.ppermute(array, axis, [(i, i ^ distance) for i in range(count)])


def transposed_dot(a, b):
    return lax.dot_general(a, b, (((0,), (0,)), ((), ())), preferred_element_type=F32)


def dot_transposed(a, b):
    return lax.dot_general(a, b, (((1,), (1,)), ((), ())), preferred_element_type=F32)


def dot(a, b):
    return lax.dot_general(a, b, (((1,), (0,)), ((), ())), preferred_element_type=F32)


def flag(row):
    return jnp.where(row, 1.0, 0.0).astype(F32)


def call(token, kernel, operands, out_shape, cost=0, scratch=(), aliases=None, specs=None, out_specs=None):
    count, results = len(operands), len(out_shape)

    def ordered(*refs):
        kernel(*refs[:count], *refs[count + 1 : count + 1 + results], *refs[count + 2 + results :])

    *outs, token = pl.pallas_call(
        ordered,
        in_specs=list(specs or [SMEM] + [VMEM] * (count - 1)) + [VMEM],
        out_specs=list(out_specs or [VMEM] * results) + [VMEM],
        out_shape=list(out_shape) + [jax.ShapeDtypeStruct(token.shape, token.dtype)],
        scratch_shapes=list(scratch),
        input_output_aliases={**(aliases or {}), count: results},
        compiler_params=pltpu.CompilerParams(vmem_limit_bytes=LIMIT),
        cost_estimate=pl.CostEstimate(flops=int(cost * 1e9), bytes_accessed=0, transcendentals=0),
    )(*operands, token)
    return token, outs


def document_masks(docs):
    return docs == docs[0:1], docs == docs[SPAN - 1 : SPAN]


def columns(head):
    return pl.ds(pl.multiple_of(head * DH, DH), DH)


def own_row(ref, at):
    return ref[pl.ds(at, 1), :]


def label_kernel(ids, docs_ref, labels_ref, column_ref, row_ref):
    docs = docs_ref[...]
    for k in range(DEPTH):
        row = docs[k : k + 1, :].astype(F32)
        labels_ref[k : k + 1, :] = jnp.broadcast_to(row[:, 0:1], (1, DH))
        labels_ref[DEPTH + k : DEPTH + k + 1, :] = jnp.broadcast_to(row[:, SPAN - 1 :], (1, DH))
    own = own_row(docs_ref, ids[2]).astype(F32)
    column_ref[...] = jnp.broadcast_to(own, (SPAN, SPAN)).T
    row_ref[...] = jnp.broadcast_to(own, (8, SPAN))


def fetch(pairs_of_refs, sems):
    copies = [pltpu.make_async_copy(source, target, sems.at[n]) for n, (source, target) in enumerate(pairs_of_refs)]
    for copy in copies:
        copy.start()
    return copies


def add_terms(factor, part, docs_ref, c, q_ref, k_ref, v_ref, g_ref, outs, off, extra=None):
    in_first, in_last = document_masks(docs_ref[...])
    for t, out in enumerate(outs):
        for i in range(part):
            at = columns((c ^ t) * part + i)
            forward = transposed_dot(jnp.where(in_last, k_ref[:, at], 0), v_ref[:, at]) * factor
            backward = transposed_dot(jnp.where(in_first, q_ref[:, at], 0), g_ref[:, at]) * factor
            if extra is not None:
                add_f, add_b = extra((c ^ t) * part + i)
                forward, backward = forward + add_f, backward + add_b
            out[0, off + i] = forward.astype(BF16)
            out[1, off + i] = backward.astype(BF16)


def group_columns(group, unit):
    return pl.ds(group * unit * DH, unit * DH)


def rest_terms(factor, unit, part, places, mates, ids, docs_ref, q_hbm, k_hbm, v_hbm, g_hbm, *refs):
    outs, (q_ref, k_ref, v_ref, g_ref, sems) = refs[:-5], refs[-5:]
    waiting = []
    for s, (g, mate) in enumerate(zip(places, mates)):
        forward, backward = group_columns(g, unit), group_columns(mate, unit)
        waiting.append(fetch(
            [
                (k_hbm.at[:, forward], k_ref.at[s]), (v_hbm.at[:, forward], v_ref.at[s]),
                (q_hbm.at[:, backward], q_ref.at[s]), (g_hbm.at[:, backward], g_ref.at[s]),
            ],
            sems.at[s],
        ))
    for s in range(len(places)):
        for copy in waiting[s]:
            copy.wait()
        add_terms(
            factor, part, docs_ref, ids[1], q_ref.at[s], k_ref.at[s], v_ref.at[s], g_ref.at[s], outs, s * part
        )


def lead_terms(
    factor, unit, part, places, mates, outer, inner, ids, docs_ref, labels, q_hbm, k_hbm, v_hbm, g_hbm, carry_hbm, cot_hbm,
    *refs,
):
    outs, sent, (q_ref, k_ref, v_ref, g_ref, carry_ref, cot_ref, sems) = refs[:inner], refs[inner], refs[inner + 1 :]
    o, c, z = ids[0], ids[1], ids[2]
    waiting = [fetch([(carry_hbm, carry_ref), (cot_hbm, cot_ref)], sems.at[len(places)])]
    for s, (g, mate) in enumerate(zip(places, mates)):
        forward, backward = group_columns(g, unit), group_columns(mate, unit)
        waiting.append(fetch(
            [
                (k_hbm.at[:, forward], k_ref.at[s]), (v_hbm.at[:, forward], v_ref.at[s]),
                (q_hbm.at[:, backward], q_ref.at[s]), (g_hbm.at[:, backward], g_ref.at[s]),
            ],
            sems.at[s],
        ))
    for copy in waiting[0]:
        copy.wait()
    first, last = own_row(labels, z), own_row(labels, DEPTH + z)
    newest = labels[2 * DEPTH - 1 : 2 * DEPTH, :]
    opens, closes = jnp.logical_and(o == 0, c == 0), jnp.logical_and(o == outer - 1, c == inner - 1)
    for s in range(len(places)):
        for copy in waiting[1 + s]:
            copy.wait()
        open_f = flag(jnp.logical_and(jnp.logical_and(opens, z == s), last == 0.0))
        close_b = flag(jnp.logical_and(jnp.logical_and(closes, z == DEPTH - 1 - s), first == newest)) * factor

        def extra(place):
            return open_f * carry_ref[place], close_b * cot_ref[place]

        add_terms(
            factor, part, docs_ref, c, q_ref.at[s], k_ref.at[s], v_ref.at[s], g_ref.at[s], outs, s * part, extra
        )
    _, side, at_end = place_of(ids)

    @pl.when(at_end)
    def _():
        for t, term in enumerate(outs):
            hop(side, edge_rows(z, labels, None), True, 0, part, term, None, None, 0, sent, t * part)

    @pl.when(jnp.logical_not(at_end))
    def _():
        for i in range(unit):
            sent[0, i] = jnp.where(side == 0, carry_ref[i], cot_ref[i] * factor).astype(BF16)


def block_rows(labels, z, grouped):
    if grouped:
        return [l[0:1, :] for l in labels], [l[2 * DEPTH - 1 : 2 * DEPTH, :] for l in labels]
    return [own_row(l, z) for l in labels], [own_row(l, DEPTH + z) for l in labels]


def sum_kernel(inner, levels, grouped, ids, *refs):
    labels, terms, outs = refs[:inner], refs[inner : 2 * inner], refs[2 * inner :]
    o, z = ids[0], ids[2]
    count = terms[0].shape[1]
    newest = functools.reduce(jnp.maximum, [l[2 * DEPTH - 1 : 2 * DEPTH, :] for l in labels])
    oldest = functools.reduce(jnp.minimum, [l[0:1, :] for l in labels])
    firsts, lasts = block_rows(labels, z, grouped)
    keep_f = [flag(l == newest) for l in lasts]
    keep_b = [flag(l == oldest) for l in firsts]
    low = [((o >> level) & 1) == 0 for level in range(levels)]
    for i in range(count):
        sum_f = sum(m * r[0, i].astype(F32) for m, r in zip(keep_f, terms)).astype(BF16)
        sum_b = sum(m * r[1, i].astype(F32) for m, r in zip(keep_b, terms)).astype(BF16)
        for chosen, out in zip(low, outs):
            out[i * DH : (i + 1) * DH, :] = jnp.where(chosen, sum_f, sum_b)
    rows = lax.broadcasted_iota(jnp.int32, (LABELS, DH), 0)
    marks = jnp.where(rows < LABELS // 2, jnp.broadcast_to(newest, (LABELS, DH)), jnp.broadcast_to(oldest, (LABELS, DH)))
    for out in outs:
        out[count * DH :, :] = marks.astype(BF16)


def prefix_kernel(factor, unit, part, places, mates, inner, outer, grouped, lacking, ids, carry_ref, cot_ref, *refs):
    lacked, refs = (refs[0], refs[1:]) if lacking else (None, refs)
    labels, terms, fans = refs[:inner], refs[inner : 2 * inner], refs[2 * inner : 2 * inner + outer - 1]
    outs, edge_ref = refs[2 * inner + outer - 1 : -1], refs[-1]
    o, c, z = ids[0], ids[1], ids[2]
    held = carry_ref.shape[0]
    count = terms[0].shape[1]
    group_first, group_last = block_rows(labels, z, True)
    block_first, block_last = block_rows(labels, z, grouped)
    marks = [r[count * DH : count * DH + LABELS, :].astype(F32) for r in fans]
    outer_last = [m[0:1] for m in marks]
    outer_first = [m[LABELS // 2 : LABELS // 2 + 1] for m in marks]
    newest = functools.reduce(jnp.maximum, group_last + outer_last)
    prior_base, later_base = jnp.zeros_like(newest), newest
    earlier = [(o ^ (d + 1)) < o for d in range(outer - 1)]
    for d in range(outer - 1):
        prior_base = jnp.maximum(prior_base, jnp.where(earlier[d], outer_last[d], 0.0))
        later_base = jnp.minimum(later_base, jnp.where(earlier[d], newest, outer_first[d]))
    priors, laters, plans = [], [], []
    for t in range(inner):
        prior, later = prior_base, later_base
        for d in range(inner):
            if d != t:
                before = (c ^ d) < (c ^ t)
                prior = jnp.maximum(prior, jnp.where(before, group_last[d], 0.0))
                later = jnp.minimum(later, jnp.where(before, newest, group_first[d]))
        forward = [(flag(jnp.logical_and(earlier[d], outer_last[d] == prior)), fans[d], None) for d in range(outer - 1)]
        backward = [
            (flag(jnp.logical_and(jnp.logical_not(earlier[d]), outer_first[d] == later)), fans[d], None)
            for d in range(outer - 1)
        ]
        for d in range(inner):
            if d != t:
                before = (c ^ d) < (c ^ t)
                forward.append((flag(jnp.logical_and(before, block_last[d] == prior)), terms[d], 0))
                backward.append((flag(jnp.logical_and(jnp.logical_not(before), block_first[d] == later)), terms[d], 1))
        take_f, take_b = prior == 0.0, later == newest
        if grouped:
            take_f = jnp.logical_and(take_f, jnp.logical_and(o == 0, (c ^ t) == 0))
            take_b = jnp.logical_and(take_b, jnp.logical_and(o == outer - 1, (c ^ t) == inner - 1))
        priors.append(prior)
        laters.append(later)
        plans.append((forward, backward, flag(take_f), flag(take_b)))
    for s, (g, mate) in enumerate(zip(places, mates)):
        for i in range(part):
            at = s * part + i

            def carried(head, ref):
                place = head - z * held
                mine = jnp.logical_and(place >= 0, place < held)
                return jnp.where(mine, ref[jnp.clip(place, 0, held - 1)], 0.0)

            carries = [
                carried(g * unit + c * part + i, carry_ref),
                carried(mate * unit + c * part + i, cot_ref) * factor,
            ]
            if lacking:
                more = lacked[0, c * part + i].astype(F32)
                carries[0] = carries[0] + jnp.where(z == 0, more, 0.0)
                carries[1] = carries[1] + jnp.where(z == DEPTH - 1, more, 0.0)

            def value(ref, side):
                return (ref[at * DH : (at + 1) * DH, :] if side is None else ref[side, at]).astype(F32)

            for t, out in enumerate(outs):
                for side in range(2):
                    amount = plans[t][2 + side] * carries[side]
                    for weight, ref, which in plans[t][side]:
                        amount = amount + weight * value(ref, which)
                    out[side, at] = amount.astype(BF16)
    edge_ref[0:1, :] = priors[0]
    edge_ref[1:2, :] = laters[0]
    edge_ref[2:8, :] = jnp.broadcast_to(newest, (6, DH))


def place_of(ids):
    z = ids[2]
    side = jnp.where(z >= DEPTH // 2, 1, 0)
    return z, side, jnp.logical_or(z == 0, z == DEPTH - 1)


def edge_rows(z, labels, edges):
    first, last = own_row(labels, z), own_row(labels, DEPTH + z)
    last_before = own_row(labels, DEPTH + jnp.maximum(z - 1, 0))
    first_after = own_row(labels, jnp.minimum(z + 1, DEPTH - 1))
    final_f, final_b = labels[2 * DEPTH - 1 : 2 * DEPTH, :], labels[0:1, :]
    prior = later = final_f
    if edges is not None:
        prior, later = edges[0:1, :], edges[1:2, :]
    return (last, last_before, final_f, first, prior), (first, first_after, final_b, last, later)


def pick(which, rows):
    return [jnp.where(which == 0, a, b) for a, b in zip(*rows)]


def hop(side, rows, lead, off, part, term_ref, prefix_ref, got_ref, got_off, out, out_off):
    own, neighbour, _, _, prior = pick(side, rows)
    other, _, final, _, _ = pick(1 - side, rows)
    join, keep, counts = flag(prior == own), flag(neighbour == own), flag(other == final)
    for i in range(part):
        state = term_ref[side, off + i].astype(F32)
        if lead:
            rest = counts * term_ref[1 - side, off + i].astype(F32)
        else:
            state = state + join * prefix_ref[side, off + i].astype(F32)
            rest = prefix_ref[1 - side, off + i].astype(F32)
        if got_ref is not None:
            state = state + keep * got_ref[0, got_off + i].astype(F32)
            rest = rest + got_ref[1, got_off + i].astype(F32)
        out[0, out_off + i] = state.astype(BF16)
        out[1, out_off + i] = rest.astype(BF16)


def hop_kernel(part, near, far, across, has_edges, ids, labels, *refs):
    z, side, at_end = place_of(ids)
    out, refs = refs[-1], list(refs[:-1])
    rows = edge_rows(z, labels, refs.pop(0) if has_edges else None)

    def take(plans):
        return [(plan, refs.pop(0), None if plan[0] else refs.pop(0), refs.pop(0) if plan[2] is not None else None) for plan in plans]

    near, far = take(near), take(far)

    def write(side, entries):
        for n, ((lead, off, got_off), term, prefix, got) in enumerate(entries):
            hop(side, rows, lead, off, part, term, prefix, got, got_off, out, n * part)

    if near:
        pl.when(at_end)(lambda: write(side, near))
    if far:
        pl.when(jnp.logical_not(at_end))(lambda: write(side if across else 1 - side, far))


def lead_total_kernel(part, plans, ids, labels, *refs):
    z, side, at_end = place_of(ids)
    rows = edge_rows(z, labels, None)
    for t, (off, near_off, middle_off, far_off) in enumerate(plans):
        term, near, middle, far = refs[4 * t : 4 * t + 4]
        out = refs[4 * len(plans) + t]

        def total(which, over, over_off, rest, rest_off):
            own, neighbour, final, _, _ = pick(which, rows)
            counts, come = flag(own == final), flag(neighbour == final)
            for i in range(part):
                value = counts * term[which, off + i].astype(F32)
                if over is not None:
                    value = value + come * over[0, over_off + i].astype(F32)
                if rest is not None:
                    value = value + rest[1, rest_off + i].astype(F32)
                out[which, i] = value.astype(BF16)

        @pl.when(at_end)
        def _():
            total(side, None, 0, far, far_off)
            total(1 - side, far, far_off, None, 0)

        @pl.when(jnp.logical_not(at_end))
        def _():
            total(side, near, near_off, middle, middle_off)
            total(1 - side, middle, middle_off, near, near_off)


def local_kernel(factor, base, count, docs_ref, row_ref, q_ref, k_ref, v_ref, g_ref, out):
    docs = docs_ref[...]
    places = lax.broadcasted_iota(jnp.int32, (SPAN, SPAN), 0)
    others = lax.broadcasted_iota(jnp.int32, (SPAN, SPAN), 1)
    allowed = jnp.logical_and(others <= places, docs == row_ref[0:1])
    for i in range(count):
        at = slice((base + i) * DH, (base + i + 1) * DH)
        q, k, v, g = q_ref[:, at], k_ref[:, at], v_ref[:, at], g_ref[:, at]
        scores = jnp.where(allowed, dot_transposed(q, k) * factor, 0.0).astype(BF16)
        grad_scores = jnp.where(allowed, dot_transposed(g, v) * factor, 0.0).astype(BF16)
        out[0, i] = dot(scores, v)
        out[1, i] = dot(grad_scores, k)
        out[2, i] = transposed_dot(grad_scores, q)
        out[3, i] = transposed_dot(scores, g)


def output_kernel(unit, part, plans, ids, labels, edges, docs_ref, q_ref, k_ref, v_ref, g_ref, *refs):
    count = len(plans)
    sources, locals_ = refs[: 4 * count], refs[4 * count : 5 * count]
    outs, (states, held, sems) = refs[-7:-3], refs[-3:]
    c = ids[1]
    z, side, at_end = place_of(ids)
    rows = edge_rows(z, labels, edges)

    def make_states(ends, side):
        for n, (which, _, _, lead, off, near_off, middle_off, far_off) in enumerate(plans):
            prefix, near, middle, far = sources[4 * n : 4 * n + 4]
            _, neighbour, _, target, prior = rows[which]
            reach, come = flag(prior == target), flag(neighbour == target)
            if ends:
                over, rest = (None, (far, far_off)) if side == which else ((far, far_off), None)
            elif side == which:
                over, rest = (near, near_off), (middle, middle_off)
            else:
                over, rest = (middle, middle_off), (near, near_off)
            for i in range(part):
                value = reach * prefix[which, off + i].astype(F32)
                if over is not None:
                    value = value + come * over[0][0, over[1] + i].astype(F32)
                if rest is not None and not lead:
                    value = value + reach * rest[0][1, rest[1] + i].astype(F32)
                states[n, i] = value.astype(BF16)

    for ends in (True, False):
        for which in range(2):
            here = jnp.logical_and(at_end if ends else jnp.logical_not(at_end), side == which)
            pl.when(here)(functools.partial(make_states, ends, which))

    in_first, in_last = document_masks(docs_ref[...])
    copies = []
    for n, (which, group, turn, *_) in enumerate(plans):
        place = (c ^ turn) * part
        for i in range(part):
            at = columns(group * unit + place + i)
            state = states[n, i]
            if which == 0:
                results = (
                    dot(jnp.where(in_first, q_ref[:, at], 0), state),
                    dot_transposed(jnp.where(in_first, g_ref[:, at], 0), state),
                )
            else:
                results = (
                    dot_transposed(jnp.where(in_last, v_ref[:, at], 0), state),
                    dot(jnp.where(in_last, k_ref[:, at], 0), state),
                )
            for m, result in enumerate(results):
                held[n, m, i] = (locals_[n][2 * which + m, place + i] + result).astype(BF16)
                copy = pltpu.make_async_copy(held.at[n, m, i], outs[2 * which + m].at[:, at], sems.at[n, m, i])
                copy.start()
                copies.append(copy)
    for copy in copies:
        copy.wait()


def shards(queries, keys, values, out_grad, doc_ids, carry_in, carry_cot):
    outer, inner, depth = (lax.axis_size(a) for a in ("outer", "inner", "heads"))
    assert depth == DEPTH
    tokens_all = doc_ids.shape[0] * outer * inner
    factor = float(DH * (tokens_all // 2)) ** (-0.5)
    head_count = queries.shape[1] // DH
    held = carry_in.shape[0]
    part = min(4, head_count // inner)
    unit = part * inner
    groups = head_count // unit
    leads = 2 if held == unit and groups == DEPTH and inner == 2 else 0
    costs = iter(COSTS if leads else ())

    def mate(g):
        return groups - 1 - g if leads else g

    ids = jnp.stack([lax.axis_index(a) for a in ("outer", "inner", "heads")]).astype(jnp.int32)
    token, (own_labels, docs_column, docs_row) = call(
        jnp.zeros((8, DH), F32),
        label_kernel,
        (ids, doc_ids.reshape(depth, SPAN)),
        [
            jax.ShapeDtypeStruct((2 * depth, DH), F32),
            jax.ShapeDtypeStruct((SPAN, SPAN), F32),
            jax.ShapeDtypeStruct((8, SPAN), F32),
        ],
    )
    labels = [own_labels] + [pairs(own_labels, "inner", d) for d in range(1, inner)]

    levels = (outer - 1).bit_length()

    def state_pair(count):
        return jax.ShapeDtypeStruct((2, count, DH, DH), BF16)

    terms, prefixes, near, middle, far, local = {}, {}, {}, {}, {}, {}
    edge, arrays, carries = None, (queries, keys, values, out_grad), (carry_in, carry_cot)
    far_arrays, far_carries = (
        tuple(pltpu.with_memory_space_constraint(a, pltpu.HBM) for a in group) for group in (arrays, carries)
    )

    def exchange(own):
        return [own[0]] + [pairs(own[d], "inner", d) for d in range(1, inner)]

    def receive(units, kind, sent, perm):
        got = lax.ppermute(sent, "heads", perm)
        for n, u in enumerate(units):
            kind[u] = (got, n * part)
        return got

    def run(*args, **options):
        nonlocal token
        token, outs = call(token, *args, cost=next(costs, 0), **options)
        return outs

    def make_lead_terms():
        places = tuple(range(leads))
        block = pltpu.VMEM((leads, SPAN, unit * DH), BF16)
        carry = pltpu.VMEM((unit, DH, DH), F32)
        own = run(
            functools.partial(
                lead_terms, factor, unit, part, places, tuple(mate(g) for g in places), outer, inner
            ),
            (ids, docs_column, own_labels) + far_arrays + far_carries,
            [state_pair(part * leads)] * inner + [state_pair(unit)],
            scratch=[block] * 4 + [carry] * 2 + [pltpu.SemaphoreType.DMA((leads + 1, 4))],
            specs=[SMEM, VMEM, VMEM] + [HBM] * 6,
        )
        for g in places:
            terms[g] = [(a, g * part) for a in own[:inner]]
        return receive([(0, t) for t in range(inner)], near, own[inner], [(0, 1), (3, 2), (1, 0), (2, 3)])

    def make_terms(places):
        own = run(
            functools.partial(rest_terms, factor, unit, part, places, tuple(mate(g) for g in places)),
            (ids, docs_column) + far_arrays,
            [state_pair(part * len(places))] * inner,
            scratch=[pltpu.VMEM((len(places), SPAN, unit * DH), BF16)] * 4
            + [pltpu.SemaphoreType.DMA((len(places), 4))],
            specs=[SMEM, VMEM] + [HBM] * 4,
        )
        for s, g in enumerate(places):
            terms[g] = [(a, s * part) for a in own]
        return exchange(own)

    def make_sums(received, grouped):
        nonlocal token
        count = received[0].shape[1]
        sums = run(
            functools.partial(sum_kernel, inner, levels, grouped),
            (ids, *labels, *received),
            [jax.ShapeDtypeStruct((count * DH + LABELS, DH), BF16)] * levels,
        )
        return [pairs(sums[d.bit_length() - 1], "outer", d) for d in range(1, outer)]

    def make_prefixes(places, received, fans, grouped, lacked=None):
        nonlocal edge
        count = received[0].shape[1]
        given = run(
            functools.partial(
                prefix_kernel, factor, unit, part, places, tuple(mate(g) for g in places), inner, outer, grouped,
                lacked is not None,
            ),
            (ids, *carries, *([] if lacked is None else [lacked]), *labels, *received, *fans),
            [state_pair(count)] * inner + [jax.ShapeDtypeStruct((8, DH), F32)],
        )
        edge = given[-1] if edge is None else edge
        given = exchange(given[:-1])
        for s, g in enumerate(places):
            prefixes[g] = [(a, s * part) for a in given]

    def move(near_units, far_units, across):
        units = list(near_units) + list(far_units)
        use_edges = not all(g < leads for g, _ in units)
        operands = [ids, own_labels] + ([edge] if use_edges else [])

        def plans_of(chosen, got):
            plans = []
            for u in chosen:
                g, t = u
                lead = g < leads
                array, off = terms[g][t]
                operands.append(array)
                if not lead:
                    operands.append(prefixes[g][t][0])
                if got is not None:
                    operands.append(got[u][0])
                plans.append((lead, off, None if got is None else got[u][1]))
            return plans

        near_plans = plans_of(near_units, None)
        far_plans = plans_of(far_units, near if across else middle)
        sent = run(
            functools.partial(hop_kernel, part, near_plans, far_plans, across, use_edges),
            operands,
            [state_pair(part * max(len(near_units), len(far_units)))],
        )
        return sent[0]

    def ends(near_units, far_units):
        perm = ([(0, 1), (3, 2)] if near_units else []) + ([(1, 0), (2, 3)] if far_units else [])
        got = receive(near_units, near, move(near_units, far_units, False), perm)
        for n, u in enumerate(far_units):
            far[u] = (got, n * part)

    def across(units):
        receive(units, middle, move([], units, True), [(1, 2), (2, 1)])

    def make_local(g):
        out = run(
            functools.partial(local_kernel, factor, g * unit, unit),
            (docs_column, docs_row) + arrays,
            [jax.ShapeDtypeStruct((4, unit, SPAN, DH), F32)],
            specs=[VMEM] * 6,
        )
        local[g] = out[0]

    out_shape = jax.ShapeDtypeStruct(queries.shape, BF16)
    results = ()

    def make_outputs(halves):
        nonlocal results
        operands, plans = (ids, own_labels, edge, docs_column) + arrays, []
        for which, g, t in halves:
            array, off = prefixes[g][t]
            kept = [kind[g, t] for kind in (near, middle, far)]
            heads = mate(g) if which else g
            plans.append((which, heads, t, g < leads, off) + tuple(at for _, at in kept))
            operands += (array,) + tuple(a for a, _ in kept)
        operands += tuple(local[mate(g) if which else g] for which, g, _ in halves)
        count = len(halves)
        results = run(
            functools.partial(output_kernel, unit, part, plans),
            operands + tuple(results),
            [out_shape] * 4,
            scratch=[
                pltpu.VMEM((count, part, DH, DH), BF16),
                pltpu.VMEM((count, 2, part, SPAN, DH), BF16),
                pltpu.SemaphoreType.DMA((count, 2, part)),
            ],
            aliases={len(operands) + i: i for i in range(len(results))},
            specs=[SMEM] + [VMEM] * (len(operands) - 1) + [HBM] * len(results),
            out_specs=[HBM] * 4,
        )

    def make_totals(g):
        operands, plans = [ids, own_labels], []
        for t in range(inner):
            array, off = terms[g][t]
            kept = [kind[g, t] for kind in (near, middle, far)]
            operands += [array] + [a for a, _ in kept]
            plans.append((off,) + tuple(at for _, at in kept))
        totals = run(
            functools.partial(lead_total_kernel, part, plans),
            operands,
            [state_pair(part)] * inner,
        )
        return exchange(totals)

    def chunk(n):
        return [(n, t) for t in range(inner)] if n < leads else [(g, n - leads) for g in range(leads, groups)]

    def halves_of(n):
        return [(which, g, t) for which in range(2) for g, t in chunk(n)]

    if leads:
        kept = {}

        def keep(name, make, *args):
            kept[name] = make(*args)

        def rest_sums():
            kept["fans"] = make_sums(kept["got"], False)

        def rest_prefixes():
            make_prefixes((2, 3), kept["got"], kept["fans"], False)

        def lead_sums(g):
            kept["fans", g] = make_sums(kept["totals", g], True)

        def lead_prefixes(g):
            make_prefixes((g,), kept["totals", g], kept["fans", g], True, kept["lacked"] if g else None)

        steps = {
            "K": lambda g: keep("lacked", make_lead_terms) if g == 0 else keep("got", make_terms, (2, 3)),
            "A": lambda g: rest_sums(),
            "B": lambda g: rest_prefixes(),
            "L": make_local,
            "E": lambda g: ends(chunk(g), []),
            "O": lambda g: across(chunk(g)),
            "F": lambda g: ends([], chunk(g)),
            "J": lambda g: ends(chunk(g), chunk(g - leads)),
            "T": lambda g: keep(("totals", g), make_totals, g),
            "S": lead_sums,
            "P": lead_prefixes,
            "W": lambda g: make_outputs(halves_of(g)),
        }
        for step in ORDER.split():
            steps[step[0]](int(step[1]))
    else:
        assert not leads
        places = tuple(range(groups))
        got = make_terms(places)
        make_prefixes(places, got, make_sums(got, False), False)
        units = [(g, t) for g in range(groups) for t in range(inner)]
        lag = 4
        for k in range(len(units) + lag):
            ends(units[k : k + 1], units[k - lag : k - lag + 1] if k >= lag else [])
            if k < len(units):
                across([units[k]])
        for g in range(groups):
            make_local(g)
        for g, t in units:
            make_outputs([(0, g, t), (1, g, t)])
    return tuple(results)


def solution(mesh):
    tokens = P(("outer", "inner", "heads"), None)
    carry = P("heads", None, None)
    return jax.shard_map(
        shards,
        mesh=mesh,
        in_specs=(tokens,) * 4 + (P(("outer", "inner")), carry, carry),
        out_specs=(tokens,) * 4,
        check_vma=False,
    )
```

```python
import functools

import jax
import jax.numpy as jnp
from jax import lax
from jax.experimental import pallas as pl
from jax.experimental.pallas import tpu as pltpu
from jax.sharding import PartitionSpec as P

DH = 128
SPAN = 128
LABELS = 16
DEPTH = 4
F32 = jnp.float32
BF16 = jnp.bfloat16
VMEM = pl.BlockSpec(memory_space=pltpu.VMEM)
SMEM = pl.BlockSpec(memory_space=pltpu.SMEM)
HBM = pl.BlockSpec(memory_space=pltpu.HBM)
LIMIT = 24 * 1024 * 1024
COSTS = (0, 0, 0, 0, 0, 16, 0, 0, 0, 0, 0, 0, 0, 0, 0, 0, 8, 0, 0, 4, 0, 0, 0, 0, 0, 0, 0)
ORDER = (
    "K0 K1 A0 E1"
    " L3 O0 B0 L0"
    " O1 J2 L1 L2"
    " J3 O2 T0 S0"
    " O3 T1 F2 P0"
    " S1 F3 W0 W2"
    " P1 W1 W3"
)


def pairs(array, axis, distance):
    count = lax.axis_size(axis)
    return lax.ppermute(array, axis, [(i, i ^ distance) for i in range(count)])


def transposed_dot(a, b):
    return lax.dot_general(a, b, (((0,), (0,)), ((), ())), preferred_element_type=F32)


def dot_transposed(a, b):
    return lax.dot_general(a, b, (((1,), (1,)), ((), ())), preferred_element_type=F32)


def dot(a, b):
    return lax.dot_general(a, b, (((1,), (0,)), ((), ())), preferred_element_type=F32)


def flag(row):
    return jnp.where(row, 1.0, 0.0).astype(F32)


def call(token, kernel, operands, out_shape, cost=0, scratch=(), aliases=None, specs=None, out_specs=None):
    count, results = len(operands), len(out_shape)

    def ordered(*refs):
        kernel(*refs[:count], *refs[count + 1 : count + 1 + results], *refs[count + 2 + results :])

    *outs, token = pl.pallas_call(
        ordered,
        in_specs=list(specs or [SMEM] + [VMEM] * (count - 1)) + [VMEM],
        out_specs=list(out_specs or [VMEM] * results) + [VMEM],
        out_shape=list(out_shape) + [jax.ShapeDtypeStruct(token.shape, token.dtype)],
        scratch_shapes=list(scratch),
        input_output_aliases={**(aliases or {}), count: results},
        compiler_params=pltpu.CompilerParams(vmem_limit_bytes=LIMIT),
        cost_estimate=pl.CostEstimate(flops=int(cost * 1e9), bytes_accessed=0, transcendentals=0),
    )(*operands, token)
    return token, outs


def document_masks(docs):
    return docs == docs[0:1], docs == docs[SPAN - 1 : SPAN]


def columns(head):
    return pl.ds(pl.multiple_of(head * DH, DH), DH)


class Pieces:
    def __init__(self, refs):
        self.refs, self.each = refs, refs[0].shape[1]
        self.count = self.each * len(refs)

    def __getitem__(self, at):
        side, i = at
        return self.refs[i // self.each][side, i % self.each]


def in_pieces(refs, counts):
    starts = [sum(counts[:n]) for n in range(len(counts))]
    return [Pieces(refs[a : a + n]) for a, n in zip(starts, counts)]


def own_row(ref, at):
    return ref[pl.ds(at, 1), :]


def label_kernel(ids, docs_hbm, labels_ref, column_ref, row_ref, docs_ref, sem):
    copy = pltpu.make_async_copy(docs_hbm, docs_ref, sem.at[0])
    copy.start()
    copy.wait()
    write_labels(ids, docs_ref, labels_ref, column_ref, row_ref)


def write_labels(ids, docs_ref, labels_ref, column_ref, row_ref):
    docs = docs_ref[...]
    for k in range(DEPTH):
        row = docs[k : k + 1, :].astype(F32)
        labels_ref[k : k + 1, :] = jnp.broadcast_to(row[:, 0:1], (1, DH))
        labels_ref[DEPTH + k : DEPTH + k + 1, :] = jnp.broadcast_to(row[:, SPAN - 1 :], (1, DH))
    own = own_row(docs_ref, ids[2]).astype(F32)
    column_ref[...] = jnp.broadcast_to(own, (SPAN, SPAN)).T
    row_ref[...] = jnp.broadcast_to(own, (8, SPAN))


def fetch(pairs_of_refs, sems):
    copies = [pltpu.make_async_copy(source, target, sems.at[n]) for n, (source, target) in enumerate(pairs_of_refs)]
    for copy in copies:
        copy.start()
    return copies


def add_terms(factor, part, docs_ref, c, q_ref, k_ref, v_ref, g_ref, outs, offs, extra=None):
    in_first, in_last = document_masks(docs_ref[...])
    for t, (out, off) in enumerate(zip(outs, offs)):
        for i in range(part):
            at = columns((c ^ t) * part + i)
            forward = transposed_dot(jnp.where(in_last, k_ref[:, at], 0), v_ref[:, at]) * factor
            backward = transposed_dot(jnp.where(in_first, q_ref[:, at], 0), g_ref[:, at]) * factor
            if extra is not None:
                add_f, add_b = extra((c ^ t) * part + i)
                forward, backward = forward + add_f, backward + add_b
            out[0, off + i] = forward.astype(BF16)
            out[1, off + i] = backward.astype(BF16)


def group_columns(group, unit):
    return pl.ds(group * unit * DH, unit * DH)


def rest_terms(factor, unit, part, places, mates, ids, docs_ref, q_hbm, k_hbm, v_hbm, g_hbm, *refs):
    outs, (q_ref, k_ref, v_ref, g_ref, sems) = refs[:-5], refs[-5:]
    waiting = []
    for s, (g, mate) in enumerate(zip(places, mates)):
        forward, backward = group_columns(g, unit), group_columns(mate, unit)
        waiting.append(fetch(
            [
                (k_hbm.at[:, forward], k_ref.at[s]), (v_hbm.at[:, forward], v_ref.at[s]),
                (q_hbm.at[:, backward], q_ref.at[s]), (g_hbm.at[:, backward], g_ref.at[s]),
            ],
            sems.at[s],
        ))
    for s in range(len(places)):
        for copy in waiting[s]:
            copy.wait()
        add_terms(
            factor, part, docs_ref, ids[1], q_ref.at[s], k_ref.at[s], v_ref.at[s], g_ref.at[s],
            [outs[0]] + list(outs[1 + s :: len(places)]), [s * part] + [0] * (len(outs) // len(places)),
        )


def lead_terms(
    factor, unit, part, places, mates, outer, inner, ids, docs_hbm, q_hbm, k_hbm, v_hbm, g_hbm, carry_hbm, cot_hbm, *refs,
):
    outs, sent, labels, docs_ref, row_ref = refs[:inner], refs[inner], *refs[inner + 1 : inner + 4]
    blocks_ref, q_ref, k_ref, v_ref, g_ref, carry_ref, sems = refs[inner + 4 :]
    o, c, z = ids[0], ids[1], ids[2]
    _, side, at_end = place_of(ids)
    copy = pltpu.make_async_copy(docs_hbm, blocks_ref, sems.at[len(places), 0])
    copy.start()
    waiting = []
    for s, (g, mate) in enumerate(zip(places, mates)):
        forward, backward = group_columns(g, unit), group_columns(mate, unit)
        waiting.append(fetch(
            [
                (k_hbm.at[:, forward], k_ref.at[s]), (v_hbm.at[:, forward], v_ref.at[s]),
                (q_hbm.at[:, backward], q_ref.at[s]), (g_hbm.at[:, backward], g_ref.at[s]),
            ],
            sems.at[s],
        ))

    def carries(act):
        for which, source in enumerate((carry_hbm, cot_hbm)):

            @pl.when(side == which)
            def _():
                act(pltpu.make_async_copy(source, carry_ref, sems.at[len(places), 1 + which]))

    carries(lambda copy: copy.start())
    copy.wait()
    write_labels(ids, blocks_ref, labels, docs_ref, row_ref)
    first, last = own_row(labels, z), own_row(labels, DEPTH + z)
    newest = labels[2 * DEPTH - 1 : 2 * DEPTH, :]
    opens, closes = jnp.logical_and(o == 0, c == 0), jnp.logical_and(o == outer - 1, c == inner - 1)
    for s in range(len(places)):
        for copy in waiting[s]:
            copy.wait()
        if s == 0:
            carries(lambda copy: copy.wait())
        open_f = flag(jnp.logical_and(jnp.logical_and(opens, z == s), last == 0.0))
        close_b = flag(jnp.logical_and(jnp.logical_and(closes, z == DEPTH - 1 - s), first == newest)) * factor

        def extra(place):
            return open_f * carry_ref[place], close_b * carry_ref[place]

        add_terms(
            factor, part, docs_ref, c, q_ref.at[s], k_ref.at[s], v_ref.at[s], g_ref.at[s], outs, [s * part] * inner, extra
        )

    @pl.when(at_end)
    def _():
        for t, term in enumerate(outs):
            hop(side, edge_rows(z, labels, None), True, 0, part, term, None, 0, None, 0, sent, t * part)

    @pl.when(jnp.logical_not(at_end))
    def _():
        scale = jnp.where(side == 0, 1.0, factor)
        for i in range(unit):
            sent[0, i] = (carry_ref[i] * scale).astype(BF16)


def block_rows(labels, z, grouped):
    if grouped:
        return [l[0:1, :] for l in labels], [l[2 * DEPTH - 1 : 2 * DEPTH, :] for l in labels]
    return [own_row(l, z) for l in labels], [own_row(l, DEPTH + z) for l in labels]


def sum_kernel(counts, levels, grouped, ids, *refs):
    inner, behind = len(counts), len(counts) + sum(counts)
    labels, terms, outs = refs[:inner], in_pieces(refs[inner:behind], counts), refs[behind:]
    o, z = ids[0], ids[2]
    count = terms[0].count
    newest = functools.reduce(jnp.maximum, [l[2 * DEPTH - 1 : 2 * DEPTH, :] for l in labels])
    oldest = functools.reduce(jnp.minimum, [l[0:1, :] for l in labels])
    firsts, lasts = block_rows(labels, z, grouped)
    keep_f = [flag(l == newest) for l in lasts]
    keep_b = [flag(l == oldest) for l in firsts]
    low = [((o >> level) & 1) == 0 for level in range(levels)]
    for i in range(count):
        sum_f = sum(m * r[0, i].astype(F32) for m, r in zip(keep_f, terms)).astype(BF16)
        sum_b = sum(m * r[1, i].astype(F32) for m, r in zip(keep_b, terms)).astype(BF16)
        for chosen, out in zip(low, outs):
            out[i * DH : (i + 1) * DH, :] = jnp.where(chosen, sum_f, sum_b)
    rows = lax.broadcasted_iota(jnp.int32, (LABELS, DH), 0)
    marks = jnp.where(rows < LABELS // 2, jnp.broadcast_to(newest, (LABELS, DH)), jnp.broadcast_to(oldest, (LABELS, DH)))
    for out in outs:
        out[count * DH :, :] = marks.astype(BF16)


def prefix_kernel(factor, unit, part, places, mates, counts, outer, grouped, lacking, ids, carry_ref, cot_ref, *refs):
    lacked, refs = (refs[0], refs[1:]) if lacking else (None, refs)
    inner, behind = len(counts), len(counts) + sum(counts)
    labels, terms, fans = refs[:inner], in_pieces(refs[inner:behind], counts), refs[behind : behind + outer - 1]
    outs, edge_ref = refs[behind + outer - 1 : -1], refs[-1]
    o, c, z = ids[0], ids[1], ids[2]
    held = carry_ref.shape[0]
    count = terms[0].count
    group_first, group_last = block_rows(labels, z, True)
    block_first, block_last = block_rows(labels, z, grouped)
    marks = [r[count * DH : count * DH + LABELS, :].astype(F32) for r in fans]
    outer_last = [m[0:1] for m in marks]
    outer_first = [m[LABELS // 2 : LABELS // 2 + 1] for m in marks]
    newest = functools.reduce(jnp.maximum, group_last + outer_last)
    prior_base, later_base = jnp.zeros_like(newest), newest
    earlier = [(o ^ (d + 1)) < o for d in range(outer - 1)]
    for d in range(outer - 1):
        prior_base = jnp.maximum(prior_base, jnp.where(earlier[d], outer_last[d], 0.0))
        later_base = jnp.minimum(later_base, jnp.where(earlier[d], newest, outer_first[d]))
    priors, laters, plans = [], [], []
    for t in range(inner):
        prior, later = prior_base, later_base
        for d in range(inner):
            if d != t:
                before = (c ^ d) < (c ^ t)
                prior = jnp.maximum(prior, jnp.where(before, group_last[d], 0.0))
                later = jnp.minimum(later, jnp.where(before, newest, group_first[d]))
        forward = [(flag(jnp.logical_and(earlier[d], outer_last[d] == prior)), fans[d], None) for d in range(outer - 1)]
        backward = [
            (flag(jnp.logical_and(jnp.logical_not(earlier[d]), outer_first[d] == later)), fans[d], None)
            for d in range(outer - 1)
        ]
        for d in range(inner):
            if d != t:
                before = (c ^ d) < (c ^ t)
                forward.append((flag(jnp.logical_and(before, block_last[d] == prior)), terms[d], 0))
                backward.append((flag(jnp.logical_and(jnp.logical_not(before), block_first[d] == later)), terms[d], 1))
        take_f, take_b = prior == 0.0, later == newest
        if grouped:
            take_f = jnp.logical_and(take_f, jnp.logical_and(o == 0, (c ^ t) == 0))
            take_b = jnp.logical_and(take_b, jnp.logical_and(o == outer - 1, (c ^ t) == inner - 1))
        priors.append(prior)
        laters.append(later)
        plans.append((forward, backward, flag(take_f), flag(take_b)))
    for s, (g, mate) in enumerate(zip(places, mates)):
        for i in range(part):
            at = s * part + i

            def carried(head, ref):
                place = head - z * held
                mine = jnp.logical_and(place >= 0, place < held)
                return jnp.where(mine, ref[jnp.clip(place, 0, held - 1)], 0.0)

            carries = [
                carried(g * unit + c * part + i, carry_ref),
                carried(mate * unit + c * part + i, cot_ref) * factor,
            ]
            if lacking:
                more = lacked[0, c * part + i].astype(F32)
                carries[0] = carries[0] + jnp.where(z == 0, more, 0.0)
                carries[1] = carries[1] + jnp.where(z == DEPTH - 1, more, 0.0)

            def value(ref, side):
                return (ref[at * DH : (at + 1) * DH, :] if side is None else ref[side, at]).astype(F32)

            for t, out in enumerate(outs):
                for side in range(2):
                    amount = plans[t][2 + side] * carries[side]
                    for weight, ref, which in plans[t][side]:
                        amount = amount + weight * value(ref, which)
                    out[side, at] = amount.astype(BF16)
    edge_ref[0:1, :] = priors[0]
    edge_ref[1:2, :] = laters[0]
    edge_ref[2:8, :] = jnp.broadcast_to(newest, (6, DH))


def place_of(ids):
    z = ids[2]
    side = jnp.where(z >= DEPTH // 2, 1, 0)
    return z, side, jnp.logical_or(z == 0, z == DEPTH - 1)


def edge_rows(z, labels, edges):
    first, last = own_row(labels, z), own_row(labels, DEPTH + z)
    last_before = own_row(labels, DEPTH + jnp.maximum(z - 1, 0))
    first_after = own_row(labels, jnp.minimum(z + 1, DEPTH - 1))
    final_f, final_b = labels[2 * DEPTH - 1 : 2 * DEPTH, :], labels[0:1, :]
    prior = later = final_f
    if edges is not None:
        prior, later = edges[0:1, :], edges[1:2, :]
    return (last, last_before, final_f, first, prior), (first, first_after, final_b, last, later)


def pick(which, rows):
    return [jnp.where(which == 0, a, b) for a, b in zip(*rows)]


def hop(side, rows, lead, off, part, term_ref, prefix_ref, prefix_off, got_ref, got_off, out, out_off):
    own, neighbour, _, _, prior = pick(side, rows)
    other, _, final, _, _ = pick(1 - side, rows)
    join, keep, counts = flag(prior == own), flag(neighbour == own), flag(other == final)
    for i in range(part):
        state = term_ref[side, off + i].astype(F32)
        if lead:
            rest = counts * term_ref[1 - side, off + i].astype(F32)
        else:
            state = state + join * prefix_ref[side, prefix_off + i].astype(F32)
            rest = prefix_ref[1 - side, prefix_off + i].astype(F32)
        if got_ref is not None:
            state = state + keep * got_ref[0, got_off + i].astype(F32)
            rest = rest + got_ref[1, got_off + i].astype(F32)
        out[0, out_off + i] = state.astype(BF16)
        out[1, out_off + i] = rest.astype(BF16)


def hop_kernel(part, near, far, across, has_edges, ids, labels, *refs):
    z, side, at_end = place_of(ids)
    out, refs = refs[-1], list(refs[:-1])
    rows = edge_rows(z, labels, refs.pop(0) if has_edges else None)

    def take(plans):
        return [(plan, refs.pop(0), None if plan[0] else refs.pop(0), refs.pop(0) if plan[3] is not None else None) for plan in plans]

    near, far = take(near), take(far)

    def write(side, entries):
        for n, ((lead, off, prefix_off, got_off), term, prefix, got) in enumerate(entries):
            hop(side, rows, lead, off, part, term, prefix, prefix_off, got, got_off, out, n * part)

    if near:
        pl.when(at_end)(lambda: write(side, near))
    if far:
        pl.when(jnp.logical_not(at_end))(lambda: write(side if across else 1 - side, far))


def lead_total_kernel(part, plans, ids, labels, *refs):
    z, side, at_end = place_of(ids)
    rows = edge_rows(z, labels, None)
    for t, (off, near_off, middle_off, far_off) in enumerate(plans):
        term, near, middle, far = refs[4 * t : 4 * t + 4]
        out = refs[4 * len(plans) + t]

        def total(which, over, over_off, rest, rest_off):
            own, neighbour, final, _, _ = pick(which, rows)
            counts, come = flag(own == final), flag(neighbour == final)
            for i in range(part):
                value = counts * term[which, off + i].astype(F32)
                if over is not None:
                    value = value + come * over[0, over_off + i].astype(F32)
                if rest is not None:
                    value = value + rest[1, rest_off + i].astype(F32)
                out[which, i] = value.astype(BF16)

        @pl.when(at_end)
        def _():
            total(side, None, 0, far, far_off)
            total(1 - side, far, far_off, None, 0)

        @pl.when(jnp.logical_not(at_end))
        def _():
            total(side, near, near_off, middle, middle_off)
            total(1 - side, middle, middle_off, near, near_off)


def local_kernel(factor, base, count, docs_ref, row_ref, q_ref, k_ref, v_ref, g_ref, out):
    docs = docs_ref[...]
    places = lax.broadcasted_iota(jnp.int32, (SPAN, SPAN), 0)
    others = lax.broadcasted_iota(jnp.int32, (SPAN, SPAN), 1)
    allowed = jnp.logical_and(others <= places, docs == row_ref[0:1])
    for i in range(count):
        at = slice((base + i) * DH, (base + i + 1) * DH)
        q, k, v, g = q_ref[:, at], k_ref[:, at], v_ref[:, at], g_ref[:, at]
        scores = jnp.where(allowed, dot_transposed(q, k) * factor, 0.0).astype(BF16)
        grad_scores = jnp.where(allowed, dot_transposed(g, v) * factor, 0.0).astype(BF16)
        out[0, i] = dot(scores, v)
        out[1, i] = dot(grad_scores, k)
        out[2, i] = transposed_dot(grad_scores, q)
        out[3, i] = transposed_dot(scores, g)


def output_kernel(unit, part, plans, ids, labels, edges, docs_ref, q_ref, k_ref, v_ref, g_ref, *refs):
    count = len(plans)
    sources, locals_ = refs[: 4 * count], refs[4 * count : 5 * count]
    outs, (states, held, sems) = refs[-7:-3], refs[-3:]
    c = ids[1]
    z, side, at_end = place_of(ids)
    rows = edge_rows(z, labels, edges)

    def make_states(ends, side):
        for n, (which, _, _, lead, off, near_off, middle_off, far_off) in enumerate(plans):
            prefix, near, middle, far = sources[4 * n : 4 * n + 4]
            _, neighbour, _, target, prior = rows[which]
            reach, come = flag(prior == target), flag(neighbour == target)
            if ends:
                over, rest = (None, (far, far_off)) if side == which else ((far, far_off), None)
            elif side == which:
                over, rest = (near, near_off), (middle, middle_off)
            else:
                over, rest = (middle, middle_off), (near, near_off)
            for i in range(part):
                value = reach * prefix[which, off + i].astype(F32)
                if over is not None:
                    value = value + come * over[0][0, over[1] + i].astype(F32)
                if rest is not None and not lead:
                    value = value + reach * rest[0][1, rest[1] + i].astype(F32)
                states[n, i] = value.astype(BF16)

    for ends in (True, False):
        for which in range(2):
            here = jnp.logical_and(at_end if ends else jnp.logical_not(at_end), side == which)
            pl.when(here)(functools.partial(make_states, ends, which))

    in_first, in_last = document_masks(docs_ref[...])
    copies = []
    for n, (which, group, turn, *_) in enumerate(plans):
        place = (c ^ turn) * part
        for i in range(part):
            at = columns(group * unit + place + i)
            state = states[n, i]
            if which == 0:
                results = (
                    dot(jnp.where(in_first, q_ref[:, at], 0), state),
                    dot_transposed(jnp.where(in_first, g_ref[:, at], 0), state),
                )
            else:
                results = (
                    dot_transposed(jnp.where(in_last, v_ref[:, at], 0), state),
                    dot(jnp.where(in_last, k_ref[:, at], 0), state),
                )
            for m, result in enumerate(results):
                held[n, m, i] = (locals_[n][2 * which + m, place + i] + result).astype(BF16)
                copy = pltpu.make_async_copy(held.at[n, m, i], outs[2 * which + m].at[:, at], sems.at[n, m, i])
                copy.start()
                copies.append(copy)
    for copy in copies:
        copy.wait()


def shards(queries, keys, values, out_grad, doc_ids, carry_in, carry_cot):
    outer, inner, depth = (lax.axis_size(a) for a in ("outer", "inner", "heads"))
    assert depth == DEPTH
    tokens_all = doc_ids.shape[0] * outer * inner
    factor = float(DH * (tokens_all // 2)) ** (-0.5)
    head_count = queries.shape[1] // DH
    held = carry_in.shape[0]
    part = min(4, head_count // inner)
    unit = part * inner
    groups = head_count // unit
    leads = 2 if held == unit and groups == DEPTH and inner == 2 else 0
    costs = iter(COSTS if leads else ())

    def mate(g):
        return groups - 1 - g if leads else g

    ids = jnp.stack([lax.axis_index(a) for a in ("outer", "inner", "heads")]).astype(jnp.int32)
    token = jnp.zeros((8, DH), F32)
    doc_blocks = pltpu.with_memory_space_constraint(doc_ids.reshape(depth, SPAN), pltpu.HBM)
    label_shapes = [
        jax.ShapeDtypeStruct((2 * depth, DH), F32),
        jax.ShapeDtypeStruct((SPAN, SPAN), F32),
        jax.ShapeDtypeStruct((8, SPAN), F32),
    ]
    own_labels = docs_column = docs_row = labels = None

    levels = (outer - 1).bit_length()

    def state_pair(count):
        return jax.ShapeDtypeStruct((2, count, DH, DH), BF16)

    terms, prefixes, near, middle, far, local = {}, {}, {}, {}, {}, {}
    edge, arrays, carries = None, (queries, keys, values, out_grad), (carry_in, carry_cot)
    far_arrays, far_carries = (
        tuple(pltpu.with_memory_space_constraint(a, pltpu.HBM) for a in group) for group in (arrays, carries)
    )

    def exchange(own):
        return [own[0]] + [pairs(own[d], "inner", d) for d in range(1, inner)]

    def exchange_pieces(own):
        return [own[0]] + [[pairs(a, "inner", d) for a in own[d]] for d in range(1, inner)]

    def receive(units, kind, sent, perm):
        got = lax.ppermute(sent, "heads", perm)
        for n, u in enumerate(units):
            kind[u] = (got, n * part)
        return got

    def take_labels(arrays):
        nonlocal own_labels, docs_column, docs_row, labels
        own_labels, docs_column, docs_row = arrays
        labels = [own_labels] + [pairs(own_labels, "inner", d) for d in range(1, inner)]

    def make_labels():
        take_labels(run(
            label_kernel,
            (ids, doc_blocks),
            label_shapes,
            scratch=[pltpu.VMEM((depth, SPAN), jnp.int32), pltpu.SemaphoreType.DMA((1,))],
            specs=[SMEM, HBM],
        ))

    def run(*args, **options):
        nonlocal token
        token, outs = call(token, *args, cost=next(costs, 0), **options)
        return outs

    def make_lead_terms():
        places = tuple(range(leads))
        block = pltpu.VMEM((leads, SPAN, unit * DH), BF16)
        carry = pltpu.VMEM((unit, DH, DH), F32)
        own = run(
            functools.partial(
                lead_terms, factor, unit, part, places, tuple(mate(g) for g in places), outer, inner
            ),
            (ids, doc_blocks) + far_arrays + far_carries,
            [state_pair(part * leads)] * inner + [state_pair(unit)] + label_shapes,
            scratch=[pltpu.VMEM((depth, SPAN), jnp.int32)] + [block] * 4 + [carry, pltpu.SemaphoreType.DMA((leads + 1, 4))],
            specs=[SMEM] + [HBM] * 7,
        )
        take_labels(own[inner + 1 :])
        for g in places:
            terms[g] = [(a, g * part) for a in own[:inner]]
        return receive([(0, t) for t in range(inner)], near, own[inner], [(0, 1), (3, 2), (1, 0), (2, 3)])

    def make_terms(places):
        own = run(
            functools.partial(rest_terms, factor, unit, part, places, tuple(mate(g) for g in places)),
            (ids, docs_column) + far_arrays,
            [state_pair(part * len(places))] + [state_pair(part)] * (len(places) * (inner - 1)),
            scratch=[pltpu.VMEM((len(places), SPAN, unit * DH), BF16)] * 4
            + [pltpu.SemaphoreType.DMA((len(places), 4))],
            specs=[SMEM, VMEM] + [HBM] * 4,
        )
        own = [own[:1]] + [own[1 + d * len(places) :][: len(places)] for d in range(inner - 1)]
        for s, g in enumerate(places):
            terms[g] = [(own[0][0], s * part)] + [(a[s], 0) for a in own[1:]]
        return exchange_pieces(own)

    def make_sums(received, grouped):
        nonlocal token
        count = sum(a.shape[1] for a in received[0])
        sums = run(
            functools.partial(sum_kernel, tuple(len(a) for a in received), levels, grouped),
            (ids, *labels, *(a for pieces in received for a in pieces)),
            [jax.ShapeDtypeStruct((count * DH + LABELS, DH), BF16)] * levels,
        )
        return [pairs(sums[d.bit_length() - 1], "outer", d) for d in range(1, outer)]

    def make_prefixes(places, received, fans, grouped, lacked=None):
        nonlocal edge
        count = sum(a.shape[1] for a in received[0])
        given = run(
            functools.partial(
                prefix_kernel, factor, unit, part, places, tuple(mate(g) for g in places),
                tuple(len(a) for a in received), outer, grouped,
                lacked is not None,
            ),
            (ids, *carries, *([] if lacked is None else [lacked]), *labels, *(a for pieces in received for a in pieces), *fans),
            [state_pair(count)] * inner + [jax.ShapeDtypeStruct((8, DH), F32)],
        )
        edge = given[-1] if edge is None else edge
        given = exchange(given[:-1])
        for s, g in enumerate(places):
            prefixes[g] = [(a, s * part) for a in given]

    def move(near_units, far_units, across):
        units = list(near_units) + list(far_units)
        use_edges = not all(g < leads for g, _ in units)
        operands = [ids, own_labels] + ([edge] if use_edges else [])

        def plans_of(chosen, got):
            plans = []
            for u in chosen:
                g, t = u
                lead = g < leads
                array, off = terms[g][t]
                operands.append(array)
                if not lead:
                    operands.append(prefixes[g][t][0])
                if got is not None:
                    operands.append(got[u][0])
                plans.append((lead, off, 0 if lead else prefixes[g][t][1], None if got is None else got[u][1]))
            return plans

        near_plans = plans_of(near_units, None)
        far_plans = plans_of(far_units, near if across else middle)
        sent = run(
            functools.partial(hop_kernel, part, near_plans, far_plans, across, use_edges),
            operands,
            [state_pair(part * max(len(near_units), len(far_units)))],
        )
        return sent[0]

    def ends(near_units, far_units):
        perm = ([(0, 1), (3, 2)] if near_units else []) + ([(1, 0), (2, 3)] if far_units else [])
        got = receive(near_units, near, move(near_units, far_units, False), perm)
        for n, u in enumerate(far_units):
            far[u] = (got, n * part)

    def across(units):
        receive(units, middle, move([], units, True), [(1, 2), (2, 1)])

    def make_local(g):
        out = run(
            functools.partial(local_kernel, factor, g * unit, unit),
            (docs_column, docs_row) + arrays,
            [jax.ShapeDtypeStruct((4, unit, SPAN, DH), F32)],
            specs=[VMEM] * 6,
        )
        local[g] = out[0]

    out_shape = jax.ShapeDtypeStruct(queries.shape, BF16)
    results = ()

    def make_outputs(halves):
        nonlocal results
        operands, plans = (ids, own_labels, edge, docs_column) + arrays, []
        for which, g, t in halves:
            array, off = prefixes[g][t]
            kept = [kind[g, t] for kind in (near, middle, far)]
            heads = mate(g) if which else g
            plans.append((which, heads, t, g < leads, off) + tuple(at for _, at in kept))
            operands += (array,) + tuple(a for a, _ in kept)
        operands += tuple(local[mate(g) if which else g] for which, g, _ in halves)
        count = len(halves)
        results = run(
            functools.partial(output_kernel, unit, part, plans),
            operands + tuple(results),
            [out_shape] * 4,
            scratch=[
                pltpu.VMEM((count, part, DH, DH), BF16),
                pltpu.VMEM((count, 2, part, SPAN, DH), BF16),
                pltpu.SemaphoreType.DMA((count, 2, part)),
            ],
            aliases={len(operands) + i: i for i in range(len(results))},
            specs=[SMEM] + [VMEM] * (len(operands) - 1) + [HBM] * len(results),
            out_specs=[HBM] * 4,
        )

    def make_totals(g):
        operands, plans = [ids, own_labels], []
        for t in range(inner):
            array, off = terms[g][t]
            kept = [kind[g, t] for kind in (near, middle, far)]
            operands += [array] + [a for a, _ in kept]
            plans.append((off,) + tuple(at for _, at in kept))
        totals = run(
            functools.partial(lead_total_kernel, part, plans),
            operands,
            [state_pair(part)] * inner,
        )
        return exchange_pieces([[a] for a in totals])

    def chunk(n):
        return [(n, t) for t in range(inner)] if n < leads else [(g, n - leads) for g in range(leads, groups)]

    def halves_of(n):
        return [(which, g, t) for which in range(2) for g, t in chunk(n)]

    if leads:
        kept = {}

        def keep(name, make, *args):
            kept[name] = make(*args)

        def rest_sums():
            kept["fans"] = make_sums(kept["got"], False)

        def rest_prefixes():
            make_prefixes((2, 3), kept["got"], kept["fans"], False)

        def lead_sums(g):
            kept["fans", g] = make_sums(kept["totals", g], True)

        def lead_prefixes(g):
            make_prefixes((g,), kept["totals", g], kept["fans", g], True, kept["lacked"] if g else None)

        steps = {
            "K": lambda g: keep("lacked", make_lead_terms) if g == 0 else keep("got", make_terms, (2, 3)),
            "A": lambda g: rest_sums(),
            "B": lambda g: rest_prefixes(),
            "L": make_local,
            "E": lambda g: ends(chunk(g), []),
            "O": lambda g: across(chunk(g)),
            "F": lambda g: ends([], chunk(g)),
            "J": lambda g: ends(chunk(g), chunk(g - leads)),
            "M": lambda g: ends(chunk(g), chunk(0)),
            "T": lambda g: keep(("totals", g), make_totals, g),
            "S": lead_sums,
            "P": lead_prefixes,
            "W": lambda g: make_outputs(halves_of(g)),
        }
        for step in ORDER.split():
            steps[step[0]](int(step[1]))
    else:
        assert not leads
        make_labels()
        places = tuple(range(groups))
        got = make_terms(places)
        make_prefixes(places, got, make_sums(got, False), False)
        units = [(g, t) for g in range(groups) for t in range(inner)]
        lag = 4
        for k in range(len(units) + lag):
            ends(units[k : k + 1], units[k - lag : k - lag + 1] if k >= lag else [])
            if k < len(units):
                across([units[k]])
        for g in range(groups):
            make_local(g)
        for g, t in units:
            make_outputs([(0, g, t), (1, g, t)])
    return tuple(results)


def solution(mesh):
    tokens = P(("outer", "inner", "heads"), None)
    carry = P("heads", None, None)
    return jax.shard_map(
        shards,
        mesh=mesh,
        in_specs=(tokens,) * 4 + (P(("outer", "inner")), carry, carry),
        out_specs=(tokens,) * 4,
        check_vma=False,
    )
```

```python
import functools

import jax
import jax.numpy as jnp
from jax import lax
from jax.experimental import pallas as pl
from jax.experimental.pallas import tpu as pltpu
from jax.sharding import PartitionSpec as P

DH = 128
SPAN = 128
LABELS = 16
DEPTH = 4
F32 = jnp.float32
BF16 = jnp.bfloat16
VMEM = pl.BlockSpec(memory_space=pltpu.VMEM)
SMEM = pl.BlockSpec(memory_space=pltpu.SMEM)
HBM = pl.BlockSpec(memory_space=pltpu.HBM)
LIMIT = 24 * 1024 * 1024
COSTS = (0, 0, 0, 0, 0, 16, 0, 0, 0, 0, 0, 0, 0, 0, 0, 0, 8, 0, 0, 4, 0, 0, 0, 0, 4, 16, 0)
ORDER = (
    "K0 K1 A0 E1"
    " L3 O0 B0 L0"
    " O1 J2 L1 L2"
    " J3 O2 T0 S0"
    " O3 T1 F2 P0"
    " S1 W0 F3 P1"
    " W2 W1 W3"
)


def pairs(array, axis, distance):
    count = lax.axis_size(axis)
    return lax.ppermute(array, axis, [(i, i ^ distance) for i in range(count)])


def transposed_dot(a, b):
    return lax.dot_general(a, b, (((0,), (0,)), ((), ())), preferred_element_type=F32)


def dot_transposed(a, b):
    return lax.dot_general(a, b, (((1,), (1,)), ((), ())), preferred_element_type=F32)


def dot(a, b):
    return lax.dot_general(a, b, (((1,), (0,)), ((), ())), preferred_element_type=F32)


def flag(row):
    return jnp.where(row, 1.0, 0.0).astype(F32)


def call(token, kernel, operands, out_shape, cost=0, scratch=(), aliases=None, specs=None, out_specs=None):
    count, results = len(operands), len(out_shape)

    def ordered(*refs):
        kernel(*refs[:count], *refs[count + 1 : count + 1 + results], *refs[count + 2 + results :])

    *outs, token = pl.pallas_call(
        ordered,
        in_specs=list(specs or [SMEM] + [VMEM] * (count - 1)) + [VMEM],
        out_specs=list(out_specs or [VMEM] * results) + [VMEM],
        out_shape=list(out_shape) + [jax.ShapeDtypeStruct(token.shape, token.dtype)],
        scratch_shapes=list(scratch),
        input_output_aliases={**(aliases or {}), count: results},
        compiler_params=pltpu.CompilerParams(vmem_limit_bytes=LIMIT),
        cost_estimate=pl.CostEstimate(flops=int(cost * 1e9), bytes_accessed=0, transcendentals=0),
    )(*operands, token)
    return token, outs


def document_masks(docs):
    return docs == docs[0:1], docs == docs[SPAN - 1 : SPAN]


def columns(head):
    return pl.ds(pl.multiple_of(head * DH, DH), DH)


class Pieces:
    def __init__(self, refs):
        self.refs, self.each = refs, refs[0].shape[1]
        self.count = self.each * len(refs)

    def __getitem__(self, at):
        side, i = at
        return self.refs[i // self.each][side, i % self.each]


def in_pieces(refs, counts):
    starts = [sum(counts[:n]) for n in range(len(counts))]
    return [Pieces(refs[a : a + n]) for a, n in zip(starts, counts)]


def own_row(ref, at):
    return ref[pl.ds(at, 1), :]


def label_kernel(ids, docs_hbm, labels_ref, column_ref, row_ref, docs_ref, sem):
    copy = pltpu.make_async_copy(docs_hbm, docs_ref, sem.at[0])
    copy.start()
    copy.wait()
    write_labels(ids, docs_ref, labels_ref, column_ref, row_ref)


def write_labels(ids, docs_ref, labels_ref, column_ref, row_ref):
    docs = docs_ref[...]
    for k in range(DEPTH):
        row = docs[k : k + 1, :].astype(F32)
        labels_ref[k : k + 1, :] = jnp.broadcast_to(row[:, 0:1], (1, DH))
        labels_ref[DEPTH + k : DEPTH + k + 1, :] = jnp.broadcast_to(row[:, SPAN - 1 :], (1, DH))
    own = own_row(docs_ref, ids[2]).astype(F32)
    column_ref[...] = jnp.broadcast_to(own, (SPAN, SPAN)).T
    row_ref[...] = jnp.broadcast_to(own, (8, SPAN))


def fetch(pairs_of_refs, sems):
    copies = [pltpu.make_async_copy(source, target, sems.at[n]) for n, (source, target) in enumerate(pairs_of_refs)]
    for copy in copies:
        copy.start()
    return copies


def add_terms(factor, part, docs_ref, c, q_ref, k_ref, v_ref, g_ref, outs, offs, extra=None):
    in_first, in_last = document_masks(docs_ref[...])
    for t, (out, off) in enumerate(zip(outs, offs)):
        for i in range(part):
            at = columns((c ^ t) * part + i)
            forward = transposed_dot(jnp.where(in_last, k_ref[:, at], 0), v_ref[:, at]) * factor
            backward = transposed_dot(jnp.where(in_first, q_ref[:, at], 0), g_ref[:, at]) * factor
            if extra is not None:
                add_f, add_b = extra((c ^ t) * part + i)
                forward, backward = forward + add_f, backward + add_b
            out[0, off + i] = forward.astype(BF16)
            out[1, off + i] = backward.astype(BF16)


def group_columns(group, unit):
    return pl.ds(group * unit * DH, unit * DH)


def rest_terms(factor, unit, part, places, mates, ids, docs_ref, q_hbm, k_hbm, v_hbm, g_hbm, *refs):
    outs, (q_ref, k_ref, v_ref, g_ref, sems) = refs[:-5], refs[-5:]
    waiting = []
    for s, (g, mate) in enumerate(zip(places, mates)):
        forward, backward = group_columns(g, unit), group_columns(mate, unit)
        waiting.append(fetch(
            [
                (k_hbm.at[:, forward], k_ref.at[s]), (v_hbm.at[:, forward], v_ref.at[s]),
                (q_hbm.at[:, backward], q_ref.at[s]), (g_hbm.at[:, backward], g_ref.at[s]),
            ],
            sems.at[s],
        ))
    for s in range(len(places)):
        for copy in waiting[s]:
            copy.wait()
        add_terms(
            factor, part, docs_ref, ids[1], q_ref.at[s], k_ref.at[s], v_ref.at[s], g_ref.at[s],
            [outs[0]] + list(outs[1 + s :: len(places)]), [s * part] + [0] * (len(outs) // len(places)),
        )


def lead_terms(
    factor, unit, part, places, mates, outer, inner, ids, docs_hbm, q_hbm, k_hbm, v_hbm, g_hbm, carry_hbm, cot_hbm, *refs,
):
    outs, sent, labels, docs_ref, row_ref = refs[:inner], refs[inner], *refs[inner + 1 : inner + 4]
    blocks_ref, q_ref, k_ref, v_ref, g_ref, carry_ref, sems = refs[inner + 4 :]
    o, c, z = ids[0], ids[1], ids[2]
    _, side, at_end = place_of(ids)
    copy = pltpu.make_async_copy(docs_hbm, blocks_ref, sems.at[len(places), 0])
    copy.start()
    waiting = []
    for s, (g, mate) in enumerate(zip(places, mates)):
        forward, backward = group_columns(g, unit), group_columns(mate, unit)
        waiting.append(fetch(
            [
                (k_hbm.at[:, forward], k_ref.at[s]), (v_hbm.at[:, forward], v_ref.at[s]),
                (q_hbm.at[:, backward], q_ref.at[s]), (g_hbm.at[:, backward], g_ref.at[s]),
            ],
            sems.at[s],
        ))

    def carries(act):
        for which, source in enumerate((carry_hbm, cot_hbm)):

            @pl.when(side == which)
            def _():
                act(pltpu.make_async_copy(source, carry_ref, sems.at[len(places), 1 + which]))

    carries(lambda copy: copy.start())
    copy.wait()
    write_labels(ids, blocks_ref, labels, docs_ref, row_ref)
    first, last = own_row(labels, z), own_row(labels, DEPTH + z)
    newest = labels[2 * DEPTH - 1 : 2 * DEPTH, :]
    opens, closes = jnp.logical_and(o == 0, c == 0), jnp.logical_and(o == outer - 1, c == inner - 1)
    for s in range(len(places)):
        for copy in waiting[s]:
            copy.wait()
        if s == 0:
            carries(lambda copy: copy.wait())
        open_f = flag(jnp.logical_and(jnp.logical_and(opens, z == s), last == 0.0))
        close_b = flag(jnp.logical_and(jnp.logical_and(closes, z == DEPTH - 1 - s), first == newest)) * factor

        def extra(place):
            return open_f * carry_ref[place], close_b * carry_ref[place]

        add_terms(
            factor, part, docs_ref, c, q_ref.at[s], k_ref.at[s], v_ref.at[s], g_ref.at[s], outs, [s * part] * inner, extra
        )

    @pl.when(at_end)
    def _():
        for t, term in enumerate(outs):
            hop(side, edge_rows(z, labels, None), True, 0, part, term, None, 0, None, 0, sent, t * part)

    @pl.when(jnp.logical_not(at_end))
    def _():
        scale = jnp.where(side == 0, 1.0, factor)
        for i in range(unit):
            sent[0, i] = (carry_ref[i] * scale).astype(BF16)


def block_rows(labels, z, grouped):
    if grouped:
        return [l[0:1, :] for l in labels], [l[2 * DEPTH - 1 : 2 * DEPTH, :] for l in labels]
    return [own_row(l, z) for l in labels], [own_row(l, DEPTH + z) for l in labels]


def sum_kernel(counts, levels, grouped, ids, *refs):
    inner, behind = len(counts), len(counts) + sum(counts)
    labels, terms, outs = refs[:inner], in_pieces(refs[inner:behind], counts), refs[behind:]
    o, z = ids[0], ids[2]
    count = terms[0].count
    newest = functools.reduce(jnp.maximum, [l[2 * DEPTH - 1 : 2 * DEPTH, :] for l in labels])
    oldest = functools.reduce(jnp.minimum, [l[0:1, :] for l in labels])
    firsts, lasts = block_rows(labels, z, grouped)
    keep_f = [flag(l == newest) for l in lasts]
    keep_b = [flag(l == oldest) for l in firsts]
    low = [((o >> level) & 1) == 0 for level in range(levels)]
    for i in range(count):
        sum_f = sum(m * r[0, i].astype(F32) for m, r in zip(keep_f, terms)).astype(BF16)
        sum_b = sum(m * r[1, i].astype(F32) for m, r in zip(keep_b, terms)).astype(BF16)
        for chosen, out in zip(low, outs):
            out[i * DH : (i + 1) * DH, :] = jnp.where(chosen, sum_f, sum_b)
    rows = lax.broadcasted_iota(jnp.int32, (LABELS, DH), 0)
    marks = jnp.where(rows < LABELS // 2, jnp.broadcast_to(newest, (LABELS, DH)), jnp.broadcast_to(oldest, (LABELS, DH)))
    for out in outs:
        out[count * DH :, :] = marks.astype(BF16)


def prefix_kernel(factor, unit, part, places, mates, counts, outer, grouped, lacking, ids, carry_ref, cot_ref, *refs):
    lacked, refs = (refs[0], refs[1:]) if lacking else (None, refs)
    inner, behind = len(counts), len(counts) + sum(counts)
    labels, terms, fans = refs[:inner], in_pieces(refs[inner:behind], counts), refs[behind : behind + outer - 1]
    outs, edge_ref = refs[behind + outer - 1 : -1], refs[-1]
    o, c, z = ids[0], ids[1], ids[2]
    held = carry_ref.shape[0]
    count = terms[0].count
    group_first, group_last = block_rows(labels, z, True)
    block_first, block_last = block_rows(labels, z, grouped)
    marks = [r[count * DH : count * DH + LABELS, :].astype(F32) for r in fans]
    outer_last = [m[0:1] for m in marks]
    outer_first = [m[LABELS // 2 : LABELS // 2 + 1] for m in marks]
    newest = functools.reduce(jnp.maximum, group_last + outer_last)
    prior_base, later_base = jnp.zeros_like(newest), newest
    earlier = [(o ^ (d + 1)) < o for d in range(outer - 1)]
    for d in range(outer - 1):
        prior_base = jnp.maximum(prior_base, jnp.where(earlier[d], outer_last[d], 0.0))
        later_base = jnp.minimum(later_base, jnp.where(earlier[d], newest, outer_first[d]))
    priors, laters, plans = [], [], []
    for t in range(inner):
        prior, later = prior_base, later_base
        for d in range(inner):
            if d != t:
                before = (c ^ d) < (c ^ t)
                prior = jnp.maximum(prior, jnp.where(before, group_last[d], 0.0))
                later = jnp.minimum(later, jnp.where(before, newest, group_first[d]))
        forward = [(flag(jnp.logical_and(earlier[d], outer_last[d] == prior)), fans[d], None) for d in range(outer - 1)]
        backward = [
            (flag(jnp.logical_and(jnp.logical_not(earlier[d]), outer_first[d] == later)), fans[d], None)
            for d in range(outer - 1)
        ]
        for d in range(inner):
            if d != t:
                before = (c ^ d) < (c ^ t)
                forward.append((flag(jnp.logical_and(before, block_last[d] == prior)), terms[d], 0))
                backward.append((flag(jnp.logical_and(jnp.logical_not(before), block_first[d] == later)), terms[d], 1))
        take_f, take_b = prior == 0.0, later == newest
        if grouped:
            take_f = jnp.logical_and(take_f, jnp.logical_and(o == 0, (c ^ t) == 0))
            take_b = jnp.logical_and(take_b, jnp.logical_and(o == outer - 1, (c ^ t) == inner - 1))
        priors.append(prior)
        laters.append(later)
        plans.append((forward, backward, flag(take_f), flag(take_b)))
    for s, (g, mate) in enumerate(zip(places, mates)):
        for i in range(part):
            at = s * part + i

            def carried(head, ref):
                place = head - z * held
                mine = jnp.logical_and(place >= 0, place < held)
                return jnp.where(mine, ref[jnp.clip(place, 0, held - 1)], 0.0)

            carries = [
                carried(g * unit + c * part + i, carry_ref),
                carried(mate * unit + c * part + i, cot_ref) * factor,
            ]
            if lacking:
                more = lacked[0, c * part + i].astype(F32)
                carries[0] = carries[0] + jnp.where(z == 0, more, 0.0)
                carries[1] = carries[1] + jnp.where(z == DEPTH - 1, more, 0.0)

            def value(ref, side):
                return (ref[at * DH : (at + 1) * DH, :] if side is None else ref[side, at]).astype(F32)

            for t, out in enumerate(outs):
                for side in range(2):
                    amount = plans[t][2 + side] * carries[side]
                    for weight, ref, which in plans[t][side]:
                        amount = amount + weight * value(ref, which)
                    out[side, at] = amount.astype(BF16)
    edge_ref[0:1, :] = priors[0]
    edge_ref[1:2, :] = laters[0]
    edge_ref[2:8, :] = jnp.broadcast_to(newest, (6, DH))


def place_of(ids):
    z = ids[2]
    side = jnp.where(z >= DEPTH // 2, 1, 0)
    return z, side, jnp.logical_or(z == 0, z == DEPTH - 1)


def edge_rows(z, labels, edges):
    first, last = own_row(labels, z), own_row(labels, DEPTH + z)
    last_before = own_row(labels, DEPTH + jnp.maximum(z - 1, 0))
    first_after = own_row(labels, jnp.minimum(z + 1, DEPTH - 1))
    final_f, final_b = labels[2 * DEPTH - 1 : 2 * DEPTH, :], labels[0:1, :]
    prior = later = final_f
    if edges is not None:
        prior, later = edges[0:1, :], edges[1:2, :]
    return (last, last_before, final_f, first, prior), (first, first_after, final_b, last, later)


def pick(which, rows):
    return [jnp.where(which == 0, a, b) for a, b in zip(*rows)]


def hop(side, rows, lead, off, part, term_ref, prefix_ref, prefix_off, got_ref, got_off, out, out_off):
    own, neighbour, _, _, prior = pick(side, rows)
    other, _, final, _, _ = pick(1 - side, rows)
    join, keep, counts = flag(prior == own), flag(neighbour == own), flag(other == final)
    for i in range(part):
        state = term_ref[side, off + i].astype(F32)
        if lead:
            rest = counts * term_ref[1 - side, off + i].astype(F32)
        else:
            state = state + join * prefix_ref[side, prefix_off + i].astype(F32)
            rest = prefix_ref[1 - side, prefix_off + i].astype(F32)
        if got_ref is not None:
            state = state + keep * got_ref[0, got_off + i].astype(F32)
            rest = rest + got_ref[1, got_off + i].astype(F32)
        out[0, out_off + i] = state.astype(BF16)
        out[1, out_off + i] = rest.astype(BF16)


def hop_kernel(part, near, far, across, has_edges, ids, labels, *refs):
    z, side, at_end = place_of(ids)
    out, refs = refs[-1], list(refs[:-1])
    rows = edge_rows(z, labels, refs.pop(0) if has_edges else None)

    def take(plans):
        return [(plan, refs.pop(0), None if plan[0] else refs.pop(0), refs.pop(0) if plan[3] is not None else None) for plan in plans]

    near, far = take(near), take(far)

    def write(side, entries):
        for n, ((lead, off, prefix_off, got_off), term, prefix, got) in enumerate(entries):
            hop(side, rows, lead, off, part, term, prefix, prefix_off, got, got_off, out, n * part)

    if near:
        pl.when(at_end)(lambda: write(side, near))
    if far:
        pl.when(jnp.logical_not(at_end))(lambda: write(side if across else 1 - side, far))


def lead_total_kernel(part, plans, ids, labels, *refs):
    z, side, at_end = place_of(ids)
    rows = edge_rows(z, labels, None)
    for t, (off, near_off, middle_off, far_off) in enumerate(plans):
        term, near, middle, far = refs[4 * t : 4 * t + 4]
        out = refs[4 * len(plans) + t]

        def total(which, over, over_off, rest, rest_off):
            own, neighbour, final, _, _ = pick(which, rows)
            counts, come = flag(own == final), flag(neighbour == final)
            for i in range(part):
                value = counts * term[which, off + i].astype(F32)
                if over is not None:
                    value = value + come * over[0, over_off + i].astype(F32)
                if rest is not None:
                    value = value + rest[1, rest_off + i].astype(F32)
                out[which, i] = value.astype(BF16)

        @pl.when(at_end)
        def _():
            total(side, None, 0, far, far_off)
            total(1 - side, far, far_off, None, 0)

        @pl.when(jnp.logical_not(at_end))
        def _():
            total(side, near, near_off, middle, middle_off)
            total(1 - side, middle, middle_off, near, near_off)


def local_kernel(factor, base, count, docs_ref, row_ref, q_ref, k_ref, v_ref, g_ref, out):
    docs = docs_ref[...]
    places = lax.broadcasted_iota(jnp.int32, (SPAN, SPAN), 0)
    others = lax.broadcasted_iota(jnp.int32, (SPAN, SPAN), 1)
    allowed = jnp.logical_and(others <= places, docs == row_ref[0:1])
    for i in range(count):
        at = slice((base + i) * DH, (base + i + 1) * DH)
        q, k, v, g = q_ref[:, at], k_ref[:, at], v_ref[:, at], g_ref[:, at]
        scores = jnp.where(allowed, dot_transposed(q, k) * factor, 0.0).astype(BF16)
        grad_scores = jnp.where(allowed, dot_transposed(g, v) * factor, 0.0).astype(BF16)
        out[0, i] = dot(scores, v)
        out[1, i] = dot(grad_scores, k)
        out[2, i] = transposed_dot(grad_scores, q)
        out[3, i] = transposed_dot(scores, g)


def output_kernel(unit, part, plans, ids, labels, edges, docs_ref, q_ref, k_ref, v_ref, g_ref, *refs):
    count = len(plans)
    sources, locals_ = refs[: 4 * count], refs[4 * count : 5 * count]
    outs, (states, held, sems) = refs[-7:-3], refs[-3:]
    c = ids[1]
    z, side, at_end = place_of(ids)
    rows = edge_rows(z, labels, edges)

    def make_states(ends, side):
        for n, (which, _, _, lead, off, near_off, middle_off, far_off) in enumerate(plans):
            prefix, near, middle, far = sources[4 * n : 4 * n + 4]
            _, neighbour, _, target, prior = rows[which]
            reach, come = flag(prior == target), flag(neighbour == target)
            if ends:
                over, rest = (None, (far, far_off)) if side == which else ((far, far_off), None)
            elif side == which:
                over, rest = (near, near_off), (middle, middle_off)
            else:
                over, rest = (middle, middle_off), (near, near_off)
            for i in range(part):
                value = reach * prefix[which, off + i].astype(F32)
                if over is not None:
                    value = value + come * over[0][0, over[1] + i].astype(F32)
                if rest is not None and not lead:
                    value = value + reach * rest[0][1, rest[1] + i].astype(F32)
                states[n, i] = value.astype(BF16)

    for ends in (True, False):
        for which in range(2):
            here = jnp.logical_and(at_end if ends else jnp.logical_not(at_end), side == which)
            pl.when(here)(functools.partial(make_states, ends, which))

    in_first, in_last = document_masks(docs_ref[...])
    copies = []
    for n, (which, group, turn, *_) in enumerate(plans):
        place = (c ^ turn) * part
        for i in range(part):
            at = columns(group * unit + place + i)
            state = states[n, i]
            if which == 0:
                results = (
                    dot(jnp.where(in_first, q_ref[:, at], 0), state),
                    dot_transposed(jnp.where(in_first, g_ref[:, at], 0), state),
                )
            else:
                results = (
                    dot_transposed(jnp.where(in_last, v_ref[:, at], 0), state),
                    dot(jnp.where(in_last, k_ref[:, at], 0), state),
                )
            for m, result in enumerate(results):
                held[n, m, i] = (locals_[n][2 * which + m, place + i] + result).astype(BF16)
                copy = pltpu.make_async_copy(held.at[n, m, i], outs[2 * which + m].at[:, at], sems.at[n, m, i])
                copy.start()
                copies.append(copy)
    for copy in copies:
        copy.wait()


def shards(queries, keys, values, out_grad, doc_ids, carry_in, carry_cot):
    outer, inner, depth = (lax.axis_size(a) for a in ("outer", "inner", "heads"))
    assert depth == DEPTH
    tokens_all = doc_ids.shape[0] * outer * inner
    factor = float(DH * (tokens_all // 2)) ** (-0.5)
    head_count = queries.shape[1] // DH
    held = carry_in.shape[0]
    part = min(4, head_count // inner)
    unit = part * inner
    groups = head_count // unit
    leads = 2 if held == unit and groups == DEPTH and inner == 2 else 0
    costs = iter(COSTS if leads else ())

    def mate(g):
        return groups - 1 - g if leads else g

    ids = jnp.stack([lax.axis_index(a) for a in ("outer", "inner", "heads")]).astype(jnp.int32)
    token = jnp.zeros((8, DH), F32)
    doc_blocks = pltpu.with_memory_space_constraint(doc_ids.reshape(depth, SPAN), pltpu.HBM)
    label_shapes = [
        jax.ShapeDtypeStruct((2 * depth, DH), F32),
        jax.ShapeDtypeStruct((SPAN, SPAN), F32),
        jax.ShapeDtypeStruct((8, SPAN), F32),
    ]
    own_labels = docs_column = docs_row = labels = None

    levels = (outer - 1).bit_length()

    def state_pair(count):
        return jax.ShapeDtypeStruct((2, count, DH, DH), BF16)

    terms, prefixes, near, middle, far, local = {}, {}, {}, {}, {}, {}
    edge, arrays, carries = None, (queries, keys, values, out_grad), (carry_in, carry_cot)
    far_arrays, far_carries = (
        tuple(pltpu.with_memory_space_constraint(a, pltpu.HBM) for a in group) for group in (arrays, carries)
    )

    def exchange(own):
        return [own[0]] + [pairs(own[d], "inner", d) for d in range(1, inner)]

    def exchange_pieces(own):
        return [own[0]] + [[pairs(a, "inner", d) for a in own[d]] for d in range(1, inner)]

    def receive(units, kind, sent, perm):
        got = lax.ppermute(sent, "heads", perm)
        for n, u in enumerate(units):
            kind[u] = (got, n * part)
        return got

    def take_labels(arrays):
        nonlocal own_labels, docs_column, docs_row, labels
        own_labels, docs_column, docs_row = arrays
        labels = [own_labels] + [pairs(own_labels, "inner", d) for d in range(1, inner)]

    def make_labels():
        take_labels(run(
            label_kernel,
            (ids, doc_blocks),
            label_shapes,
            scratch=[pltpu.VMEM((depth, SPAN), jnp.int32), pltpu.SemaphoreType.DMA((1,))],
            specs=[SMEM, HBM],
        ))

    def run(*args, **options):
        nonlocal token
        token, outs = call(token, *args, cost=next(costs, 0), **options)
        return outs

    def make_lead_terms():
        places = tuple(range(leads))
        block = pltpu.VMEM((leads, SPAN, unit * DH), BF16)
        carry = pltpu.VMEM((unit, DH, DH), F32)
        own = run(
            functools.partial(
                lead_terms, factor, unit, part, places, tuple(mate(g) for g in places), outer, inner
            ),
            (ids, doc_blocks) + far_arrays + far_carries,
            [state_pair(part * leads)] * inner + [state_pair(unit)] + label_shapes,
            scratch=[pltpu.VMEM((depth, SPAN), jnp.int32)] + [block] * 4 + [carry, pltpu.SemaphoreType.DMA((leads + 1, 4))],
            specs=[SMEM] + [HBM] * 7,
        )
        take_labels(own[inner + 1 :])
        for g in places:
            terms[g] = [(a, g * part) for a in own[:inner]]
        return receive([(0, t) for t in range(inner)], near, own[inner], [(0, 1), (3, 2), (1, 0), (2, 3)])

    def make_terms(places):
        own = run(
            functools.partial(rest_terms, factor, unit, part, places, tuple(mate(g) for g in places)),
            (ids, docs_column) + far_arrays,
            [state_pair(part * len(places))] + [state_pair(part)] * (len(places) * (inner - 1)),
            scratch=[pltpu.VMEM((len(places), SPAN, unit * DH), BF16)] * 4
            + [pltpu.SemaphoreType.DMA((len(places), 4))],
            specs=[SMEM, VMEM] + [HBM] * 4,
        )
        own = [own[:1]] + [own[1 + d * len(places) :][: len(places)] for d in range(inner - 1)]
        for s, g in enumerate(places):
            terms[g] = [(own[0][0], s * part)] + [(a[s], 0) for a in own[1:]]
        return exchange_pieces(own)

    def make_sums(received, grouped):
        nonlocal token
        count = sum(a.shape[1] for a in received[0])
        sums = run(
            functools.partial(sum_kernel, tuple(len(a) for a in received), levels, grouped),
            (ids, *labels, *(a for pieces in received for a in pieces)),
            [jax.ShapeDtypeStruct((count * DH + LABELS, DH), BF16)] * levels,
        )
        return [pairs(sums[d.bit_length() - 1], "outer", d) for d in range(1, outer)]

    def make_prefixes(places, received, fans, grouped, lacked=None):
        nonlocal edge
        count = sum(a.shape[1] for a in received[0])
        given = run(
            functools.partial(
                prefix_kernel, factor, unit, part, places, tuple(mate(g) for g in places),
                tuple(len(a) for a in received), outer, grouped,
                lacked is not None,
            ),
            (ids, *carries, *([] if lacked is None else [lacked]), *labels, *(a for pieces in received for a in pieces), *fans),
            [state_pair(count)] * inner + [jax.ShapeDtypeStruct((8, DH), F32)],
        )
        edge = given[-1] if edge is None else edge
        given = exchange(given[:-1])
        for s, g in enumerate(places):
            prefixes[g] = [(a, s * part) for a in given]

    def move(near_units, far_units, across):
        units = list(near_units) + list(far_units)
        use_edges = not all(g < leads for g, _ in units)
        operands = [ids, own_labels] + ([edge] if use_edges else [])

        def plans_of(chosen, got):
            plans = []
            for u in chosen:
                g, t = u
                lead = g < leads
                array, off = terms[g][t]
                operands.append(array)
                if not lead:
                    operands.append(prefixes[g][t][0])
                if got is not None:
                    operands.append(got[u][0])
                plans.append((lead, off, 0 if lead else prefixes[g][t][1], None if got is None else got[u][1]))
            return plans

        near_plans = plans_of(near_units, None)
        far_plans = plans_of(far_units, near if across else middle)
        sent = run(
            functools.partial(hop_kernel, part, near_plans, far_plans, across, use_edges),
            operands,
            [state_pair(part * max(len(near_units), len(far_units)))],
        )
        return sent[0]

    def ends(near_units, far_units):
        perm = ([(0, 1), (3, 2)] if near_units else []) + ([(1, 0), (2, 3)] if far_units else [])
        got = receive(near_units, near, move(near_units, far_units, False), perm)
        for n, u in enumerate(far_units):
            far[u] = (got, n * part)

    def across(units):
        receive(units, middle, move([], units, True), [(1, 2), (2, 1)])

    def make_local(g):
        out = run(
            functools.partial(local_kernel, factor, g * unit, unit),
            (docs_column, docs_row) + arrays,
            [jax.ShapeDtypeStruct((4, unit, SPAN, DH), F32)],
            specs=[VMEM] * 6,
        )
        local[g] = out[0]

    out_shape = jax.ShapeDtypeStruct(queries.shape, BF16)
    results = ()

    def make_outputs(halves):
        nonlocal results
        operands, plans = (ids, own_labels, edge, docs_column) + arrays, []
        for which, g, t in halves:
            array, off = prefixes[g][t]
            kept = [kind[g, t] for kind in (near, middle, far)]
            heads = mate(g) if which else g
            plans.append((which, heads, t, g < leads, off) + tuple(at for _, at in kept))
            operands += (array,) + tuple(a for a, _ in kept)
        operands += tuple(local[mate(g) if which else g] for which, g, _ in halves)
        count = len(halves)
        results = run(
            functools.partial(output_kernel, unit, part, plans),
            operands + tuple(results),
            [out_shape] * 4,
            scratch=[
                pltpu.VMEM((count, part, DH, DH), BF16),
                pltpu.VMEM((count, 2, part, SPAN, DH), BF16),
                pltpu.SemaphoreType.DMA((count, 2, part)),
            ],
            aliases={len(operands) + i: i for i in range(len(results))},
            specs=[SMEM] + [VMEM] * (len(operands) - 1) + [HBM] * len(results),
            out_specs=[HBM] * 4,
        )

    def make_totals(g):
        operands, plans = [ids, own_labels], []
        for t in range(inner):
            array, off = terms[g][t]
            kept = [kind[g, t] for kind in (near, middle, far)]
            operands += [array] + [a for a, _ in kept]
            plans.append((off,) + tuple(at for _, at in kept))
        totals = run(
            functools.partial(lead_total_kernel, part, plans),
            operands,
            [state_pair(part)] * inner,
        )
        return exchange_pieces([[a] for a in totals])

    def chunk(n):
        return [(n, t) for t in range(inner)] if n < leads else [(g, n - leads) for g in range(leads, groups)]

    def halves_of(n):
        return [(which, g, t) for which in range(2) for g, t in chunk(n)]

    if leads:
        kept = {}

        def keep(name, make, *args):
            kept[name] = make(*args)

        def rest_sums():
            kept["fans"] = make_sums(kept["got"], False)

        def rest_prefixes():
            make_prefixes((2, 3), kept["got"], kept["fans"], False)

        def lead_sums(g):
            kept["fans", g] = make_sums(kept["totals", g], True)

        def lead_prefixes(g):
            make_prefixes((g,), kept["totals", g], kept["fans", g], True, kept["lacked"] if g else None)

        steps = {
            "K": lambda g: keep("lacked", make_lead_terms) if g == 0 else keep("got", make_terms, (2, 3)),
            "A": lambda g: rest_sums(),
            "B": lambda g: rest_prefixes(),
            "L": make_local,
            "E": lambda g: ends(chunk(g), []),
            "O": lambda g: across(chunk(g)),
            "F": lambda g: ends([], chunk(g)),
            "J": lambda g: ends(chunk(g), chunk(g - leads)),
            "M": lambda g: ends(chunk(g), chunk(0)),
            "T": lambda g: keep(("totals", g), make_totals, g),
            "S": lead_sums,
            "P": lead_prefixes,
            "W": lambda g: make_outputs(halves_of(g)),
        }
        for step in ORDER.split():
            steps[step[0]](int(step[1]))
    else:
        assert not leads
        make_labels()
        places = tuple(range(groups))
        got = make_terms(places)
        make_prefixes(places, got, make_sums(got, False), False)
        units = [(g, t) for g in range(groups) for t in range(inner)]
        lag = 4
        for k in range(len(units) + lag):
            ends(units[k : k + 1], units[k - lag : k - lag + 1] if k >= lag else [])
            if k < len(units):
                across([units[k]])
        for g in range(groups):
            make_local(g)
        for g, t in units:
            make_outputs([(0, g, t), (1, g, t)])
    return tuple(results)


def solution(mesh):
    tokens = P(("outer", "inner", "heads"), None)
    carry = P("heads", None, None)
    return jax.shard_map(
        shards,
        mesh=mesh,
        in_specs=(tokens,) * 4 + (P(("outer", "inner")), carry, carry),
        out_specs=(tokens,) * 4,
        check_vma=False,
    )
```

```python
import functools

import jax
import jax.numpy as jnp
from jax import lax
from jax.experimental import pallas as pl
from jax.experimental.pallas import tpu as pltpu
from jax.sharding import PartitionSpec as P

DH = 128
SPAN = 128
LABELS = 16
DEPTH = 4
F32 = jnp.float32
BF16 = jnp.bfloat16
VMEM = pl.BlockSpec(memory_space=pltpu.VMEM)
SMEM = pl.BlockSpec(memory_space=pltpu.SMEM)
HBM = pl.BlockSpec(memory_space=pltpu.HBM)
LIMIT = 24 * 1024 * 1024
COSTS = (0, 0, 0, 0, 0, 16, 0, 0, 0, 0, 0, 0, 0, 0, 0, 0, 8, 0, 0, 4, 0, 0, 0, 0, 0, 0, 0)
ORDER = (
    "K0 K1 A0 E1",
    "L3 O0 B0 L0",
    "O1 J2 L1 L2",
    "J3 O2 T0 S0",
    "O3 T1 F2 P0",
    "S1 F3 W0 W2",
    "P1 W1 W3",
)


def pairs(array, axis, distance):
    count = lax.axis_size(axis)
    return lax.ppermute(array, axis, [(i, i ^ distance) for i in range(count)])


def transposed_dot(a, b):
    return lax.dot_general(a, b, (((0,), (0,)), ((), ())), preferred_element_type=F32)


def dot_transposed(a, b):
    return lax.dot_general(a, b, (((1,), (1,)), ((), ())), preferred_element_type=F32)


def dot(a, b):
    return lax.dot_general(a, b, (((1,), (0,)), ((), ())), preferred_element_type=F32)


def flag(row):
    return jnp.where(row, 1.0, 0.0).astype(F32)


def call(token, kernel, operands, out_shape, cost=0, scratch=(), aliases=None, specs=None, out_specs=None):
    count, results = len(operands), len(out_shape)

    def ordered(*refs):
        kernel(*refs[:count], *refs[count + 1 : count + 1 + results], *refs[count + 2 + results :])

    *outs, token = pl.pallas_call(
        ordered,
        in_specs=list(specs or [SMEM] + [VMEM] * (count - 1)) + [VMEM],
        out_specs=list(out_specs or [VMEM] * results) + [VMEM],
        out_shape=list(out_shape) + [jax.ShapeDtypeStruct(token.shape, token.dtype)],
        scratch_shapes=list(scratch),
        input_output_aliases={**(aliases or {}), count: results},
        compiler_params=pltpu.CompilerParams(vmem_limit_bytes=LIMIT),
        cost_estimate=pl.CostEstimate(flops=int(cost * 1e9), bytes_accessed=0, transcendentals=0),
    )(*operands, token)
    return token, outs


def document_masks(docs):
    return docs == docs[0:1], docs == docs[SPAN - 1 : SPAN]


def columns(head):
    return pl.ds(pl.multiple_of(head * DH, DH), DH)


class Pieces:
    def __init__(self, refs):
        self.refs, self.each = refs, refs[0].shape[1]
        self.count = self.each * len(refs)

    def __getitem__(self, at):
        side, i = at
        return self.refs[i // self.each][side, i % self.each]


def in_pieces(refs, counts):
    starts = [sum(counts[:n]) for n in range(len(counts))]
    return [Pieces(refs[a : a + n]) for a, n in zip(starts, counts)]


def own_row(ref, at):
    return ref[pl.ds(at, 1), :]


def label_kernel(ids, docs_hbm, labels_ref, column_ref, row_ref, docs_ref, sem):
    copy = pltpu.make_async_copy(docs_hbm, docs_ref, sem.at[0])
    copy.start()
    copy.wait()
    write_labels(ids, docs_ref, labels_ref, column_ref, row_ref)


def write_labels(ids, docs_ref, labels_ref, column_ref, row_ref):
    docs = docs_ref[...]
    for k in range(DEPTH):
        row = docs[k : k + 1, :].astype(F32)
        labels_ref[k : k + 1, :] = jnp.broadcast_to(row[:, 0:1], (1, DH))
        labels_ref[DEPTH + k : DEPTH + k + 1, :] = jnp.broadcast_to(row[:, SPAN - 1 :], (1, DH))
    own = own_row(docs_ref, ids[2]).astype(F32)
    column_ref[...] = jnp.broadcast_to(own, (SPAN, SPAN)).T
    row_ref[...] = jnp.broadcast_to(own, (8, SPAN))


def fetch(pairs_of_refs, sems):
    copies = [pltpu.make_async_copy(source, target, sems.at[n]) for n, (source, target) in enumerate(pairs_of_refs)]
    for copy in copies:
        copy.start()
    return copies


def add_terms(factor, part, docs_ref, c, q_ref, k_ref, v_ref, g_ref, outs, offs, extra=None):
    in_first, in_last = document_masks(docs_ref[...])
    for t, (out, off) in enumerate(zip(outs, offs)):
        for i in range(part):
            at = columns((c ^ t) * part + i)
            forward = transposed_dot(jnp.where(in_last, k_ref[:, at], 0), v_ref[:, at]) * factor
            backward = transposed_dot(jnp.where(in_first, q_ref[:, at], 0), g_ref[:, at]) * factor
            if extra is not None:
                add_f, add_b = extra((c ^ t) * part + i)
                forward, backward = forward + add_f, backward + add_b
            out[0, off + i] = forward.astype(BF16)
            out[1, off + i] = backward.astype(BF16)


def group_columns(group, unit):
    return pl.ds(group * unit * DH, unit * DH)


def rest_terms(factor, unit, part, places, mates, ids, docs_ref, q_hbm, k_hbm, v_hbm, g_hbm, *refs):
    outs, (q_ref, k_ref, v_ref, g_ref, sems) = refs[:-5], refs[-5:]
    waiting = []
    for s, (g, mate) in enumerate(zip(places, mates)):
        forward, backward = group_columns(g, unit), group_columns(mate, unit)
        waiting.append(fetch(
            [
                (k_hbm.at[:, forward], k_ref.at[s]), (v_hbm.at[:, forward], v_ref.at[s]),
                (q_hbm.at[:, backward], q_ref.at[s]), (g_hbm.at[:, backward], g_ref.at[s]),
            ],
            sems.at[s],
        ))
    for s in range(len(places)):
        for copy in waiting[s]:
            copy.wait()
        add_terms(
            factor, part, docs_ref, ids[1], q_ref.at[s], k_ref.at[s], v_ref.at[s], g_ref.at[s],
            [outs[0]] + list(outs[1 + s :: len(places)]), [s * part] + [0] * (len(outs) // len(places)),
        )


def lead_terms(
    factor, unit, part, places, mates, outer, inner, ids, docs_hbm, q_hbm, k_hbm, v_hbm, g_hbm, carry_hbm, cot_hbm, *refs,
):
    outs, sent, labels, docs_ref, row_ref = refs[:inner], refs[inner], *refs[inner + 1 : inner + 4]
    blocks_ref, q_ref, k_ref, v_ref, g_ref, carry_ref, sems = refs[inner + 4 :]
    o, c, z = ids[0], ids[1], ids[2]
    _, side, at_end = place_of(ids)
    copy = pltpu.make_async_copy(docs_hbm, blocks_ref, sems.at[len(places), 0])
    copy.start()
    waiting = []
    for s, (g, mate) in enumerate(zip(places, mates)):
        forward, backward = group_columns(g, unit), group_columns(mate, unit)
        waiting.append(fetch(
            [
                (k_hbm.at[:, forward], k_ref.at[s]), (v_hbm.at[:, forward], v_ref.at[s]),
                (q_hbm.at[:, backward], q_ref.at[s]), (g_hbm.at[:, backward], g_ref.at[s]),
            ],
            sems.at[s],
        ))

    def carries(act):
        for which, source in enumerate((carry_hbm, cot_hbm)):

            @pl.when(side == which)
            def _():
                act(pltpu.make_async_copy(source, carry_ref, sems.at[len(places), 1 + which]))

    carries(lambda copy: copy.start())
    copy.wait()
    write_labels(ids, blocks_ref, labels, docs_ref, row_ref)
    first, last = own_row(labels, z), own_row(labels, DEPTH + z)
    newest = labels[2 * DEPTH - 1 : 2 * DEPTH, :]
    opens, closes = jnp.logical_and(o == 0, c == 0), jnp.logical_and(o == outer - 1, c == inner - 1)
    for s in range(len(places)):
        for copy in waiting[s]:
            copy.wait()
        if s == 0:
            carries(lambda copy: copy.wait())
        open_f = flag(jnp.logical_and(jnp.logical_and(opens, z == s), last == 0.0))
        close_b = flag(jnp.logical_and(jnp.logical_and(closes, z == DEPTH - 1 - s), first == newest)) * factor

        def extra(place):
            return open_f * carry_ref[place], close_b * carry_ref[place]

        add_terms(
            factor, part, docs_ref, c, q_ref.at[s], k_ref.at[s], v_ref.at[s], g_ref.at[s], outs, [s * part] * inner, extra
        )

    @pl.when(at_end)
    def _():
        for t, term in enumerate(outs):
            hop(side, edge_rows(z, labels, None), True, 0, part, term, None, 0, None, 0, sent, t * part)

    @pl.when(jnp.logical_not(at_end))
    def _():
        scale = jnp.where(side == 0, 1.0, factor)
        for i in range(unit):
            sent[0, i] = (carry_ref[i] * scale).astype(BF16)


def block_rows(labels, z, grouped):
    if grouped:
        return [l[0:1, :] for l in labels], [l[2 * DEPTH - 1 : 2 * DEPTH, :] for l in labels]
    return [own_row(l, z) for l in labels], [own_row(l, DEPTH + z) for l in labels]


def sum_kernel(counts, levels, grouped, ids, *refs):
    inner, behind = len(counts), len(counts) + sum(counts)
    labels, terms, outs = refs[:inner], in_pieces(refs[inner:behind], counts), refs[behind:]
    o, z = ids[0], ids[2]
    count = terms[0].count
    newest = functools.reduce(jnp.maximum, [l[2 * DEPTH - 1 : 2 * DEPTH, :] for l in labels])
    oldest = functools.reduce(jnp.minimum, [l[0:1, :] for l in labels])
    firsts, lasts = block_rows(labels, z, grouped)
    keep_f = [flag(l == newest) for l in lasts]
    keep_b = [flag(l == oldest) for l in firsts]
    low = [((o >> level) & 1) == 0 for level in range(levels)]
    for i in range(count):
        sum_f = sum(m * r[0, i].astype(F32) for m, r in zip(keep_f, terms)).astype(BF16)
        sum_b = sum(m * r[1, i].astype(F32) for m, r in zip(keep_b, terms)).astype(BF16)
        for chosen, out in zip(low, outs):
            out[i * DH : (i + 1) * DH, :] = jnp.where(chosen, sum_f, sum_b)
    rows = lax.broadcasted_iota(jnp.int32, (LABELS, DH), 0)
    marks = jnp.where(rows < LABELS // 2, jnp.broadcast_to(newest, (LABELS, DH)), jnp.broadcast_to(oldest, (LABELS, DH)))
    for out in outs:
        out[count * DH :, :] = marks.astype(BF16)


def prefix_kernel(factor, unit, part, places, mates, counts, outer, grouped, lacking, ids, carry_ref, cot_ref, *refs):
    lacked, refs = (refs[0], refs[1:]) if lacking else (None, refs)
    inner, behind = len(counts), len(counts) + sum(counts)
    labels, terms, fans = refs[:inner], in_pieces(refs[inner:behind], counts), refs[behind : behind + outer - 1]
    outs, edge_ref = refs[behind + outer - 1 : -1], refs[-1]
    o, c, z = ids[0], ids[1], ids[2]
    held = carry_ref.shape[0]
    count = terms[0].count
    group_first, group_last = block_rows(labels, z, True)
    block_first, block_last = block_rows(labels, z, grouped)
    marks = [r[count * DH : count * DH + LABELS, :].astype(F32) for r in fans]
    outer_last = [m[0:1] for m in marks]
    outer_first = [m[LABELS // 2 : LABELS // 2 + 1] for m in marks]
    newest = functools.reduce(jnp.maximum, group_last + outer_last)
    prior_base, later_base = jnp.zeros_like(newest), newest
    earlier = [(o ^ (d + 1)) < o for d in range(outer - 1)]
    for d in range(outer - 1):
        prior_base = jnp.maximum(prior_base, jnp.where(earlier[d], outer_last[d], 0.0))
        later_base = jnp.minimum(later_base, jnp.where(earlier[d], newest, outer_first[d]))
    priors, laters, plans = [], [], []
    for t in range(inner):
        prior, later = prior_base, later_base
        for d in range(inner):
            if d != t:
                before = (c ^ d) < (c ^ t)
                prior = jnp.maximum(prior, jnp.where(before, group_last[d], 0.0))
                later = jnp.minimum(later, jnp.where(before, newest, group_first[d]))
        forward = [(flag(jnp.logical_and(earlier[d], outer_last[d] == prior)), fans[d], None) for d in range(outer - 1)]
        backward = [
            (flag(jnp.logical_and(jnp.logical_not(earlier[d]), outer_first[d] == later)), fans[d], None)
            for d in range(outer - 1)
        ]
        for d in range(inner):
            if d != t:
                before = (c ^ d) < (c ^ t)
                forward.append((flag(jnp.logical_and(before, block_last[d] == prior)), terms[d], 0))
                backward.append((flag(jnp.logical_and(jnp.logical_not(before), block_first[d] == later)), terms[d], 1))
        take_f, take_b = prior == 0.0, later == newest
        if grouped:
            take_f = jnp.logical_and(take_f, jnp.logical_and(o == 0, (c ^ t) == 0))
            take_b = jnp.logical_and(take_b, jnp.logical_and(o == outer - 1, (c ^ t) == inner - 1))
        priors.append(prior)
        laters.append(later)
        plans.append((forward, backward, flag(take_f), flag(take_b)))
    for s, (g, mate) in enumerate(zip(places, mates)):
        for i in range(part):
            at = s * part + i

            def carried(head, ref):
                place = head - z * held
                mine = jnp.logical_and(place >= 0, place < held)
                return jnp.where(mine, ref[jnp.clip(place, 0, held - 1)], 0.0)

            carries = [
                carried(g * unit + c * part + i, carry_ref),
                carried(mate * unit + c * part + i, cot_ref) * factor,
            ]
            if lacking:
                more = lacked[0, c * part + i].astype(F32)
                carries[0] = carries[0] + jnp.where(z == 0, more, 0.0)
                carries[1] = carries[1] + jnp.where(z == DEPTH - 1, more, 0.0)

            def value(ref, side):
                return (ref[at * DH : (at + 1) * DH, :] if side is None else ref[side, at]).astype(F32)

            for t, out in enumerate(outs):
                for side in range(2):
                    amount = plans[t][2 + side] * carries[side]
                    for weight, ref, which in plans[t][side]:
                        amount = amount + weight * value(ref, which)
                    out[side, at] = amount.astype(BF16)
    edge_ref[0:1, :] = priors[0]
    edge_ref[1:2, :] = laters[0]
    edge_ref[2:8, :] = jnp.broadcast_to(newest, (6, DH))


def place_of(ids):
    z = ids[2]
    side = jnp.where(z >= DEPTH // 2, 1, 0)
    return z, side, jnp.logical_or(z == 0, z == DEPTH - 1)


def edge_rows(z, labels, edges):
    first, last = own_row(labels, z), own_row(labels, DEPTH + z)
    last_before = own_row(labels, DEPTH + jnp.maximum(z - 1, 0))
    first_after = own_row(labels, jnp.minimum(z + 1, DEPTH - 1))
    final_f, final_b = labels[2 * DEPTH - 1 : 2 * DEPTH, :], labels[0:1, :]
    prior = later = final_f
    if edges is not None:
        prior, later = edges[0:1, :], edges[1:2, :]
    return (last, last_before, final_f, first, prior), (first, first_after, final_b, last, later)


def pick(which, rows):
    return [jnp.where(which == 0, a, b) for a, b in zip(*rows)]


def hop(side, rows, lead, off, part, term_ref, prefix_ref, prefix_off, got_ref, got_off, out, out_off):
    own, neighbour, _, _, prior = pick(side, rows)
    other, _, final, _, _ = pick(1 - side, rows)
    join, keep, counts = flag(prior == own), flag(neighbour == own), flag(other == final)
    for i in range(part):
        state = term_ref[side, off + i].astype(F32)
        if lead:
            rest = counts * term_ref[1 - side, off + i].astype(F32)
        else:
            state = state + join * prefix_ref[side, prefix_off + i].astype(F32)
            rest = prefix_ref[1 - side, prefix_off + i].astype(F32)
        if got_ref is not None:
            state = state + keep * got_ref[0, got_off + i].astype(F32)
            rest = rest + got_ref[1, got_off + i].astype(F32)
        out[0, out_off + i] = state.astype(BF16)
        out[1, out_off + i] = rest.astype(BF16)


def hop_kernel(part, near, far, across, has_edges, ids, labels, *refs):
    z, side, at_end = place_of(ids)
    out, refs = refs[-1], list(refs[:-1])
    rows = edge_rows(z, labels, refs.pop(0) if has_edges else None)

    def take(plans):
        return [(plan, refs.pop(0), None if plan[0] else refs.pop(0), refs.pop(0) if plan[3] is not None else None) for plan in plans]

    near, far = take(near), take(far)

    def write(side, entries):
        for n, ((lead, off, prefix_off, got_off), term, prefix, got) in enumerate(entries):
            hop(side, rows, lead, off, part, term, prefix, prefix_off, got, got_off, out, n * part)

    if near:
        pl.when(at_end)(lambda: write(side, near))
    if far:
        pl.when(jnp.logical_not(at_end))(lambda: write(side if across else 1 - side, far))


def lead_total_kernel(part, plans, ids, labels, *refs):
    z, side, at_end = place_of(ids)
    rows = edge_rows(z, labels, None)
    for t, (off, near_off, middle_off, far_off) in enumerate(plans):
        term, near, middle, far = refs[4 * t : 4 * t + 4]
        out = refs[4 * len(plans) + t]

        def total(which, over, over_off, rest, rest_off):
            own, neighbour, final, _, _ = pick(which, rows)
            counts, come = flag(own == final), flag(neighbour == final)
            for i in range(part):
                value = counts * term[which, off + i].astype(F32)
                if over is not None:
                    value = value + come * over[0, over_off + i].astype(F32)
                if rest is not None:
                    value = value + rest[1, rest_off + i].astype(F32)
                out[which, i] = value.astype(BF16)

        @pl.when(at_end)
        def _():
            total(side, None, 0, far, far_off)
            total(1 - side, far, far_off, None, 0)

        @pl.when(jnp.logical_not(at_end))
        def _():
            total(side, near, near_off, middle, middle_off)
            total(1 - side, middle, middle_off, near, near_off)


def local_kernel(factor, base, count, docs_ref, row_ref, q_ref, k_ref, v_ref, g_ref, out):
    docs = docs_ref[...]
    places = lax.broadcasted_iota(jnp.int32, (SPAN, SPAN), 0)
    others = lax.broadcasted_iota(jnp.int32, (SPAN, SPAN), 1)
    allowed = jnp.logical_and(others <= places, docs == row_ref[0:1])
    for i in range(count):
        at = slice((base + i) * DH, (base + i + 1) * DH)
        q, k, v, g = q_ref[:, at], k_ref[:, at], v_ref[:, at], g_ref[:, at]
        scores = jnp.where(allowed, dot_transposed(q, k) * factor, 0.0).astype(BF16)
        grad_scores = jnp.where(allowed, dot_transposed(g, v) * factor, 0.0).astype(BF16)
        out[0, i] = dot(scores, v)
        out[1, i] = dot(grad_scores, k)
        out[2, i] = transposed_dot(grad_scores, q)
        out[3, i] = transposed_dot(scores, g)


def output_kernel(unit, part, plans, ids, labels, edges, docs_ref, q_ref, k_ref, v_ref, g_ref, *refs):
    count = len(plans)
    sources, locals_ = refs[: 4 * count], refs[4 * count : 5 * count]
    outs, (states, held, sems) = refs[-7:-3], refs[-3:]
    c = ids[1]
    z, side, at_end = place_of(ids)
    rows = edge_rows(z, labels, edges)

    def make_states(ends, side):
        for n, (which, _, _, lead, off, near_off, middle_off, far_off) in enumerate(plans):
            prefix, near, middle, far = sources[4 * n : 4 * n + 4]
            _, neighbour, _, target, prior = rows[which]
            reach, come = flag(prior == target), flag(neighbour == target)
            if ends:
                over, rest = (None, (far, far_off)) if side == which else ((far, far_off), None)
            elif side == which:
                over, rest = (near, near_off), (middle, middle_off)
            else:
                over, rest = (middle, middle_off), (near, near_off)
            for i in range(part):
                value = reach * prefix[which, off + i].astype(F32)
                if over is not None:
                    value = value + come * over[0][0, over[1] + i].astype(F32)
                if rest is not None and not lead:
                    value = value + reach * rest[0][1, rest[1] + i].astype(F32)
                states[n, i] = value.astype(BF16)

    for ends in (True, False):
        for which in range(2):
            here = jnp.logical_and(at_end if ends else jnp.logical_not(at_end), side == which)
            pl.when(here)(functools.partial(make_states, ends, which))

    in_first, in_last = document_masks(docs_ref[...])
    copies = []
    for n, (which, group, turn, *_) in enumerate(plans):
        place = (c ^ turn) * part
        for i in range(part):
            at = columns(group * unit + place + i)
            state = states[n, i]
            if which == 0:
                results = (
                    dot(jnp.where(in_first, q_ref[:, at], 0), state),
                    dot_transposed(jnp.where(in_first, g_ref[:, at], 0), state),
                )
            else:
                results = (
                    dot_transposed(jnp.where(in_last, v_ref[:, at], 0), state),
                    dot(jnp.where(in_last, k_ref[:, at], 0), state),
                )
            for m, result in enumerate(results):
                held[n, m, i] = (locals_[n][2 * which + m, place + i] + result).astype(BF16)
                copy = pltpu.make_async_copy(held.at[n, m, i], outs[2 * which + m].at[:, at], sems.at[n, m, i])
                copy.start()
                copies.append(copy)
    for copy in copies:
        copy.wait()


def shards(queries, keys, values, out_grad, doc_ids, carry_in, carry_cot):
    outer, inner, depth = (lax.axis_size(a) for a in ("outer", "inner", "heads"))
    assert depth == DEPTH
    tokens_all = doc_ids.shape[0] * outer * inner
    factor = float(DH * (tokens_all // 2)) ** (-0.5)
    head_count = queries.shape[1] // DH
    held = carry_in.shape[0]
    part = min(4, head_count // inner)
    unit = part * inner
    groups = head_count // unit
    leads = 2 if held == unit and groups == DEPTH and inner == 2 else 0
    costs = iter(COSTS if leads else ())

    def mate(g):
        return groups - 1 - g if leads else g

    ids = jnp.stack([lax.axis_index(a) for a in ("outer", "inner", "heads")]).astype(jnp.int32)
    token = jnp.zeros((8, DH), F32)
    doc_blocks = pltpu.with_memory_space_constraint(doc_ids.reshape(depth, SPAN), pltpu.HBM)
    label_shapes = [
        jax.ShapeDtypeStruct((2 * depth, DH), F32),
        jax.ShapeDtypeStruct((SPAN, SPAN), F32),
        jax.ShapeDtypeStruct((8, SPAN), F32),
    ]
    own_labels = docs_column = docs_row = labels = None

    levels = (outer - 1).bit_length()

    def state_pair(count):
        return jax.ShapeDtypeStruct((2, count, DH, DH), BF16)

    terms, prefixes, near, middle, far, local = {}, {}, {}, {}, {}, {}
    edge, arrays, carries = None, (queries, keys, values, out_grad), (carry_in, carry_cot)
    far_arrays, far_carries = (
        tuple(pltpu.with_memory_space_constraint(a, pltpu.HBM) for a in group) for group in (arrays, carries)
    )

    def exchange(own):
        return [own[0]] + [pairs(own[d], "inner", d) for d in range(1, inner)]

    def exchange_pieces(own):
        return [own[0]] + [[pairs(a, "inner", d) for a in own[d]] for d in range(1, inner)]

    def receive(units, kind, sent, perm):
        got = lax.ppermute(sent, "heads", perm)
        for n, u in enumerate(units):
            kind[u] = (got, n * part)
        return got

    def take_labels(arrays):
        nonlocal own_labels, docs_column, docs_row, labels
        own_labels, docs_column, docs_row = arrays
        labels = [own_labels] + [pairs(own_labels, "inner", d) for d in range(1, inner)]

    def make_labels():
        take_labels(run(
            label_kernel,
            (ids, doc_blocks),
            label_shapes,
            scratch=[pltpu.VMEM((depth, SPAN), jnp.int32), pltpu.SemaphoreType.DMA((1,))],
            specs=[SMEM, HBM],
        ))

    def run(*args, **options):
        nonlocal token
        token, outs = call(token, *args, cost=next(costs, 0), **options)
        return outs

    def make_lead_terms():
        places = tuple(range(leads))
        block = pltpu.VMEM((leads, SPAN, unit * DH), BF16)
        carry = pltpu.VMEM((unit, DH, DH), F32)
        own = run(
            functools.partial(
                lead_terms, factor, unit, part, places, tuple(mate(g) for g in places), outer, inner
            ),
            (ids, doc_blocks) + far_arrays + far_carries,
            [state_pair(part * leads)] * inner + [state_pair(unit)] + label_shapes,
            scratch=[pltpu.VMEM((depth, SPAN), jnp.int32)] + [block] * 4 + [carry, pltpu.SemaphoreType.DMA((leads + 1, 4))],
            specs=[SMEM] + [HBM] * 7,
        )
        take_labels(own[inner + 1 :])
        for g in places:
            terms[g] = [(a, g * part) for a in own[:inner]]
        return receive([(0, t) for t in range(inner)], near, own[inner], [(0, 1), (3, 2), (1, 0), (2, 3)])

    def make_terms(places):
        own = run(
            functools.partial(rest_terms, factor, unit, part, places, tuple(mate(g) for g in places)),
            (ids, docs_column) + far_arrays,
            [state_pair(part * len(places))] + [state_pair(part)] * (len(places) * (inner - 1)),
            scratch=[pltpu.VMEM((len(places), SPAN, unit * DH), BF16)] * 4
            + [pltpu.SemaphoreType.DMA((len(places), 4))],
            specs=[SMEM, VMEM] + [HBM] * 4,
        )
        own = [own[:1]] + [own[1 + d * len(places) :][: len(places)] for d in range(inner - 1)]
        for s, g in enumerate(places):
            terms[g] = [(own[0][0], s * part)] + [(a[s], 0) for a in own[1:]]
        return exchange_pieces(own)

    def make_sums(received, grouped):
        nonlocal token
        count = sum(a.shape[1] for a in received[0])
        sums = run(
            functools.partial(sum_kernel, tuple(len(a) for a in received), levels, grouped),
            (ids, *labels, *(a for pieces in received for a in pieces)),
            [jax.ShapeDtypeStruct((count * DH + LABELS, DH), BF16)] * levels,
        )
        return [pairs(sums[d.bit_length() - 1], "outer", d) for d in range(1, outer)]

    def make_prefixes(places, received, fans, grouped, lacked=None):
        nonlocal edge
        count = sum(a.shape[1] for a in received[0])
        given = run(
            functools.partial(
                prefix_kernel, factor, unit, part, places, tuple(mate(g) for g in places),
                tuple(len(a) for a in received), outer, grouped,
                lacked is not None,
            ),
            (ids, *carries, *([] if lacked is None else [lacked]), *labels, *(a for pieces in received for a in pieces), *fans),
            [state_pair(count)] * inner + [jax.ShapeDtypeStruct((8, DH), F32)],
        )
        edge = given[-1] if edge is None else edge
        given = exchange(given[:-1])
        for s, g in enumerate(places):
            prefixes[g] = [(a, s * part) for a in given]

    def move(near_units, far_units, across):
        units = list(near_units) + list(far_units)
        use_edges = not all(g < leads for g, _ in units)
        operands = [ids, own_labels] + ([edge] if use_edges else [])

        def plans_of(chosen, got):
            plans = []
            for u in chosen:
                g, t = u
                lead = g < leads
                array, off = terms[g][t]
                operands.append(array)
                if not lead:
                    operands.append(prefixes[g][t][0])
                if got is not None:
                    operands.append(got[u][0])
                plans.append((lead, off, 0 if lead else prefixes[g][t][1], None if got is None else got[u][1]))
            return plans

        near_plans = plans_of(near_units, None)
        far_plans = plans_of(far_units, near if across else middle)
        sent = run(
            functools.partial(hop_kernel, part, near_plans, far_plans, across, use_edges),
            operands,
            [state_pair(part * max(len(near_units), len(far_units)))],
        )
        return sent[0]

    def ends(near_units, far_units):
        perm = ([(0, 1), (3, 2)] if near_units else []) + ([(1, 0), (2, 3)] if far_units else [])
        got = receive(near_units, near, move(near_units, far_units, False), perm)
        for n, u in enumerate(far_units):
            far[u] = (got, n * part)

    def across(units):
        receive(units, middle, move([], units, True), [(1, 2), (2, 1)])

    def make_local(g):
        out = run(
            functools.partial(local_kernel, factor, g * unit, unit),
            (docs_column, docs_row) + arrays,
            [jax.ShapeDtypeStruct((4, unit, SPAN, DH), F32)],
            specs=[VMEM] * 6,
        )
        local[g] = out[0]

    out_shape = jax.ShapeDtypeStruct(queries.shape, BF16)
    results = ()

    def make_outputs(halves):
        nonlocal results
        operands, plans = (ids, own_labels, edge, docs_column) + arrays, []
        for which, g, t in halves:
            array, off = prefixes[g][t]
            kept = [kind[g, t] for kind in (near, middle, far)]
            heads = mate(g) if which else g
            plans.append((which, heads, t, g < leads, off) + tuple(at for _, at in kept))
            operands += (array,) + tuple(a for a, _ in kept)
        operands += tuple(local[mate(g) if which else g] for which, g, _ in halves)
        count = len(halves)
        results = run(
            functools.partial(output_kernel, unit, part, plans),
            operands + tuple(results),
            [out_shape] * 4,
            scratch=[
                pltpu.VMEM((count, part, DH, DH), BF16),
                pltpu.VMEM((count, 2, part, SPAN, DH), BF16),
                pltpu.SemaphoreType.DMA((count, 2, part)),
            ],
            aliases={len(operands) + i: i for i in range(len(results))},
            specs=[SMEM] + [VMEM] * (len(operands) - 1) + [HBM] * len(results),
            out_specs=[HBM] * 4,
        )

    def make_totals(g):
        operands, plans = [ids, own_labels], []
        for t in range(inner):
            array, off = terms[g][t]
            kept = [kind[g, t] for kind in (near, middle, far)]
            operands += [array] + [a for a, _ in kept]
            plans.append((off,) + tuple(at for _, at in kept))
        totals = run(
            functools.partial(lead_total_kernel, part, plans),
            operands,
            [state_pair(part)] * inner,
        )
        return exchange_pieces([[a] for a in totals])

    def chunk(n):
        return [(n, t) for t in range(inner)] if n < leads else [(g, n - leads) for g in range(leads, groups)]

    def halves_of(n):
        return [(which, g, t) for which in range(2) for g, t in chunk(n)]

    if leads:
        kept = {}

        def keep(name, make, *args):
            kept[name] = make(*args)

        def rest_sums():
            kept["fans"] = make_sums(kept["got"], False)

        def rest_prefixes():
            make_prefixes((2, 3), kept["got"], kept["fans"], False)

        def lead_sums(g):
            kept["fans", g] = make_sums(kept["totals", g], True)

        def lead_prefixes(g):
            make_prefixes((g,), kept["totals", g], kept["fans", g], True, kept["lacked"] if g else None)

        steps = {
            "K": lambda g: keep("lacked", make_lead_terms) if g == 0 else keep("got", make_terms, (2, 3)),
            "A": lambda g: rest_sums(),
            "B": lambda g: rest_prefixes(),
            "L": make_local,
            "E": lambda g: ends(chunk(g), []),
            "O": lambda g: across(chunk(g)),
            "F": lambda g: ends([], chunk(g)),
            "J": lambda g: ends(chunk(g), chunk(g - leads)),
            "M": lambda g: ends(chunk(g), chunk(0)),
            "T": lambda g: keep(("totals", g), make_totals, g),
            "S": lead_sums,
            "P": lead_prefixes,
            "W": lambda g: make_outputs(halves_of(g)),
        }
        for step in [step for line in ORDER for step in line.split()]:
            steps[step[0]](int(step[1]))
    else:
        assert not leads
        make_labels()
        places = tuple(range(groups))
        got = make_terms(places)
        make_prefixes(places, got, make_sums(got, False), False)
        units = [(g, t) for g in range(groups) for t in range(inner)]
        lag = 4
        for k in range(len(units) + lag):
            ends(units[k : k + 1], units[k - lag : k - lag + 1] if k >= lag else [])
            if k < len(units):
                across([units[k]])
        for g in range(groups):
            make_local(g)
        for g, t in units:
            make_outputs([(0, g, t), (1, g, t)])
    return tuple(results)


def solution(mesh):
    tokens = P(("outer", "inner", "heads"), None)
    carry = P("heads", None, None)
    return jax.shard_map(
        shards,
        mesh=mesh,
        in_specs=(tokens,) * 4 + (P(("outer", "inner")), carry, carry),
        out_specs=(tokens,) * 4,
        check_vma=False,
    )
```
